128 devices in a mesh: section: 2 (over core), dp: 64 (over x, y, z).
Axes of the slice: x: 4, y: 4, z: 4, core: 2. Of those that a mesh axis runs over, the one named last changes fastest.
Arguments:
- ends: bfloat16 [2, 3, 4096, 896], P('section', None, 'dp'), may hold values from -9 to 9
- segment_ids: int32 [3, 4096], replicated, may hold values from 0 to 3, as said below
- valid_blocks: int32 [3, 32], replicated, may hold values from 0 to 1, as said below
- qkv_weight: bfloat16 [2, 896, 1152], P('section', 'dp'), may hold values from -0.1875 to 0.1875
- qkv_bias: bfloat16 [2, 1152], P('section'), may hold values from -3 to 3
- out_weight: bfloat16 [2, 896, 896], P('section', 'dp'), may hold values from -2 to 2
- gate_up_weight: bfloat16 [2, 896, 9728], P('section', 'dp'), may hold values from -0.1875 to 0.1875
- down_weight: bfloat16 [2, 896, 4864], P('section', 'dp'), may hold values from -0.078125 to 0.078125
- norm_gains: bfloat16 [2, 2, 896], P('section'), may hold values from 0.5 to 1.5
Outputs:
- boundary: bfloat16 [2, 3, 4096, 896], P('section', None, 'dp')
- qkv_weight_grad: float32 [2, 896, 1152], P('section', 'dp')
- qkv_bias_grad: float32 [2, 1152], P('section')
- out_weight_grad: float32 [2, 896, 896], P('section', 'dp')
- gate_up_weight_grad: float32 [2, 896, 9728], P('section', 'dp')
- down_weight_grad: float32 [2, 896, 4864], P('section', 'dp')
- norm_gains_grad: float32 [2, 2, 896], P('section')
- rms_stats: float32 [2, 3, 3], P('section')
The draws below stay inside these ranges and needn't reach their ends.
Inputs may be any that keep to these rules, and one draw needn't show every extreme that they name: `segment_ids`: along each micro-batch the ids never fall; in one micro-batch, drawn from the seed, all tokens form one document. `valid_blocks`: in each micro-batch the valid blocks form a prefix of 16 blocks or more; every block of the single-document micro-batch is valid.
All inputs are finite; a program needn't handle non-finite values.
Results may differ from the reference program's by a relative error of at most 0.013.
Values may be sent and summed in bfloat16 or wider, within the bound.
A program may use at most 320 MiB of HBM per device.

```python
import math
import jax
import jax.numpy as jnp
from jax import lax

D = 896
HEADS = 14
KV_HEADS = 2
HEAD = 64
FF = 4864
MICRO = 3
BLOCK = 128
DOCS = 4
SECTIONS = 2
SEQ = 4096
NBLK = 32
HD = 896
KVD = 128
QKV = 1152


def full_batch(key):
    return jax.random.randint(jax.random.fold_in(key, 5), (), 0, MICRO)


def draw_ends(key, part):
    key = jax.random.fold_in(key, 23)
    full_shape = (SECTIONS, MICRO, SEQ, D)
    places = jnp.arange(SEQ, dtype=jnp.float32) / max(SEQ - 1, 1)
    rising = 0.6 * jnp.exp(places * math.log(3.0))
    noise = jnp.clip(jax.random.normal(key, full_shape, jnp.float32), -5.0, 5.0)
    row_scale = jnp.stack([rising, jnp.ones_like(rising)])[:, None, :, None]
    return (noise * row_scale).astype(jnp.bfloat16)


def draw_segment_ids(key, part):
    chosen = full_batch(key)
    key = jax.random.fold_in(key, 21)
    cuts = jax.random.randint(key, (MICRO, DOCS - 1, 1), 1, SEQ)
    places = jnp.arange(SEQ, dtype=jnp.int32)[None, None, :]
    segments = jnp.sum((cuts <= places).astype(jnp.int32), axis=1)
    batch_rows = jnp.arange(MICRO, dtype=jnp.int32)[:, None]
    return jnp.where(batch_rows == chosen, 0, segments).astype(jnp.int32)


def draw_valid_blocks(key, part):
    chosen = full_batch(key)
    key = jax.random.fold_in(key, 22)
    counts = jax.random.randint(key, (MICRO, 1), NBLK // 2, NBLK)
    batch_rows = jnp.arange(MICRO, dtype=jnp.int32)[:, None]
    counts = jnp.where(batch_rows == chosen, NBLK, counts)
    return (jnp.arange(NBLK, dtype=jnp.int32)[None, :] < counts).astype(jnp.int32)


def level_of(stream_key, extent, cuts, least, largest):
    loudness = 1.0
    for dim, blocks in cuts:
        draws = jax.random.uniform(jax.random.fold_in(jax.random.fold_in(stream_key, 6), dim), (blocks,), jnp.float32, least / len(cuts), largest / len(cuts))
        loudness = loudness * jnp.repeat(jnp.exp(draws), extent[dim] // blocks).reshape((-1,) + (1,) * (len(extent) - 1 - dim))
    return loudness


def normal_values(own_key, dims, deviation, bound, cuts=(), kind=jnp.bfloat16):
    array = jax.random.normal(own_key, dims, jnp.float32) * deviation
    if len(cuts) > 0:
        array = level_of(own_key, dims, cuts, -0.22, 0.18) * array
    return jnp.clip(array, min=-bound, max=bound).astype(kind)


def setup_inputs(seed: int = 0) -> dict:
    arg_keys = jax.random.split(jax.random.key(seed), 10)
    ends = draw_ends(jax.random.fold_in(arg_keys[9], 71), 0)
    segment_ids = draw_segment_ids(jax.random.fold_in(arg_keys[9], 71), 0)
    valid_blocks = draw_valid_blocks(jax.random.fold_in(arg_keys[9], 71), 0)
    qkv_weight = normal_values(arg_keys[3], (SECTIONS, D, QKV), D ** -0.5, 0.1875, ((0, 2), (1, 64)))
    qkv_bias = normal_values(arg_keys[4], (SECTIONS, QKV), 0.5, 3.0, ((0, 2),))
    out_weight = normal_values(arg_keys[5], (SECTIONS, D, HD), (max(D * 8 * DOCS // SEQ, 1)) ** -0.5, 2.0, ((0, 2), (1, 64)))
    gate_up_weight = normal_values(arg_keys[6], (SECTIONS, D, 2 * FF), D ** -0.5, 0.1875, ((0, 2), (1, 64)))
    down_weight = normal_values(arg_keys[7], (SECTIONS, D, FF), FF ** -0.5, 0.078125, ((0, 2), (1, 64)))
    norm_gains = jnp.clip(1.0 + 0.1 * jax.random.normal(arg_keys[8], (SECTIONS, 2, D), jnp.float32), 0.5, 1.5).astype(jnp.bfloat16)
    return dict(ends=ends, segment_ids=segment_ids, valid_blocks=valid_blocks, qkv_weight=qkv_weight, qkv_bias=qkv_bias, out_weight=out_weight, gate_up_weight=gate_up_weight, down_weight=down_weight, norm_gains=norm_gains)


EPS = 1e-06
THETA = 1000000.0
MASKED = -1e+30

@jax.custom_vjp
def low(v):
    return lax.optimization_barrier(v.astype(jnp.bfloat16)).astype(jnp.float32)

@jax.custom_vjp
def low_back(v):
    return v

def low_keep(v):
    return (low(v), None)

def low_pass(kept, grad):
    return (grad,)

def back_keep(v):
    return (v, None)

def back_low(kept, grad):
    return (low(grad),)
low.defvjp(low_keep, low_pass)
low_back.defvjp(back_keep, back_low)

def precise_dot(left, right):
    return jnp.dot(left, right, precision=lax.Precision.HIGHEST)

def normalize(features, gain_vec):
    return features * lax.rsqrt(lax.optimization_barrier(jnp.mean(features * features, axis=-1, keepdims=True)) + EPS) * gain_vec

def rope_tables(length):
    positions = jnp.arange(length, dtype=jnp.float32)
    frequency = THETA ** (-jnp.arange(HEAD // 2, dtype=jnp.float32) * 2.0 / HEAD)
    angles = positions[:, None] * frequency[None, :]
    return (jnp.cos(angles), jnp.sin(angles))

def rotate(heads_in, cosine_rows, sine_rows):
    half_size = HEAD // 2
    first_half = heads_in[..., :half_size]
    second_half = heads_in[..., half_size:]
    cos_part = cosine_rows[:, None, :]
    sin_part = sine_rows[:, None, :]
    return jnp.concatenate([first_half * cos_part - second_half * sin_part, second_half * cos_part + first_half * sin_part], axis=-1)

def attend(queries, key_heads, value_heads, segment_row, valid_row):
    query_rows = min(512, SEQ)
    groups = HEADS // KV_HEADS
    softmax_scale = 1.0 / HEAD ** 0.5
    blocked = queries.reshape(SEQ // query_rows, query_rows, KV_HEADS, groups, HEAD)
    starts = jnp.arange(SEQ // query_rows, dtype=jnp.int32) * query_rows
    key_pos = jnp.arange(SEQ, dtype=jnp.int32)

    def query_block(pair):
        block_queries, block_start = pair
        query_pos = block_start + jnp.arange(query_rows, dtype=jnp.int32)
        query_segment = lax.dynamic_slice_in_dim(segment_row, block_start, query_rows)
        same_doc = query_segment[:, None] == segment_row[None, :]
        causal = key_pos[None, :] <= query_pos[:, None]
        usable = (valid_row[None, :] > 0) | (key_pos[None, :] == query_pos[:, None])
        allowed = same_doc & causal & usable
        scores = jnp.einsum('qngd,knd->ngqk', block_queries, key_heads, precision=lax.Precision.HIGHEST) * softmax_scale
        scores = low_back(scores)
        scores = jnp.where(allowed[None, None], scores, MASKED)
        prob_table = jax.nn.softmax(scores, axis=-1)
        mixed = jnp.einsum('ngqk,knd->qngd', low(prob_table), value_heads, precision=lax.Precision.HIGHEST)
        return low(low_back(mixed.reshape(query_rows, HD)))
    return lax.map(jax.checkpoint(query_block), (blocked, starts)).reshape(SEQ, HD)

def decoder_layer(hidden_in, weights, segment_row, valid_row, cosine_rows, sine_rows):
    w_qkv, b_qkv, w_out, w_gate_up, w_down, gain_rows = weights
    normed = low(normalize(hidden_in, gain_rows[0]))
    projected = low_back(precise_dot(normed, w_qkv) + b_qkv)
    queries = projected[:, :HD].reshape(SEQ, HEADS, HEAD)
    key_heads = projected[:, HD:HD + KVD].reshape(SEQ, KV_HEADS, HEAD)
    value_heads = projected[:, HD + KVD:].reshape(SEQ, KV_HEADS, HEAD)
    queries = low(rotate(queries, cosine_rows, sine_rows))
    key_heads = low(rotate(key_heads, cosine_rows, sine_rows))
    value_heads = low(value_heads)
    attended = attend(queries, key_heads, value_heads, segment_row, valid_row)
    branch = low_back(precise_dot(attended, w_out.T))
    middle = hidden_in + branch
    normed_two = low(normalize(middle, gain_rows[1]))
    gate_up = low_back(precise_dot(normed_two, w_gate_up))
    hidden = low(jax.nn.silu(gate_up[:, :FF]) * gate_up[:, FF:])
    mlp_out = low_back(precise_dot(hidden, w_down.T))
    return (middle + mlp_out, (hidden_in, branch, mlp_out))

def reference(ends, segment_ids, valid_blocks, qkv_weight, qkv_bias, out_weight, gate_up_weight, down_weight, norm_gains):
    inputs = ends[0].astype(jnp.float32)
    cotangent = ends[1].astype(jnp.float32)
    params = tuple((weight.astype(jnp.float32) for weight in (qkv_weight, qkv_bias, out_weight, gate_up_weight, down_weight, norm_gains)))
    valid_tokens = jnp.repeat(valid_blocks, BLOCK, axis=1)
    cosine_rows, sine_rows = rope_tables(SEQ)

    def forward(layer_inputs, layer_params):
        results = []
        pieces_all = []
        for batch_num in range(MICRO):
            state_now = layer_inputs[batch_num]
            for section_num in range(SECTIONS):
                weights = tuple((member[section_num] for member in layer_params))
                state_now, pieces = decoder_layer(state_now, weights, segment_ids[batch_num], valid_tokens[batch_num], cosine_rows, sine_rows)
                pieces_all.append(pieces)
                if section_num + 1 < SECTIONS:
                    state_now = low(low_back(state_now))
            results.append(state_now)
        return (jnp.stack(results), pieces_all)
    result, pullback, pieces_all = jax.vjp(forward, inputs, params, has_aux=True)
    input_grad, param_grads = pullback(cotangent)
    boundary = jnp.stack([input_grad, result]).astype(jnp.bfloat16)
    stat_rows = []
    for section_num in range(SECTIONS):
        batch_rows = []
        for batch_num in range(MICRO):
            pieces = pieces_all[batch_num * SECTIONS + section_num]
            valid_weight = valid_tokens[batch_num].astype(jnp.float32)[:, None]
            valid_count = jnp.sum(valid_tokens[batch_num]).astype(jnp.float32) * D
            batch_rows.append(jnp.stack([jnp.sqrt(jnp.sum(piece * piece * valid_weight) / valid_count) for piece in pieces]))
        stat_rows.append(jnp.stack(batch_rows))
    rms_stats = jnp.stack(stat_rows)
    return (boundary, param_grads[0], param_grads[1], param_grads[2], param_grads[3], param_grads[4], param_grads[5], rms_stats)
```

```python
import functools
import math

import jax
import jax.numpy as jnp
from jax import lax
from jax.experimental import pallas as pl
from jax.experimental.pallas import tpu as pltpu
from jax.sharding import PartitionSpec as P

MESH = pl.DeviceIdType.MESH
EPS = 1e-06
THETA = 1000000.0
MASKED = -1e30

MB = 3
T = 64
R = MB * T
D = 896
DP = 1024
FFH = 2432
QS = 512
C_UP, C_DOWN, C_QK, C_VO, C = FFH, 2 * FFH, 3 * FFH, 3 * FFH + QS, 3 * FFH + 2 * QS
KB = 512
SEQ = 4096
MIB = 1024 * 1024

THIRDS = ((0, 22 * 128), (22 * 128, 22 * 128), (44 * 128, 21 * 128))
ORDERS = (("z", "y", "x"), ("y", "x", "z"), ("x", "z", "y"))
FF_CHUNKS = ((0, 512), (512, 512), (1024, 512), (1536, 512), (2048, 384))


def position():
    chip = lax.axis_index("dp")
    return {"x": chip // 16, "y": (chip // 4) % 4, "z": chip % 4}


def moved(place, axis, distance):
    other = dict(place)
    other[axis] = (place[axis] + distance + 4) % 4
    return other


def chip_id(place):
    return {"dp": place["x"] * 16 + place["y"] * 4 + place["z"]}


def other_core():
    return {"section": 1 - lax.axis_index("section")}


def meet(place, core=False, chips=True, far=False):
    barrier = pltpu.get_barrier_semaphore()
    count = 0
    if chips:
        for axis in "xyz":
            for distance in (1, -1, 2) if far else (1, -1):
                pl.semaphore_signal(
                    barrier,
                    inc=1,
                    device_id=chip_id(moved(place, axis, distance)),
                    device_id_type=MESH,
                )
                count += 1
    if core:
        pl.semaphore_signal(barrier, inc=1, device_id=other_core(), device_id_type=MESH)
        count += 1
    pl.semaphore_wait(barrier, count)


def send(src, dst, send_sem, recv_sem, device):
    return pltpu.make_async_remote_copy(
        src, dst, send_sem, recv_sem, device_id=device, device_id_type=MESH
    )


def cube(done, place):
    return tuple(slice(None) if axis in done else place[axis] for axis in "xyz")


def gather_stages(view, place, send_sems, recv_sems):
    pending = []

    def copy(j, phase, k, whose, part, distance):
        ref = view(cube(ORDERS[j][:phase], whose), j, part)
        return send(
            ref,
            ref,
            send_sems.at[j, phase, k],
            recv_sems.at[j, phase, k],
            chip_id(moved(place, ORDERS[j][phase], distance)),
        )

    def first(phase):
        for j in range(3):
            for k, distance in ((0, 1), (1, -1)):
                one = copy(j, phase, k, place, None, distance)
                one.start()
                pending.append(one)

    def second(phase):
        for j in range(3):
            for k, distance in ((0, 1), (1, -1)):
                whose = moved(place, ORDERS[j][phase], -distance)
                copy(j, phase, k, whose, None, distance).wait_recv()
                one = copy(j, phase, 2 + k, whose, k, distance)
                one.start()
                pending.append(one)

    def third(phase):
        for j in range(3):
            for k, distance in ((0, 1), (1, -1)):
                whose = moved(place, ORDERS[j][phase], 2)
                copy(j, phase, 2 + k, whose, k, distance).wait_recv()

    def finish():
        for one in pending:
            one.wait_send()

    stages = []
    for phase in range(3):
        stages.append(functools.partial(first, phase))
        stages.append(functools.partial(second, phase))
        stages.append(functools.partial(third, phase))
    stages.append(finish)
    return stages


def scatter_stages(view, halves, wholes, place, send_sems, recv_sems, width, final):
    pending = []

    def chips_of(j, phase, whose):
        order = ORDERS[j][::-1]
        return cube(order[phase + 1 :], whose)

    def axis_of(j, phase):
        return ORDERS[j][::-1][phase]

    def add(dst, *terms):
        dst[...] = sum(term[...].astype(jnp.float32) for term in terms).astype(dst.dtype)

    def half_copy(j, phase, k, distance):
        src = view(chips_of(j, phase, moved(place, axis_of(j, phase), 2)), j, k)
        return send(
            src,
            halves[phase](j, k),
            send_sems.at[j, phase, k],
            recv_sems.at[j, phase, k],
            chip_id(moved(place, axis_of(j, phase), distance)),
        )

    def whole_copy(j, phase, k, distance):
        src = view(chips_of(j, phase, moved(place, axis_of(j, phase), distance)), j, None)
        return send(
            src,
            wholes[phase](j, k, None),
            send_sems.at[j, phase, 2 + k],
            recv_sems.at[j, phase, 2 + k],
            chip_id(moved(place, axis_of(j, phase), distance)),
        )

    def first(phase):
        for j in range(3):
            for k, distance in ((0, 1), (1, -1)):
                one = half_copy(j, phase, k, distance)
                one.start()
                pending.append(one)

    def second(phase):
        for j in range(3):
            for k, distance in ((0, 1), (1, -1)):
                half_copy(j, phase, k, distance).wait_recv()
                mine = view(chips_of(j, phase, moved(place, axis_of(j, phase), distance)), j, k)
                add(mine, mine, halves[phase](j, k))
                one = whole_copy(j, phase, k, distance)
                one.start()
                pending.append(one)

    def third(phase):
        for j in range(3):
            for k, distance in ((0, 1), (1, -1)):
                whole_copy(j, phase, k, distance).wait_recv()
            mine = view(chips_of(j, phase, place), j, None)
            if phase < 2:
                add(mine, mine, wholes[phase](j, 0, None), wholes[phase](j, 1, None))
            else:
                final(j, mine, wholes[phase](j, 0, None), wholes[phase](j, 1, None))

    def finish():
        for one in pending:
            one.wait_send()

    stages = []
    for phase in range(3):
        stages.append(functools.partial(first, phase))
        stages.append(functools.partial(second, phase))
        stages.append(functools.partial(third, phase))
    stages.append(finish)
    return stages


def weight_view(ref):
    def view(chips, j, part):
        start, size = THIRDS[j]
        if part is not None:
            half = size // 256 * 128
            start, size = (start, half) if part == 0 else (start + half, size - half)
        return ref.at[tuple(chips) + (slice(None), pl.ds(start, size))]

    return view


def token_view(ref):
    def view(chips, j, part):
        rows = slice(None) if part is None else pl.ds(part * 32, 32)
        return ref.at[tuple(chips) + (j, rows, slice(None))]

    return view


def params(collective_id=None, vmem=56):
    if collective_id is None:
        return pltpu.CompilerParams(vmem_limit_bytes=vmem * MIB)
    return pltpu.CompilerParams(
        collective_id=collective_id, has_side_effects=True, vmem_limit_bytes=vmem * MIB
    )


ANY = pl.BlockSpec(memory_space=pl.ANY)
VMEM = pl.BlockSpec(memory_space=pltpu.VMEM)
SMEM = pl.BlockSpec(memory_space=pltpu.SMEM)
DMA = pltpu.SemaphoreType.DMA


def shape(dims, dtype):
    return jax.ShapeDtypeStruct(dims, dtype)


def nn(left, right):
    return jnp.dot(left, right, preferred_element_type=jnp.float32)


def nt(left, right):
    return lax.dot_general(
        left, right, (((1,), (1,)), ((), ())), preferred_element_type=jnp.float32
    )


def tn(left, right):
    return lax.dot_general(
        left, right, (((0,), (0,)), ((), ())), preferred_element_type=jnp.float32
    )


def gather_weights_kernel(mine, theirs, ends, small, w, ends_all, small_all, lsem, xs, xr, ss, rs):
    place = position()
    core = lax.axis_index("section")
    meet(place, core=True)
    here = (place["x"], place["y"], place["z"])
    own = w.at[(core,) + here]
    locals_ = [
        pltpu.make_async_copy(mine, own, lsem.at[0]),
        pltpu.make_async_copy(ends, ends_all.at[core], lsem.at[1]),
        pltpu.make_async_copy(small, small_all.at[core], lsem.at[2]),
    ]
    swaps = [
        send(theirs, own, xs.at[0], xr.at[0], other_core()),
        send(ends, ends_all.at[core], xs.at[1], xr.at[1], other_core()),
        send(small, small_all.at[core], xs.at[2], xr.at[2], other_core()),
    ]
    arrivals = [
        send(theirs, w.at[(1 - core,) + here], xs.at[0], xr.at[0], other_core()),
        send(ends, ends_all.at[1 - core], xs.at[1], xr.at[1], other_core()),
        send(small, small_all.at[1 - core], xs.at[2], xr.at[2], other_core()),
    ]
    for one in locals_ + swaps:
        one.start()
    for one in locals_:
        one.wait()
    for one in arrivals:
        one.wait_recv()
    stages = [
        gather_stages(weight_view(w.at[layer]), place, ss.at[layer], rs.at[layer])
        for layer in range(2)
    ]
    for step in zip(*stages):
        for stage in step:
            stage()
    for one in swaps:
        one.wait_send()


def gather_weights(mine, theirs, ends, small):
    return pl.pallas_call(
        gather_weights_kernel,
        out_shape=(
            shape((2, 4, 4, 4, 16, C), jnp.bfloat16),
            shape((2,) + ends.shape, ends.dtype),
            shape((2,) + small.shape, small.dtype),
        ),
        in_specs=[ANY] * 4,
        out_specs=(ANY,) * 3,
        scratch_shapes=[DMA((3,)), DMA((3,)), DMA((3,)), DMA((2, 3, 3, 4)), DMA((2, 3, 3, 4))],
        compiler_params=params(0),
        name="gather_weights",
    )(mine, theirs, ends, small)


def gather_tokens_kernel(own, everything, lsem, ss, rs):
    place = position()
    meet(place)
    local = pltpu.make_async_copy(
        own, everything.at[place["x"], place["y"], place["z"]], lsem
    )
    local.start()
    local.wait()
    for stage in gather_stages(token_view(everything), place, ss, rs):
        stage()


def gather_tokens(own):
    return pl.pallas_call(
        gather_tokens_kernel,
        out_shape=shape((4, 4, 4) + own.shape, own.dtype),
        in_specs=[ANY],
        out_specs=ANY,
        scratch_shapes=[DMA, DMA((3, 3, 4)), DMA((3, 3, 4))],
        compiler_params=params(1),
        name="gather_keys_values",
    )(own)


def scatter_tokens_kernel(terms, out, buf, h0, h1, h2, w0, w1, w2, lsem, ss, rs):
    place = position()
    meet(place)
    load = pltpu.make_async_copy(terms, buf, lsem)
    load.start()
    load.wait()
    halves = [lambda j, k, ref=ref: ref.at[j, k] for ref in (h0, h1, h2)]
    wholes = [lambda j, k, part, ref=ref: ref.at[j, k] for ref in (w0, w1, w2)]

    def final(j, mine, left, right):
        out[j] = (
            mine[...].astype(jnp.float32)
            + left[...].astype(jnp.float32)
            + right[...].astype(jnp.float32)
        )

    for stage in scatter_stages(
        token_view(buf), halves, wholes, place, ss, rs, None, final
    ):
        stage()


def scatter_tokens(terms):
    kv = jnp.bfloat16
    return pl.pallas_call(
        scatter_tokens_kernel,
        out_shape=shape((MB, T, 128), jnp.float32),
        in_specs=[ANY],
        out_specs=VMEM,
        scratch_shapes=[
            pltpu.VMEM((4, 4, 4, MB, T, 128), kv),
            pltpu.VMEM((3, 2, 4, 4, T // 2, 128), kv),
            pltpu.VMEM((3, 2, 4, T // 2, 128), kv),
            pltpu.VMEM((3, 2, T // 2, 128), kv),
            pltpu.VMEM((3, 2, 4, 4, T, 128), kv),
            pltpu.VMEM((3, 2, 4, T, 128), kv),
            pltpu.VMEM((3, 2, T, 128), kv),
            DMA,
            DMA((3, 3, 4)),
            DMA((3, 3, 4)),
        ],
        compiler_params=params(2),
        name="scatter_key_value_grads",
    )(terms)


def pair_mask(base, bounds):
    keys = base + lax.broadcasted_iota(jnp.int32, (KB, 128), 0)
    start, end, own = bounds[0:1, :], bounds[1:2, :], bounds[2:3, :]
    allowed = ((keys >= start) & (keys < end)) | (keys == own)
    bias = jnp.where(allowed, 0.0, MASKED)
    return jnp.concatenate([bias] * 4, axis=1)


def attend_kernel(blocks, qt, kv, bounds, out, lse):
    batch = pl.program_id(0)
    queries = qt[0]

    def step(index, carry):
        top, total, mixed = carry
        rows = kv[pl.ds(index * (KB // T), KB // T), 0].reshape(KB, 128)
        scores = nn(rows, queries) + pair_mask(index * KB, bounds[0])
        new_top = jnp.maximum(top, jnp.max(scores, axis=0, keepdims=True))
        shrink = jnp.exp(top - new_top)
        probs = jnp.exp(scores - new_top)
        total = total * shrink + jnp.sum(probs, axis=0, keepdims=True)
        mixed = mixed * shrink + tn(rows, probs.astype(jnp.bfloat16))
        return new_top, total, mixed

    top, total, mixed = lax.fori_loop(
        blocks[batch, 0],
        blocks[batch, 1],
        step,
        (
            jnp.full((1, QS), MASKED, jnp.float32),
            jnp.zeros((1, QS), jnp.float32),
            jnp.zeros((128, QS), jnp.float32),
        ),
    )
    out[0] = (mixed / total)[64:, :]
    lse[0] = jnp.broadcast_to(top + jnp.log(total), (8, QS))


def attend(blocks, qt, kv, bounds):
    return pl.pallas_call(
        attend_kernel,
        grid=(MB,),
        out_shape=(shape((MB, 64, QS), jnp.float32), shape((MB, 8, QS), jnp.float32)),
        in_specs=[
            SMEM,
            pl.BlockSpec((1, 128, QS), lambda m: (m, 0, 0)),
            pl.BlockSpec((64, 1, T, 128), lambda m: (0, m, 0, 0)),
            pl.BlockSpec((1, 8, 128), lambda m: (m, 0, 0)),
        ],
        out_specs=(
            pl.BlockSpec((1, 64, QS), lambda m: (m, 0, 0)),
            pl.BlockSpec((1, 8, QS), lambda m: (m, 0, 0)),
        ),
        compiler_params=params(),
        name="attention",
    )(blocks, qt, kv, bounds)


def attend_back_kernel(blocks, qt, dot_, kv, bounds, out, lse, dqt, dkv):
    batch = pl.program_id(0)
    queries, grads = qt[0], dot_[0]
    log_total = lse[0, 0:1, :]
    inner = jnp.sum(out[0] * grads[64:, :].astype(jnp.float32), axis=0, keepdims=True)
    dkv[...] = jnp.zeros_like(dkv)

    def step(index, total):
        chips = pl.ds(index * (KB // T), KB // T)
        rows = kv[chips, 0].reshape(KB, 128)
        scores = nn(rows, queries) + pair_mask(index * KB, bounds[0])
        probs = jnp.exp(scores - log_total)
        slopes = (probs * (nn(rows, grads) - inner)).astype(jnp.bfloat16)
        both = nt(slopes, queries) + nt(probs.astype(jnp.bfloat16), grads)
        dkv[chips, 0] = both.astype(jnp.bfloat16).reshape(KB // T, T, 128)
        return total + tn(rows, slopes)

    total = lax.fori_loop(
        blocks[batch, 0], blocks[batch, 1], step, jnp.zeros((128, QS), jnp.float32)
    )
    dqt[0] = total[:64, :] * (1.0 / 8.0)


def attend_back(blocks, qt, dot_, kv, bounds, out, lse):
    return pl.pallas_call(
        attend_back_kernel,
        grid=(MB,),
        out_shape=(
            shape((MB, 64, QS), jnp.float32),
            shape((64, MB, T, 128), jnp.bfloat16),
        ),
        in_specs=[
            SMEM,
            pl.BlockSpec((1, 128, QS), lambda m: (m, 0, 0)),
            pl.BlockSpec((1, 128, QS), lambda m: (m, 0, 0)),
            pl.BlockSpec((64, 1, T, 128), lambda m: (0, m, 0, 0)),
            pl.BlockSpec((1, 8, 128), lambda m: (m, 0, 0)),
            pl.BlockSpec((1, 64, QS), lambda m: (m, 0, 0)),
            pl.BlockSpec((1, 8, QS), lambda m: (m, 0, 0)),
        ],
        out_specs=(
            pl.BlockSpec((1, 64, QS), lambda m: (m, 0, 0)),
            pl.BlockSpec((64, 1, T, 128), lambda m: (0, m, 0, 0)),
        ),
        compiler_params=params(),
        name="attention_back",
    )(blocks, qt, dot_, kv, bounds, out, lse)


def mean_of(values):
    return jnp.sum(values, axis=-1, keepdims=True) * (1.0 / D)


def turn(values, cosine, sine):
    lane = lax.broadcasted_iota(jnp.int32, values.shape, 1) % 64
    swapped = jnp.where(lane < 32, pltpu.roll(values, QS - 32, 1), pltpu.roll(values, 32, 1))
    return values * cosine + swapped * sine


def tiled(table):
    wide = jnp.concatenate([table] * 4, axis=1)
    return jnp.concatenate([wide] * MB, axis=0)


def project_kernel(layer, x, gains, bias, cosine, sine, w, n1, qk, v, wbuf, sem):
    load = pltpu.make_async_copy(w.at[layer, :, :, pl.ds(C_QK, 2 * QS)], wbuf, sem)
    load.start()
    rows = x[...].astype(jnp.float32)
    normed = (rows * lax.rsqrt(mean_of(rows * rows) + EPS) * gains[0:1, :]).astype(jnp.bfloat16)
    n1[...] = normed
    load.wait()
    weights = wbuf[...].reshape(DP, 2 * QS)
    projected = nn(normed, weights[:, : QS + 128]) + bias[0:1, : QS + 128]
    turned = turn(projected[:, :QS], tiled(cosine[...]), tiled(sine[...]))
    qk[...] = turned.astype(jnp.bfloat16)
    v[...] = projected[:, QS:].astype(jnp.bfloat16)


def project(layer, x, gains, bias, cosine, sine, w):
    return pl.pallas_call(
        functools.partial(project_kernel, layer),
        out_shape=(
            shape((R, DP), jnp.bfloat16),
            shape((R, QS), jnp.bfloat16),
            shape((R, 128), jnp.bfloat16),
        ),
        in_specs=[VMEM] * 5 + [ANY],
        out_specs=(VMEM,) * 3,
        scratch_shapes=[pltpu.VMEM((64, 16, 2 * QS), jnp.bfloat16), DMA],
        compiler_params=params(),
        name="project",
    )(x, gains, bias, cosine, sine, w)


def mlp_kernel(
    layer, x, attended, gains, w, xo, mid, n2, gu, hid, sq, wbuf, mine, theirs, wsem, xs, xr
):
    meet(position(), core=True, chips=False)

    def load(index, start, size):
        cols = pl.ds(start, size)
        return pltpu.make_async_copy(
            w.at[layer, :, :, cols], wbuf.at[:, :, cols], wsem.at[index]
        )

    loads = [load(0, C_VO, QS)]
    for index, (start, size) in enumerate(FF_CHUNKS):
        for part in range(3):
            loads.append(load(1 + 3 * index + part, part * FFH + start, size))
    for one in loads:
        one.start()

    def weights(start, size):
        return wbuf[:, :, pl.ds(start, size)].reshape(DP, size)

    def swap(slot):
        return send(
            mine.at[slot], theirs.at[slot], xs.at[slot], xr.at[slot], other_core()
        )

    loads[0].wait()
    mine[0] = nt(attended[...], weights(C_VO, QS))
    one = swap(0)
    one.start()
    one.wait()
    branch = mine[0] + theirs[0]
    rows = x[...].astype(jnp.float32)
    middle = rows + branch
    mid[...] = middle
    normed = (middle * lax.rsqrt(mean_of(middle * middle) + EPS) * gains[1:2, :]).astype(
        jnp.bfloat16
    )
    n2[...] = normed
    total = jnp.zeros((R, DP), jnp.float32)
    for index, (start, size) in enumerate(FF_CHUNKS):
        for part in range(3):
            loads[1 + 3 * index + part].wait()
        gate = nn(normed, weights(start, size))
        up = nn(normed, weights(C_UP + start, size))
        gu[:, pl.ds(start, size)] = gate
        gu[:, pl.ds(C_UP + start, size)] = up
        hidden = (gate * jax.nn.sigmoid(gate) * up).astype(jnp.bfloat16)
        hid[:, pl.ds(start, size)] = hidden
        total = total + nt(hidden, weights(C_DOWN + start, size))
    mine[1] = total
    two = swap(1)
    two.start()
    two.wait()
    out = mine[1] + theirs[1]
    xo[...] = (middle + out).astype(jnp.bfloat16)
    row = lax.broadcasted_iota(jnp.int32, (8, 128), 0)
    lane = lax.broadcasted_iota(jnp.int32, (8, 128), 1)
    sums = jnp.zeros((8, 128), jnp.float32)
    for kind, values in enumerate((rows, branch, out)):
        squares = jnp.sum(values * values, axis=1, keepdims=True)
        for batch in range(MB):
            one = jnp.sum(squares[batch * T : (batch + 1) * T], axis=0, keepdims=True)
            sums = jnp.where((row == batch) & (lane == kind), one, sums)
    sq[...] = sums


def mlp(layer, x, attended, gains, w):
    return pl.pallas_call(
        functools.partial(mlp_kernel, layer),
        out_shape=(
            shape((R, DP), jnp.bfloat16),
            shape((R, DP), jnp.float32),
            shape((R, DP), jnp.bfloat16),
            shape((R, 2 * FFH), jnp.float32),
            shape((R, FFH), jnp.bfloat16),
            shape((8, 128), jnp.float32),
        ),
        in_specs=[VMEM] * 3 + [ANY],
        out_specs=(VMEM,) * 6,
        scratch_shapes=[
            pltpu.VMEM((64, 16, C), jnp.bfloat16),
            pltpu.VMEM((2, R, DP), jnp.float32),
            pltpu.VMEM((2, R, DP), jnp.float32),
            DMA((16,)),
            DMA((2,)),
            DMA((2,)),
        ],
        compiler_params=params(3 + layer),
        name="mlp",
    )(x, attended, gains, w)


def norm_back(grad, rows, gain):
    scale = lax.rsqrt(mean_of(rows * rows) + EPS)
    scaled = grad * gain
    back = scale * scaled - rows * (scale * scale * scale) * mean_of(scaled * rows)
    return back, jnp.sum(grad * rows * scale, axis=0, keepdims=True)


def mlp_back_kernel(
    layer, dout, gu, mid, gains, w, dgu, dmid, da, datt, gain, wbuf, mine, theirs, wsem, xs, xr
):
    meet(position(), core=True, chips=False)

    def load(index, start, size):
        cols = pl.ds(start, size)
        return pltpu.make_async_copy(
            w.at[layer, :, :, cols], wbuf.at[:, :, cols], wsem.at[index]
        )

    loads = []
    for index, (start, size) in enumerate(FF_CHUNKS):
        for part in (2, 0, 1):
            loads.append(load(len(loads), part * FFH + start, size))
    loads.append(load(15, C_VO, QS))
    for one in loads:
        one.start()

    def weights(start, size):
        return wbuf[:, :, pl.ds(start, size)].reshape(DP, size)

    grad_in = dout[...].astype(jnp.float32)
    grad_low = grad_in.astype(jnp.bfloat16)
    total = jnp.zeros((R, DP), jnp.float32)
    for index, (start, size) in enumerate(FF_CHUNKS):
        for part in range(3):
            loads[3 * index + part].wait()
        grad_hidden = nn(grad_low, weights(C_DOWN + start, size))
        gate = gu[:, pl.ds(start, size)]
        up = gu[:, pl.ds(C_UP + start, size)]
        sigma = jax.nn.sigmoid(gate)
        grad_gate = grad_hidden * up * sigma * (1.0 + gate * (1.0 - sigma))
        grad_gate = grad_gate.astype(jnp.bfloat16)
        grad_up = (grad_hidden * gate * sigma).astype(jnp.bfloat16)
        dgu[:, pl.ds(start, size)] = grad_gate
        dgu[:, pl.ds(C_UP + start, size)] = grad_up
        total = total + nt(grad_gate, weights(start, size))
        total = total + nt(grad_up, weights(C_UP + start, size))
    mine[...] = total
    one = send(mine, theirs, xs, xr, other_core())
    one.start()
    one.wait()
    back, gain_row = norm_back(mine[...] + theirs[...], mid[...], gains[1:2, :])
    gain[...] = jnp.broadcast_to(gain_row, (8, DP))
    middle = grad_in + back
    dmid[...] = middle
    low = middle.astype(jnp.bfloat16)
    da[...] = low
    loads[15].wait()
    lane = lax.broadcasted_iota(jnp.int32, (R, QS), 1)
    datt[...] = jnp.where(lane < 64, 0.0, nn(low, weights(C_VO, QS))).astype(jnp.bfloat16)


def mlp_back(layer, dout, gu, mid, gains, w):
    return pl.pallas_call(
        functools.partial(mlp_back_kernel, layer),
        out_shape=(
            shape((R, 2 * FFH), jnp.bfloat16),
            shape((R, DP), jnp.float32),
            shape((R, DP), jnp.bfloat16),
            shape((R, QS), jnp.bfloat16),
            shape((8, DP), jnp.float32),
        ),
        in_specs=[VMEM] * 4 + [ANY],
        out_specs=(VMEM,) * 5,
        scratch_shapes=[
            pltpu.VMEM((64, 16, C), jnp.bfloat16),
            pltpu.VMEM((R, DP), jnp.float32),
            pltpu.VMEM((R, DP), jnp.float32),
            DMA((16,)),
            DMA,
            DMA,
        ],
        compiler_params=params(5 + layer),
        name="mlp_back",
    )(dout, gu, mid, gains, w)


def project_back_kernel(
    layer, dqk, dv, x, dmid, gains, cosine, sine, w, dx, low, vlow, gain, bias,
    wbuf, mine, theirs, wsem, xs, xr,
):
    load = pltpu.make_async_copy(w.at[layer, :, :, pl.ds(C_QK, 2 * QS)], wbuf, wsem)
    load.start()
    meet(position(), core=True, chips=False)
    turned = turn(dqk[...], tiled(cosine[...]), -tiled(sine[...])).astype(jnp.bfloat16)
    low[...] = turned
    values = dv[...].astype(jnp.bfloat16)
    vlow[...] = values
    bias[:, :QS] = jnp.broadcast_to(
        jnp.sum(turned.astype(jnp.float32), axis=0, keepdims=True), (8, QS)
    )
    bias[:, QS:] = jnp.broadcast_to(
        jnp.sum(values.astype(jnp.float32), axis=0, keepdims=True), (8, QS)
    )
    load.wait()
    mine[...] = nt(turned, wbuf[:, :, :QS].reshape(DP, QS)) + nt(
        values, wbuf[:, :, QS:].reshape(DP, QS)
    )
    one = send(mine, theirs, xs, xr, other_core())
    one.start()
    one.wait()
    back, gain_row = norm_back(
        mine[...] + theirs[...], x[...].astype(jnp.float32), gains[0:1, :]
    )
    gain[...] = jnp.broadcast_to(gain_row, (8, DP))
    dx[...] = (dmid[...] + back).astype(jnp.bfloat16)


def project_back(layer, dqk, dv, x, dmid, gains, cosine, sine, w):
    return pl.pallas_call(
        functools.partial(project_back_kernel, layer),
        out_shape=(
            shape((R, DP), jnp.bfloat16),
            shape((R, QS), jnp.bfloat16),
            shape((R, QS), jnp.bfloat16),
            shape((8, DP), jnp.float32),
            shape((8, 2 * QS), jnp.float32),
        ),
        in_specs=[VMEM] * 7 + [ANY],
        out_specs=(VMEM,) * 5,
        scratch_shapes=[
            pltpu.VMEM((64, 16, 2 * QS), jnp.bfloat16),
            pltpu.VMEM((R, DP), jnp.float32),
            pltpu.VMEM((R, DP), jnp.float32),
            DMA,
            DMA,
            DMA,
        ],
        compiler_params=params(7 + layer),
        name="project_back",
    )(dqk, dv, x, dmid, gains, cosine, sine, w)


def weight_grads_kernel(
    sums, n2, dgu, dm, hid, n1, dqk, dv, da, att, small, out, small_out,
    g, h0, h1, h2, w0, w1, w2, sbuf, ss, rs, as_, ar,
):
    place = position()
    meet(place, far=sums)

    def product(start, size, pairs):
        for first in range(0, size, 512):
            wide = min(512, size - first)
            total = sum(
                tn(left[...], right[:, first : first + wide]) for left, right in pairs
            )
            g[:, :, :, :, pl.ds(start + first, wide)] = total.astype(jnp.bfloat16).reshape(
                4, 4, 4, 16, wide
            )

    product(0, 2 * FFH, [(n2, dgu)])
    product(C_DOWN, FFH, [(dm, hid)])
    product(C_QK, QS, [(n1, dqk)])
    product(C_VO, QS, [(n1, dv), (da, att)])

    def spot(j, part):
        size = THIRDS[j][1]
        if part is None:
            return pl.ds(0, size)
        half = size // 256 * 128
        return pl.ds(0, half) if part == 0 else pl.ds(0, size - half)

    halves = [
        lambda j, k, ref=ref: ref.at[(j, k) + (slice(None),) * (ref.ndim - 3) + (spot(j, k),)]
        for ref in (h0, h1, h2)
    ]
    wholes = [
        lambda j, k, part, ref=ref: ref.at[
            (j, k) + (slice(None),) * (ref.ndim - 3) + (spot(j, None),)
        ]
        for ref in (w0, w1, w2)
    ]

    def final(j, mine, left, right):
        out[:, pl.ds(*THIRDS[j])] = (
            mine[...].astype(jnp.float32)
            + left[...].astype(jnp.float32)
            + right[...].astype(jnp.float32)
        )

    stages = scatter_stages(weight_view(g), halves, wholes, place, ss, rs, None, final)
    if sums:
        sbuf[0] = small[...]
        for phase, axis in enumerate("xyz"):
            copies = [
                send(
                    sbuf.at[4 * phase],
                    sbuf.at[4 * phase + k],
                    as_.at[phase, k - 1],
                    ar.at[phase, k - 1],
                    chip_id(moved(place, axis, distance)),
                )
                for k, distance in ((1, 1), (2, -1), (3, 2))
            ]
            for one in copies:
                one.start()
            stages[phase]()
            for one in copies:
                one.wait()
            total = (
                sbuf[4 * phase] + sbuf[4 * phase + 1] + sbuf[4 * phase + 2] + sbuf[4 * phase + 3]
            )
            if phase < 2:
                sbuf[4 * phase + 4] = total
            else:
                small_out[...] = total
        stages = stages[3:]
    else:
        small_out[...] = small[...]
    for stage in stages:
        stage()


def weight_grads(sums, n2, dgu, dm, hid, n1, dqk, dv, da, att, small):
    kind = jnp.bfloat16
    wide = THIRDS[0][1]
    half = THIRDS[0][1] // 2
    return pl.pallas_call(
        functools.partial(weight_grads_kernel, sums),
        out_shape=(shape((16, C), jnp.float32), shape((8, DP), jnp.float32)),
        in_specs=[VMEM] * 10,
        out_specs=(VMEM, VMEM),
        scratch_shapes=[
            pltpu.VMEM((4, 4, 4, 16, C), kind),
            pltpu.VMEM((3, 2, 4, 4, 16, half), kind),
            pltpu.VMEM((3, 2, 4, 16, half), kind),
            pltpu.VMEM((3, 2, 16, half), kind),
            pltpu.VMEM((3, 2, 4, 4, 16, wide), kind),
            pltpu.VMEM((3, 2, 4, 16, wide), kind),
            pltpu.VMEM((3, 2, 16, wide), kind),
            pltpu.VMEM((12, 8, DP), jnp.float32),
            DMA((3, 3, 4)),
            DMA((3, 3, 4)),
            DMA((3, 3)),
            DMA((3, 3)),
        ],
        compiler_params=params(9 + int(sums), vmem=60),
        name="weight_grads",
    )(n2, dgu, dm, hid, n1, dqk, dv, da, att, small)


def shards(
    ends,
    segment_ids,
    valid_blocks,
    qkv_weight,
    qkv_bias,
    out_weight,
    gate_up_weight,
    down_weight,
    norm_gains,
):
    core = lax.axis_index("section")
    chip = lax.axis_index("dp")
    ff = 2 * FFH

    feature = jnp.arange(D, dtype=jnp.int32)
    spread = (
        (feature // 14 * 16 + feature % 14)[:, None] == jnp.arange(DP, dtype=jnp.int32)[None, :]
    ).astype(jnp.bfloat16)

    def widen(rows):
        return nn(rows, spread).astype(jnp.bfloat16)

    def half_of(index):
        pieces = (
            lax.dynamic_slice_in_dim(gate_up_weight[0], index * FFH, FFH, 1),
            lax.dynamic_slice_in_dim(gate_up_weight[0], ff + index * FFH, FFH, 1),
            lax.dynamic_slice_in_dim(down_weight[0], index * FFH, FFH, 1),
            lax.dynamic_slice_in_dim(qkv_weight[0], D + index * 64, 64, 1),
            lax.dynamic_slice_in_dim(qkv_weight[0], index * 448, 448, 1),
            lax.dynamic_slice_in_dim(qkv_weight[0], D + 128 + index * 64, 64, 1),
            lax.dynamic_slice_in_dim(out_weight[0], index * 448, 448, 1),
        )
        return jnp.pad(jnp.concatenate(pieces, axis=1), ((0, 2), (0, 0)))

    small_in = jnp.concatenate(
        [qkv_bias[0], widen(norm_gains[0]).reshape(-1)], axis=0
    )
    small_in = jnp.broadcast_to(small_in[None], (16, small_in.shape[0]))
    small_in = jnp.pad(small_in, ((0, 0), (0, 3328 - small_in.shape[1])))
    w6, ends_all, small_all = gather_weights(
        half_of(core), half_of(1 - core), widen(ends[0].reshape(R, D)), small_in
    )
    w = w6.reshape(2, 64, 16, C)

    def bias_of(layer):
        row = small_all[layer, 0, :1152].astype(jnp.float32)
        pieces = (
            lax.dynamic_slice_in_dim(row, D + core * 64, 64),
            lax.dynamic_slice_in_dim(row, core * 448, 448),
            lax.dynamic_slice_in_dim(row, D + 128 + core * 64, 64),
            jnp.zeros((448,), jnp.float32),
        )
        return jnp.broadcast_to(jnp.concatenate(pieces)[None], (8, 2 * QS))

    def gains_of(layer):
        both = small_all[layer, 0, 1152:3200].astype(jnp.float32).reshape(2, DP)
        return jnp.pad(both, ((0, 6), (0, 0)))

    places = chip * T + jnp.arange(T, dtype=jnp.int32)
    frequency = THETA ** (-jnp.arange(32, dtype=jnp.float32) * 2.0 / 64)
    angles = places.astype(jnp.float32)[:, None] * frequency[None, :]
    cosine = jnp.tile(jnp.cos(angles), (1, 4))
    sine = jnp.sin(angles)
    sine = jnp.tile(jnp.concatenate([-sine, sine], axis=1), (1, 2))

    own_ids = lax.dynamic_slice_in_dim(segment_ids, chip * T, T, 1)
    starts = jnp.sum(
        (segment_ids[:, None, :] < own_ids[:, :, None]).astype(jnp.int32), axis=2
    )
    lengths = jnp.sum(valid_blocks, axis=1) * 128
    finish = jnp.minimum(places[None, :] + 1, lengths[:, None])
    bounds = jnp.stack([starts, finish, jnp.broadcast_to(places[None], (MB, T))], axis=1)
    bounds = jnp.pad(jnp.tile(bounds, (1, 1, 2)), ((0, 0), (0, 5), (0, 0)))
    last = (chip * T + T + KB - 1) // KB
    blocks = jnp.stack([starts[:, 0] // KB, jnp.full((MB,), last, jnp.int32)], axis=1)

    def to_columns(rows):
        turned = rows.reshape(MB, T, 8, 64).transpose(0, 3, 2, 1)
        return turned.at[:, :, 0].set(0).reshape(MB, 64, QS)

    def to_rows(columns):
        return columns.reshape(MB, 64, 8, T).transpose(0, 3, 2, 1).reshape(R, 8, 64)

    saved = []
    x = ends_all[0]
    for layer in range(2):
        gains = gains_of(layer)
        n1, qk, v = project(layer, x, gains, bias_of(layer), cosine, sine, w)
        own = jnp.concatenate([qk[:, :64], v[:, :64]], axis=1).reshape(MB, T, 128)
        kv = gather_tokens(own).reshape(64, MB, T, 128)
        qt = jnp.pad(to_columns(qk) * jnp.bfloat16(0.125), ((0, 0), (0, 64), (0, 0)))
        mixed, lse = attend(blocks, qt, kv, bounds)
        attended = to_rows(mixed).astype(jnp.bfloat16).at[:, 0].set(0).reshape(R, QS)
        xo, mid, n2, gu, hid, sq = mlp(layer, x, attended, gains, w)
        saved.append((x, gains, n1, kv, qt, mixed, lse, attended, mid, n2, gu, hid, sq))
        x = xo
    final_out = x

    dout = ends_all[1]
    grads = [None, None]
    smalls = [None, None]
    for layer in (1, 0):
        x, gains, n1, kv, qt, mixed, lse, attended, mid, n2, gu, hid, sq = saved[layer]
        dgu, dmid, da, datt, gain_two = mlp_back(layer, dout, gu, mid, gains, w)
        dot_ = jnp.pad(to_columns(datt), ((0, 0), (64, 0), (0, 0)))
        dqt, terms = attend_back(blocks, qt, dot_, kv, bounds, mixed, lse)
        own = scatter_tokens(terms.reshape(4, 4, 4, MB, T, 128)).reshape(R, 128)
        dqk = to_rows(dqt).at[:, 0].set(own[:, :64]).reshape(R, QS)
        dv = jnp.pad(own[:, 64:], ((0, 0), (0, QS - 64)))
        dx, dqk_low, dv_low, gain_one, bias_sum = project_back(
            layer, dqk, dv, x, dmid, gains, cosine, sine, w
        )
        valid = lax.dynamic_slice_in_dim(valid_blocks, chip // 2, 1, 1).astype(jnp.float32)
        squares = jnp.where(valid > 0, sq[:MB, :3], 0.0)
        smalls[layer] = jnp.stack(
            [
                gain_one[0],
                gain_two[0],
                bias_sum[0],
                jnp.pad(squares.reshape(-1), (0, DP - 9)),
            ]
        )
        small = jnp.concatenate(smalls, axis=0) if layer == 0 else jnp.zeros((8, DP), jnp.float32)
        grads[layer], small_sum = weight_grads(
            layer == 0, n2, dgu, dout, hid, n1, dqk_low, dv_low, da, attended, small
        )
        dout = dx

    def with_bias(layer):
        return grads[layer].at[14, :QS].set(small_sum[4 * layer + 2, :QS]).at[
            14, QS : 2 * QS
        ].set(small_sum[4 * layer + 2, QS:])

    ready = [with_bias(0), with_bias(1)]
    here = jnp.where(core == 0, ready[0], ready[1])
    away = lax.ppermute(jnp.where(core == 0, ready[1], ready[0]), "section", [(0, 1), (1, 0)])
    lower = jnp.where(core == 0, here, away)
    upper = jnp.where(core == 0, away, here)
    sides = (lower, upper)

    def column(start, size):
        return [side[:14, start : start + size] for side in sides]

    grad_gu = jnp.concatenate(column(0, FFH) + column(C_UP, FFH), axis=1)
    grad_down = jnp.concatenate(column(C_DOWN, FFH), axis=1)
    grad_qkv = jnp.concatenate(
        column(C_QK + 64, 448) + column(C_QK, 64) + column(C_VO, 64), axis=1
    )
    grad_out = jnp.concatenate(column(C_VO + 64, 448), axis=1)
    bias_rows = [side[14] for side in sides]
    grad_bias = jnp.concatenate(
        [row[64:QS] for row in bias_rows]
        + [row[:64] for row in bias_rows]
        + [row[QS : QS + 64] for row in bias_rows]
    )
    own_small = lax.dynamic_slice_in_dim(small_sum, 4 * core, 4, 0)
    grad_gain = own_small[:2].reshape(2, 64, 16)[:, :, :14].reshape(2, D)
    counts = jnp.sum(valid_blocks, axis=1).astype(jnp.float32) * 128 * D
    rms = jnp.sqrt(own_small[3, :9].reshape(MB, 3) / counts[:, None])
    ends_out = jnp.where(core == 0, dout, final_out)
    boundary = nt(ends_out, spread).astype(jnp.bfloat16).reshape(1, MB, T, D)
    return (
        boundary,
        grad_qkv[None],
        grad_bias[None],
        grad_out[None],
        grad_gu[None],
        grad_down[None],
        grad_gain[None],
        rms[None],
    )


def solution(mesh):
    in_specs = (
        P("section", None, "dp", None),
        P(),
        P(),
        P("section", "dp", None),
        P("section", None),
        P("section", "dp", None),
        P("section", "dp", None),
        P("section", "dp", None),
        P("section", None, None),
    )
    out_specs = (
        P("section", None, "dp", None),
        P("section", "dp", None),
        P("section", None),
        P("section", "dp", None),
        P("section", "dp", None),
        P("section", "dp", None),
        P("section", None, None),
        P("section", None, None),
    )
    return jax.shard_map(shards, mesh=mesh, in_specs=in_specs, out_specs=out_specs, check_vma=False)
```

```python
import functools
import math

import jax
import jax.numpy as jnp
from jax import lax
from jax.experimental import pallas as pl
from jax.experimental.pallas import tpu as pltpu
from jax.sharding import PartitionSpec as P

MESH = pl.DeviceIdType.MESH
EPS = 1e-06
THETA = 1000000.0
MASKED = -1e30

MB = 3
T = 64
R = MB * T
D = 896
DP = 1024
FFH = 2432
QS = 512
C_UP, C_DOWN, C_QK, C_VO, C = FFH, 2 * FFH, 3 * FFH, 3 * FFH + QS, 3 * FFH + 2 * QS
KB = 512
SEQ = 4096
MIB = 1024 * 1024

THIRDS = ((0, 22 * 128), (22 * 128, 22 * 128), (44 * 128, 21 * 128))
ORDERS = (("z", "y", "x"), ("y", "x", "z"), ("x", "z", "y"))
CM, CA = 3 * FFH, 2 * QS
M_THIRDS = ((0, FFH), (FFH, FFH), (2 * FFH, FFH))
A_THIRDS = ((0, 384), (384, 384), (768, 256))
FF_CHUNKS = ((0, 512), (512, 512), (1024, 512), (1536, 512), (2048, 384))


def position():
    chip = lax.axis_index("dp")
    return {"x": chip // 16, "y": (chip // 4) % 4, "z": chip % 4}


def moved(place, axis, distance):
    other = dict(place)
    other[axis] = (place[axis] + distance + 4) % 4
    return other


def chip_id(place):
    return {"dp": place["x"] * 16 + place["y"] * 4 + place["z"]}


def other_core():
    return {"section": 1 - lax.axis_index("section")}


def meet(place, core=False, chips=True, far=False):
    barrier = pltpu.get_barrier_semaphore()
    count = 0
    if chips:
        for axis in "xyz":
            for distance in (1, -1, 2) if far else (1, -1):
                pl.semaphore_signal(
                    barrier,
                    inc=1,
                    device_id=chip_id(moved(place, axis, distance)),
                    device_id_type=MESH,
                )
                count += 1
    if core:
        pl.semaphore_signal(barrier, inc=1, device_id=other_core(), device_id_type=MESH)
        count += 1
    pl.semaphore_wait(barrier, count)


def send(src, dst, send_sem, recv_sem, device):
    return pltpu.make_async_remote_copy(
        src, dst, send_sem, recv_sem, device_id=device, device_id_type=MESH
    )


def cube(done, place):
    return tuple(slice(None) if axis in done else place[axis] for axis in "xyz")


def gather_stages(view, place, send_sems, recv_sems):
    pending = []

    def copy(j, phase, k, whose, part, distance):
        ref = view(cube(ORDERS[j][:phase], whose), j, part)
        return send(
            ref,
            ref,
            send_sems.at[j, phase, k],
            recv_sems.at[j, phase, k],
            chip_id(moved(place, ORDERS[j][phase], distance)),
        )

    def first(phase):
        for j in range(3):
            for k, distance in ((0, 1), (1, -1)):
                one = copy(j, phase, k, place, None, distance)
                one.start()
                pending.append(one)

    def second(phase):
        for j in range(3):
            for k, distance in ((0, 1), (1, -1)):
                whose = moved(place, ORDERS[j][phase], -distance)
                copy(j, phase, k, whose, None, distance).wait_recv()
                one = copy(j, phase, 2 + k, whose, k, distance)
                one.start()
                pending.append(one)

    def third(phase):
        for j in range(3):
            for k, distance in ((0, 1), (1, -1)):
                whose = moved(place, ORDERS[j][phase], 2)
                copy(j, phase, 2 + k, whose, k, distance).wait_recv()

    def finish():
        for one in pending:
            one.wait_send()

    stages = []
    for phase in range(3):
        stages.append(functools.partial(first, phase))
        stages.append(functools.partial(second, phase))
        stages.append(functools.partial(third, phase))
    stages.append(finish)
    return stages


def scatter_stages(view, halves, wholes, place, send_sems, recv_sems, width, final):
    pending = []

    def chips_of(j, phase, whose):
        order = ORDERS[j][::-1]
        return cube(order[phase + 1 :], whose)

    def axis_of(j, phase):
        return ORDERS[j][::-1][phase]

    def add(dst, *terms):
        dst[...] = sum(term[...].astype(jnp.float32) for term in terms).astype(dst.dtype)

    def half_copy(j, phase, k, distance):
        src = view(chips_of(j, phase, moved(place, axis_of(j, phase), 2)), j, k)
        return send(
            src,
            halves[phase](j, k),
            send_sems.at[j, phase, k],
            recv_sems.at[j, phase, k],
            chip_id(moved(place, axis_of(j, phase), distance)),
        )

    def whole_copy(j, phase, k, distance):
        src = view(chips_of(j, phase, moved(place, axis_of(j, phase), distance)), j, None)
        return send(
            src,
            wholes[phase](j, k, None),
            send_sems.at[j, phase, 2 + k],
            recv_sems.at[j, phase, 2 + k],
            chip_id(moved(place, axis_of(j, phase), distance)),
        )

    def first(phase):
        for j in range(3):
            for k, distance in ((0, 1), (1, -1)):
                one = half_copy(j, phase, k, distance)
                one.start()
                pending.append(one)

    def second(phase):
        for j in range(3):
            for k, distance in ((0, 1), (1, -1)):
                half_copy(j, phase, k, distance).wait_recv()
                mine = view(chips_of(j, phase, moved(place, axis_of(j, phase), distance)), j, k)
                add(mine, mine, halves[phase](j, k))
                one = whole_copy(j, phase, k, distance)
                one.start()
                pending.append(one)

    def third(phase):
        for j in range(3):
            for k, distance in ((0, 1), (1, -1)):
                whole_copy(j, phase, k, distance).wait_recv()
            mine = view(chips_of(j, phase, place), j, None)
            if phase < 2:
                add(mine, mine, wholes[phase](j, 0, None), wholes[phase](j, 1, None))
            else:
                final(j, mine, wholes[phase](j, 0, None), wholes[phase](j, 1, None))

    def finish():
        for one in pending:
            one.wait_send()

    stages = []
    for phase in range(3):
        stages.append(functools.partial(first, phase))
        stages.append(functools.partial(second, phase))
        stages.append(functools.partial(third, phase))
    stages.append(finish)
    return stages


def weight_view(ref, thirds=THIRDS):
    def view(chips, j, part):
        start, size = thirds[j]
        if part is not None:
            half = size // 256 * 128
            start, size = (start, half) if part == 0 else (start + half, size - half)
        return ref.at[tuple(chips) + (slice(None), pl.ds(start, size))]

    return view


def token_view(ref):
    def view(chips, j, part):
        rows = slice(None) if part is None else pl.ds(part * 32, 32)
        return ref.at[tuple(chips) + (j, rows, slice(None))]

    return view


def params(collective_id=None, vmem=56):
    if collective_id is None:
        return pltpu.CompilerParams(vmem_limit_bytes=vmem * MIB)
    return pltpu.CompilerParams(
        collective_id=collective_id, has_side_effects=True, vmem_limit_bytes=vmem * MIB
    )


ANY = pl.BlockSpec(memory_space=pl.ANY)
VMEM = pl.BlockSpec(memory_space=pltpu.VMEM)
SMEM = pl.BlockSpec(memory_space=pltpu.SMEM)
DMA = pltpu.SemaphoreType.DMA


def shape(dims, dtype):
    return jax.ShapeDtypeStruct(dims, dtype)


def nn(left, right):
    return jnp.dot(left, right, preferred_element_type=jnp.float32)


def nt(left, right):
    return lax.dot_general(
        left, right, (((1,), (1,)), ((), ())), preferred_element_type=jnp.float32
    )


def tn(left, right):
    return lax.dot_general(
        left, right, (((0,), (0,)), ((), ())), preferred_element_type=jnp.float32
    )


def scatter_tokens_kernel(terms, out, buf, h0, h1, h2, w0, w1, w2, lsem, ss, rs):
    place = position()
    meet(place)
    load = pltpu.make_async_copy(terms, buf, lsem)
    load.start()
    load.wait()
    halves = [lambda j, k, ref=ref: ref.at[j, k] for ref in (h0, h1, h2)]
    wholes = [lambda j, k, part, ref=ref: ref.at[j, k] for ref in (w0, w1, w2)]

    def final(j, mine, left, right):
        out[j] = (
            mine[...].astype(jnp.float32)
            + left[...].astype(jnp.float32)
            + right[...].astype(jnp.float32)
        )

    for stage in scatter_stages(
        token_view(buf), halves, wholes, place, ss, rs, None, final
    ):
        stage()


def scatter_tokens(terms):
    kv = jnp.bfloat16
    return pl.pallas_call(
        scatter_tokens_kernel,
        out_shape=shape((MB, T, 128), jnp.float32),
        in_specs=[ANY],
        out_specs=VMEM,
        scratch_shapes=[
            pltpu.VMEM((4, 4, 4, MB, T, 128), kv),
            pltpu.VMEM((3, 2, 4, 4, T // 2, 128), kv),
            pltpu.VMEM((3, 2, 4, T // 2, 128), kv),
            pltpu.VMEM((3, 2, T // 2, 128), kv),
            pltpu.VMEM((3, 2, 4, 4, T, 128), kv),
            pltpu.VMEM((3, 2, 4, T, 128), kv),
            pltpu.VMEM((3, 2, T, 128), kv),
            DMA,
            DMA((3, 3, 4)),
            DMA((3, 3, 4)),
        ],
        compiler_params=params(2),
        name="scatter_key_value_grads",
    )(terms)


def pair_mask(base, bounds):
    keys = base + lax.broadcasted_iota(jnp.int32, (KB, 128), 0)
    start, end, own = bounds[0:1, :], bounds[1:2, :], bounds[2:3, :]
    allowed = ((keys >= start) & (keys < end)) | (keys == own)
    bias = jnp.where(allowed, 0.0, MASKED)
    return jnp.concatenate([bias] * 4, axis=1)


def attend_back_kernel(blocks, qt, dot_, kv, bounds, out, lse, dqt, dkv):
    batch = pl.program_id(0)
    queries, grads = qt[0], dot_[0]
    log_total = lse[0, 0:1, :]
    inner = jnp.sum(out[0] * grads[64:, :].astype(jnp.float32), axis=0, keepdims=True)
    dkv[...] = jnp.zeros_like(dkv)

    def step(index, total):
        chips = pl.ds(index * (KB // T), KB // T)
        rows = kv[chips, 0].reshape(KB, 128)
        scores = nn(rows, queries) + pair_mask(index * KB, bounds[0])
        probs = jnp.exp(scores - log_total)
        slopes = (probs * (nn(rows, grads) - inner)).astype(jnp.bfloat16)
        both = nt(slopes, queries) + nt(probs.astype(jnp.bfloat16), grads)
        dkv[chips, 0] = both.astype(jnp.bfloat16).reshape(KB // T, T, 128)
        return total + tn(rows, slopes)

    total = lax.fori_loop(
        blocks[batch, 0], blocks[batch, 1], step, jnp.zeros((128, QS), jnp.float32)
    )
    dqt[0] = total[:64, :] * (1.0 / 8.0)


def attend_back(blocks, qt, dot_, kv, bounds, out, lse):
    return pl.pallas_call(
        attend_back_kernel,
        grid=(MB,),
        out_shape=(
            shape((MB, 64, QS), jnp.float32),
            shape((64, MB, T, 128), jnp.bfloat16),
        ),
        in_specs=[
            SMEM,
            pl.BlockSpec((1, 128, QS), lambda m: (m, 0, 0)),
            pl.BlockSpec((1, 128, QS), lambda m: (m, 0, 0)),
            pl.BlockSpec((64, 1, T, 128), lambda m: (0, m, 0, 0)),
            pl.BlockSpec((1, 8, 128), lambda m: (m, 0, 0)),
            pl.BlockSpec((1, 64, QS), lambda m: (m, 0, 0)),
            pl.BlockSpec((1, 8, QS), lambda m: (m, 0, 0)),
        ],
        out_specs=(
            pl.BlockSpec((1, 64, QS), lambda m: (m, 0, 0)),
            pl.BlockSpec((64, 1, T, 128), lambda m: (0, m, 0, 0)),
        ),
        compiler_params=params(),
        name="attention_back",
    )(blocks, qt, dot_, kv, bounds, out, lse)


def mean_of(values):
    return jnp.sum(values, axis=-1, keepdims=True) * (1.0 / D)


def turn(values, cosine, sine):
    lane = lax.broadcasted_iota(jnp.int32, values.shape, 1) % 64
    swapped = jnp.where(lane < 32, pltpu.roll(values, QS - 32, 1), pltpu.roll(values, 32, 1))
    return values * cosine + swapped * sine


def tiled(table):
    wide = jnp.concatenate([table] * 4, axis=1)
    return jnp.concatenate([wide] * MB, axis=0)


def to_columns(rows):
    turned = rows.T
    return jnp.concatenate([turned[64 * h : 64 * h + 64] for h in range(8)], axis=1)


def to_rows(columns):
    pairs = []
    for pair in range(4):
        turned = columns[:, 128 * pair : 128 * pair + 128].T
        pairs.append(jnp.concatenate([turned[:64], turned[64:]], axis=1))
    return jnp.concatenate(pairs, axis=1)


def without_first_slot(rows):
    lane = lax.broadcasted_iota(jnp.int32, rows.shape, 1)
    return jnp.where(lane < 64, 0.0, rows)


def forward_kernel(
    mat, tat, mml, tml, ends, small, cosine, sine, bounds,
    wa, wm, kv, gu, cot, gains, n1, qt, mixed, lse, att, mid, n2, hid, xs_, sq,
    ends_v, small_v, stage_a, stage_m, wat, wml, kvb, gu_v, mine, theirs,
    lsem, ssem, rsem, a_s, a_r, m_s, m_r, k_s, k_r, osem, wsem, xsem, xrsem,
):
    place = position()
    core = lax.axis_index("section")
    chip = lax.axis_index("dp")
    here = (place["x"], place["y"], place["z"])
    meet(place, core=True)

    traded = ((mat, tat, stage_a), (mml, tml, stage_m), (ends, ends, ends_v), (small, small, small_v))
    trades = []
    for index, (keep, give, dst) in enumerate(traded):
        local = pltpu.make_async_copy(keep, dst.at[core], lsem.at[index])
        out = send(give, dst.at[core], ssem.at[index], rsem.at[index], other_core())
        back = send(give, dst.at[1 - core], ssem.at[index], rsem.at[index], other_core())
        local.start()
        out.start()
        trades.append((local, out, back))

    def arrive(index):
        local, out, back = trades[index]
        local.wait()
        back.wait_recv()
        out.wait_send()

    arrive(0)
    into = [
        pltpu.make_async_copy(stage_a.at[layer], wat.at[(layer,) + here], lsem.at[4 + layer])
        for layer in range(2)
    ]
    for one in into:
        one.start()
    for one in into:
        one.wait()
    attn = [
        gather_stages(weight_view(wat.at[layer], A_THIRDS), place, a_s.at[layer], a_r.at[layer])
        for layer in range(2)
    ]
    feed = [
        gather_stages(weight_view(wml, M_THIRDS), place, m_s.at[0], m_r.at[0]),
        gather_stages(weight_view(wm.at[1], M_THIRDS), place, m_s.at[1], m_r.at[1]),
    ]
    keys = [
        gather_stages(token_view(kvb.at[layer]), place, k_s.at[layer], k_r.at[layer])
        for layer in range(2)
    ]
    attn[0][0]()
    arrive(1)
    into = [
        pltpu.make_async_copy(stage_m.at[0], wml.at[here], lsem.at[4]),
        pltpu.make_async_copy(stage_m.at[1], wm.at[(1,) + here], lsem.at[5]),
    ]
    for one in into:
        one.start()
    for one in into:
        one.wait()
    feed[0][0]()
    attn[0][1]()
    feed[0][1]()
    attn[0][2]()
    attn[0][3]()
    feed[0][2]()
    feed[0][3]()
    attn[0][4]()
    attn[0][5]()
    attn[0][6]()
    attn[0][7]()
    arrive(2)
    arrive(3)
    cot[...] = ends_v[...]
    for layer in range(2):
        gains[layer] = small_v[layer, 0:8, :].astype(jnp.float32)
    attn[0][8]()

    outs = []

    def store(src, dst, index):
        one = pltpu.make_async_copy(src, dst, osem.at[index])
        one.start()
        outs.append(one)

    def rows_of(layer):
        return ends_v[0] if layer == 0 else xs_[0]

    def project(layer):
        rows = rows_of(layer).astype(jnp.float32)
        gain = gains[layer, 2:3, :]
        bias = jnp.where(core == 0, gains[layer, 0:1, :], gains[layer, 1:2, :])
        normed = (rows * lax.rsqrt(mean_of(rows * rows) + EPS) * gain).astype(jnp.bfloat16)
        n1[layer] = normed
        weights = wat[layer].reshape(DP, CA)
        projected = nn(normed, weights[:, : QS + 128]) + bias[:, : QS + 128]
        turned = turn(projected[:, :QS], tiled(cosine[...]), tiled(sine[...]))
        own = jnp.concatenate([turned[:, :64], projected[:, QS : QS + 64]], axis=1)
        kvb[(layer,) + here] = own.astype(jnp.bfloat16).reshape(MB, T, 128)
        heads = without_first_slot(turned).astype(jnp.bfloat16).astype(jnp.float32) * 0.125
        for batch in range(MB):
            columns = to_columns(heads[batch * T : (batch + 1) * T]).astype(jnp.bfloat16)
            qt[layer, batch] = jnp.concatenate([columns, jnp.zeros_like(columns)], axis=0)

    def attend(layer, batch):
        queries = qt[layer, batch]
        limits = bounds[batch]

        def step(index, carry):
            top, total, sums = carry
            rows = kvb[layer, index // 2, pl.ds(index % 2 * 2, 2), :, batch].reshape(KB, 128)
            scores = nn(rows, queries) + pair_mask(index * KB, limits)
            new_top = jnp.maximum(top, jnp.max(scores, axis=0, keepdims=True))
            shrink = jnp.exp(top - new_top)
            probs = jnp.exp(scores - new_top)
            total = total * shrink + jnp.sum(probs, axis=0, keepdims=True)
            sums = sums * shrink + tn(rows, probs.astype(jnp.bfloat16))
            return new_top, total, sums

        top, total, sums = lax.fori_loop(
            0,
            (chip * T + T + KB - 1) // KB,
            step,
            (
                jnp.full((1, QS), MASKED, jnp.float32),
                jnp.zeros((1, QS), jnp.float32),
                jnp.zeros((128, QS), jnp.float32),
            ),
        )
        result = (sums / total)[64:, :]
        mixed[layer, batch] = result
        lse[layer, batch] = jnp.broadcast_to(top + jnp.log(total), (8, QS))
        att[layer, pl.ds(batch * T, T), :] = without_first_slot(to_rows(result)).astype(
            jnp.bfloat16
        )

    def swap(slot):
        return send(mine.at[slot], theirs.at[slot], xsem.at[slot], xrsem.at[slot], other_core())

    def branch_of(layer):
        mine[0] = nt(att[layer], wat[layer, :, :, :, :, QS:].reshape(DP, QS))
        one = swap(0)
        one.start()
        one.wait()
        branch = mine[0] + theirs[0]
        middle = rows_of(layer).astype(jnp.float32) + branch
        mid[layer] = middle
        scale = lax.rsqrt(mean_of(middle * middle) + EPS)
        n2[layer] = (middle * scale * gains[layer, 3:4, :]).astype(jnp.bfloat16)
        return branch

    def feed_forward(layer, branch, hooks):
        normed = n2[layer]
        sums = jnp.zeros((R, DP), jnp.float32)
        for index, (start, size) in enumerate(FF_CHUNKS):
            hooks[index]()

            def weights(first, start=start, size=size):
                return wml[:, :, :, :, pl.ds(first + start, size)].reshape(DP, size)

            gate = nn(normed, weights(0))
            up = nn(normed, weights(FFH))
            gu_v[:, pl.ds(start, size)] = gate
            gu_v[:, pl.ds(FFH + start, size)] = up
            hidden = (gate * jax.nn.sigmoid(gate) * up).astype(jnp.bfloat16)
            hid[layer, :, pl.ds(start, size)] = hidden
            sums = sums + nt(hidden, weights(2 * FFH))
        store(gu_v, gu.at[layer], 4 + layer)
        mine[1] = sums
        one = swap(1)
        one.start()
        one.wait()
        result = mine[1] + theirs[1]
        middle = mid[layer]
        xs_[layer] = (middle + result).astype(jnp.bfloat16)
        rows = rows_of(layer).astype(jnp.float32)
        row = lax.broadcasted_iota(jnp.int32, (8, 128), 0)
        lane = lax.broadcasted_iota(jnp.int32, (8, 128), 1)
        table = jnp.zeros((8, 128), jnp.float32)
        for kind, values in enumerate((rows, branch, result)):
            squares = jnp.sum(values * values, axis=1, keepdims=True)
            for batch in range(MB):
                one = jnp.sum(squares[batch * T : (batch + 1) * T], axis=0, keepdims=True)
                table = jnp.where((row == batch) & (lane == kind), one, table)
        sq[layer] = table

    def nothing():
        pass

    project(0)
    keys[0][0]()
    attn[1][0]()
    feed[0][4]()
    keys[0][1]()
    attn[1][1]()
    keys[0][2]()
    keys[0][3]()
    attn[1][2]()
    attn[1][3]()
    feed[0][5]()
    keys[0][4]()
    attn[1][4]()
    keys[0][5]()
    keys[0][6]()
    attn[1][5]()
    attn[1][6]()
    keys[0][7]()
    feed[0][6]()
    feed[1][0]()
    keys[0][8]()
    store(kvb.at[0], kv.at[0], 0)
    attend(0, 0)
    feed[1][1]()
    attn[1][7]()
    attend(0, 1)
    feed[0][7]()
    feed[1][2]()
    feed[1][3]()
    attend(0, 2)
    feed[1][4]()
    attn[1][8]()
    store(wat, wa, 1)
    branch = branch_of(0)
    feed[1][5]()
    feed[0][8]()
    feed[1][6]()
    store(wml, wm.at[0], 2)
    feed_forward(0, branch, [nothing] * 5)
    project(1)
    for stage in keys[1][:8]:
        stage()
    feed[1][7]()
    keys[1][8]()
    store(kvb.at[1], kv.at[1], 3)
    for batch in range(MB):
        attend(1, batch)
    branch = branch_of(1)
    feed[1][8]()
    feed[0][9]()
    outs[2].wait()
    outs[3].wait()
    loads = []
    for index, (start, size) in enumerate(FF_CHUNKS):
        for part in range(3):
            cols = pl.ds(part * FFH + start, size)
            loads.append(
                pltpu.make_async_copy(
                    wm.at[1, :, :, :, :, cols],
                    wml.at[:, :, :, :, cols],
                    wsem.at[3 * index + part],
                )
            )
    for one in loads:
        one.start()

    def ready(index):
        for one in loads[3 * index : 3 * index + 3]:
            one.wait()

    feed_forward(1, branch, [functools.partial(ready, index) for index in range(5)])
    for index, one in enumerate(outs):
        if index not in (2, 3):
            one.wait()
    for stages in attn + feed[1:] + keys:
        stages[9]()


def forward(mat, tat, mml, tml, ends, small, cosine, sine, bounds):
    low, full = jnp.bfloat16, jnp.float32
    return pl.pallas_call(
        forward_kernel,
        out_shape=(
            shape((2, 4, 4, 4, 16, CA), low),
            shape((2, 4, 4, 4, 16, CM), low),
            shape((2, 4, 4, 4, MB, T, 128), low),
            shape((2, R, 2 * FFH), full),
            shape((2, R, DP), low),
            shape((2, 8, DP), full),
            shape((2, R, DP), low),
            shape((2, MB, 128, QS), low),
            shape((2, MB, 64, QS), full),
            shape((2, MB, 8, QS), full),
            shape((2, R, QS), low),
            shape((2, R, DP), full),
            shape((2, R, DP), low),
            shape((2, R, FFH), low),
            shape((2, R, DP), low),
            shape((2, 8, 128), full),
        ),
        in_specs=[ANY] * 6 + [VMEM] * 3,
        out_specs=(ANY,) * 4 + (VMEM,) * 12,
        scratch_shapes=[
            pltpu.VMEM((2, R, DP), low),
            pltpu.VMEM((2, 16, DP), low),
            pltpu.VMEM((2, 16, CA), low),
            pltpu.VMEM((2, 16, CM), low),
            pltpu.VMEM((2, 4, 4, 4, 16, CA), low),
            pltpu.VMEM((4, 4, 4, 16, CM), low),
            pltpu.VMEM((2, 4, 4, 4, MB, T, 128), low),
            pltpu.VMEM((R, 2 * FFH), full),
            pltpu.VMEM((2, R, DP), full),
            pltpu.VMEM((2, R, DP), full),
            DMA((6,)),
            DMA((4,)),
            DMA((4,)),
            DMA((2, 3, 3, 4)),
            DMA((2, 3, 3, 4)),
            DMA((2, 3, 3, 4)),
            DMA((2, 3, 3, 4)),
            DMA((2, 3, 3, 4)),
            DMA((2, 3, 3, 4)),
            DMA((6,)),
            DMA((15,)),
            DMA((2,)),
            DMA((2,)),
        ],
        compiler_params=params(0, vmem=60),
        name="forward",
    )(mat, tat, mml, tml, ends, small, cosine, sine, bounds)


def norm_back(grad, rows, gain):
    scale = lax.rsqrt(mean_of(rows * rows) + EPS)
    scaled = grad * gain
    back = scale * scaled - rows * (scale * scale * scale) * mean_of(scaled * rows)
    return back, jnp.sum(grad * rows * scale, axis=0, keepdims=True)


def mlp_back_kernel(
    layer, dout, gu, mid, gains, wa, wm, dgu, dmid, da, datt, gain, wbuf, mine, theirs, wsem, xs, xr
):
    meet(position(), core=True, chips=False)

    def load(index, start, size):
        cols = pl.ds(start, size)
        return pltpu.make_async_copy(
            wm.at[layer, :, :, cols], wbuf.at[:, :, cols], wsem.at[index]
        )

    loads = []
    for index, (start, size) in enumerate(FF_CHUNKS):
        for part in (2, 0, 1):
            loads.append(load(len(loads), part * FFH + start, size))
    loads.append(
        pltpu.make_async_copy(
            wa.at[layer, :, :, pl.ds(QS, QS)], wbuf.at[:, :, pl.ds(CM, QS)], wsem.at[15]
        )
    )
    for one in loads:
        one.start()

    def weights(start, size):
        return wbuf[:, :, pl.ds(start, size)].reshape(DP, size)

    grad_in = dout[...].astype(jnp.float32)
    grad_low = grad_in.astype(jnp.bfloat16)
    total = jnp.zeros((R, DP), jnp.float32)
    for index, (start, size) in enumerate(FF_CHUNKS):
        for part in range(3):
            loads[3 * index + part].wait()
        grad_hidden = nn(grad_low, weights(C_DOWN + start, size))
        gate = gu[:, pl.ds(start, size)]
        up = gu[:, pl.ds(C_UP + start, size)]
        sigma = jax.nn.sigmoid(gate)
        grad_gate = grad_hidden * up * sigma * (1.0 + gate * (1.0 - sigma))
        grad_gate = grad_gate.astype(jnp.bfloat16)
        grad_up = (grad_hidden * gate * sigma).astype(jnp.bfloat16)
        dgu[:, pl.ds(start, size)] = grad_gate
        dgu[:, pl.ds(C_UP + start, size)] = grad_up
        total = total + nt(grad_gate, weights(start, size))
        total = total + nt(grad_up, weights(C_UP + start, size))
    mine[...] = total
    one = send(mine, theirs, xs, xr, other_core())
    one.start()
    one.wait()
    back, gain_row = norm_back(mine[...] + theirs[...], mid[...], gains[3:4, :])
    gain[...] = jnp.broadcast_to(gain_row, (8, DP))
    middle = grad_in + back
    dmid[...] = middle
    low = middle.astype(jnp.bfloat16)
    da[...] = low
    loads[15].wait()
    lane = lax.broadcasted_iota(jnp.int32, (R, QS), 1)
    datt[...] = jnp.where(lane < 64, 0.0, nn(low, weights(CM, QS))).astype(jnp.bfloat16)


def mlp_back(layer, dout, gu, mid, gains, wa, wm):
    return pl.pallas_call(
        functools.partial(mlp_back_kernel, layer),
        out_shape=(
            shape((R, 2 * FFH), jnp.bfloat16),
            shape((R, DP), jnp.float32),
            shape((R, DP), jnp.bfloat16),
            shape((R, QS), jnp.bfloat16),
            shape((8, DP), jnp.float32),
        ),
        in_specs=[VMEM] * 4 + [ANY] * 2,
        out_specs=(VMEM,) * 5,
        scratch_shapes=[
            pltpu.VMEM((64, 16, CM + QS), jnp.bfloat16),
            pltpu.VMEM((R, DP), jnp.float32),
            pltpu.VMEM((R, DP), jnp.float32),
            DMA((16,)),
            DMA,
            DMA,
        ],
        compiler_params=params(5 + layer),
        name="mlp_back",
    )(dout, gu, mid, gains, wa, wm)


def project_back_kernel(
    layer, dqk, dv, x, dmid, gains, cosine, sine, w, dx, low, vlow, gain, bias,
    wbuf, mine, theirs, wsem, xs, xr,
):
    load = pltpu.make_async_copy(w.at[layer], wbuf, wsem)
    load.start()
    meet(position(), core=True, chips=False)
    turned = turn(dqk[...], tiled(cosine[...]), -tiled(sine[...])).astype(jnp.bfloat16)
    low[...] = turned
    values = dv[...].astype(jnp.bfloat16)
    vlow[...] = values
    bias[:, :QS] = jnp.broadcast_to(
        jnp.sum(turned.astype(jnp.float32), axis=0, keepdims=True), (8, QS)
    )
    bias[:, QS:] = jnp.broadcast_to(
        jnp.sum(values.astype(jnp.float32), axis=0, keepdims=True), (8, QS)
    )
    load.wait()
    mine[...] = nt(turned, wbuf[:, :, :QS].reshape(DP, QS)) + nt(
        values, wbuf[:, :, QS:].reshape(DP, QS)
    )
    one = send(mine, theirs, xs, xr, other_core())
    one.start()
    one.wait()
    back, gain_row = norm_back(
        mine[...] + theirs[...], x[...].astype(jnp.float32), gains[2:3, :]
    )
    gain[...] = jnp.broadcast_to(gain_row, (8, DP))
    dx[...] = (dmid[...] + back).astype(jnp.bfloat16)


def project_back(layer, dqk, dv, x, dmid, gains, cosine, sine, w):
    return pl.pallas_call(
        functools.partial(project_back_kernel, layer),
        out_shape=(
            shape((R, DP), jnp.bfloat16),
            shape((R, QS), jnp.bfloat16),
            shape((R, QS), jnp.bfloat16),
            shape((8, DP), jnp.float32),
            shape((8, 2 * QS), jnp.float32),
        ),
        in_specs=[VMEM] * 7 + [ANY],
        out_specs=(VMEM,) * 5,
        scratch_shapes=[
            pltpu.VMEM((64, 16, 2 * QS), jnp.bfloat16),
            pltpu.VMEM((R, DP), jnp.float32),
            pltpu.VMEM((R, DP), jnp.float32),
            DMA,
            DMA,
            DMA,
        ],
        compiler_params=params(7 + layer),
        name="project_back",
    )(dqk, dv, x, dmid, gains, cosine, sine, w)


def weight_grads_kernel(
    sums, n2, dgu, dm, hid, n1, dqk, dv, da, att, small, out, small_out,
    g, h0, h1, h2, w0, w1, w2, sbuf, ss, rs, as_, ar,
):
    place = position()
    meet(place, far=sums)

    def product(start, size, pairs):
        for first in range(0, size, 512):
            wide = min(512, size - first)
            total = sum(
                tn(left[...], right[:, first : first + wide]) for left, right in pairs
            )
            g[:, :, :, :, pl.ds(start + first, wide)] = total.astype(jnp.bfloat16).reshape(
                4, 4, 4, 16, wide
            )

    product(0, 2 * FFH, [(n2, dgu)])
    product(C_DOWN, FFH, [(dm, hid)])
    product(C_QK, QS, [(n1, dqk)])
    product(C_VO, QS, [(n1, dv), (da, att)])

    def spot(j, part):
        size = THIRDS[j][1]
        if part is None:
            return pl.ds(0, size)
        half = size // 256 * 128
        return pl.ds(0, half) if part == 0 else pl.ds(0, size - half)

    halves = [
        lambda j, k, ref=ref: ref.at[(j, k) + (slice(None),) * (ref.ndim - 3) + (spot(j, k),)]
        for ref in (h0, h1, h2)
    ]
    wholes = [
        lambda j, k, part, ref=ref: ref.at[
            (j, k) + (slice(None),) * (ref.ndim - 3) + (spot(j, None),)
        ]
        for ref in (w0, w1, w2)
    ]

    def final(j, mine, left, right):
        out[:, pl.ds(*THIRDS[j])] = (
            mine[...].astype(jnp.float32)
            + left[...].astype(jnp.float32)
            + right[...].astype(jnp.float32)
        )

    stages = scatter_stages(weight_view(g), halves, wholes, place, ss, rs, None, final)
    if sums:
        sbuf[0] = small[...]
        for phase, axis in enumerate("xyz"):
            copies = [
                send(
                    sbuf.at[4 * phase],
                    sbuf.at[4 * phase + k],
                    as_.at[phase, k - 1],
                    ar.at[phase, k - 1],
                    chip_id(moved(place, axis, distance)),
                )
                for k, distance in ((1, 1), (2, -1), (3, 2))
            ]
            for one in copies:
                one.start()
            stages[phase]()
            for one in copies:
                one.wait()
            total = (
                sbuf[4 * phase] + sbuf[4 * phase + 1] + sbuf[4 * phase + 2] + sbuf[4 * phase + 3]
            )
            if phase < 2:
                sbuf[4 * phase + 4] = total
            else:
                small_out[...] = total
        stages = stages[3:]
    else:
        small_out[...] = small[...]
    for stage in stages:
        stage()


def weight_grads(sums, n2, dgu, dm, hid, n1, dqk, dv, da, att, small):
    kind = jnp.bfloat16
    wide = THIRDS[0][1]
    half = THIRDS[0][1] // 2
    return pl.pallas_call(
        functools.partial(weight_grads_kernel, sums),
        out_shape=(shape((16, C), jnp.float32), shape((8, DP), jnp.float32)),
        in_specs=[VMEM] * 10,
        out_specs=(VMEM, VMEM),
        scratch_shapes=[
            pltpu.VMEM((4, 4, 4, 16, C), kind),
            pltpu.VMEM((3, 2, 4, 4, 16, half), kind),
            pltpu.VMEM((3, 2, 4, 16, half), kind),
            pltpu.VMEM((3, 2, 16, half), kind),
            pltpu.VMEM((3, 2, 4, 4, 16, wide), kind),
            pltpu.VMEM((3, 2, 4, 16, wide), kind),
            pltpu.VMEM((3, 2, 16, wide), kind),
            pltpu.VMEM((12, 8, DP), jnp.float32),
            DMA((3, 3, 4)),
            DMA((3, 3, 4)),
            DMA((3, 3)),
            DMA((3, 3)),
        ],
        compiler_params=params(9 + int(sums), vmem=60),
        name="weight_grads",
    )(n2, dgu, dm, hid, n1, dqk, dv, da, att, small)


def shards(
    ends,
    segment_ids,
    valid_blocks,
    qkv_weight,
    qkv_bias,
    out_weight,
    gate_up_weight,
    down_weight,
    norm_gains,
):
    core = lax.axis_index("section")
    chip = lax.axis_index("dp")
    ff = 2 * FFH

    feature = jnp.arange(D, dtype=jnp.int32)
    spread = (
        (feature // 14 * 16 + feature % 14)[:, None] == jnp.arange(DP, dtype=jnp.int32)[None, :]
    ).astype(jnp.bfloat16)

    def widen(rows):
        return nn(rows, spread).astype(jnp.bfloat16)

    def feed_half(index):
        pieces = (
            lax.dynamic_slice_in_dim(gate_up_weight[0], index * FFH, FFH, 1),
            lax.dynamic_slice_in_dim(gate_up_weight[0], ff + index * FFH, FFH, 1),
            lax.dynamic_slice_in_dim(down_weight[0], index * FFH, FFH, 1),
        )
        return jnp.pad(jnp.concatenate(pieces, axis=1), ((0, 2), (0, 0)))

    def heads_half(index):
        pieces = (
            lax.dynamic_slice_in_dim(qkv_weight[0], D + index * 64, 64, 1),
            lax.dynamic_slice_in_dim(qkv_weight[0], index * 448, 448, 1),
            lax.dynamic_slice_in_dim(qkv_weight[0], D + 128 + index * 64, 64, 1),
            lax.dynamic_slice_in_dim(out_weight[0], index * 448, 448, 1),
        )
        return jnp.pad(jnp.concatenate(pieces, axis=1), ((0, 2), (0, 0)))

    def bias_half(index):
        row = qkv_bias[0]
        pieces = (
            row[D + index * 64 : D + index * 64 + 64],
            row[index * 448 : index * 448 + 448],
            row[D + 128 + index * 64 : D + 128 + index * 64 + 64],
            jnp.zeros((448,), row.dtype),
        )
        return jnp.concatenate(pieces)[None]

    small_in = jnp.concatenate([bias_half(0), bias_half(1), widen(norm_gains[0])], axis=0)
    small_in = jnp.pad(small_in, ((0, 12), (0, 0)))

    places = chip * T + jnp.arange(T, dtype=jnp.int32)
    frequency = THETA ** (-jnp.arange(32, dtype=jnp.float32) * 2.0 / 64)
    angles = places.astype(jnp.float32)[:, None] * frequency[None, :]
    cosine = jnp.tile(jnp.cos(angles), (1, 4))
    sine = jnp.sin(angles)
    sine = jnp.tile(jnp.concatenate([-sine, sine], axis=1), (1, 2))

    own_ids = lax.dynamic_slice_in_dim(segment_ids, chip * T, T, 1)
    starts = jnp.sum(
        (segment_ids[:, None, :] < own_ids[:, :, None]).astype(jnp.int32), axis=2
    )
    lengths = jnp.sum(valid_blocks, axis=1) * 128
    finish = jnp.minimum(places[None, :] + 1, lengths[:, None])
    bounds = jnp.stack([starts, finish, jnp.broadcast_to(places[None], (MB, T))], axis=1)
    bounds = jnp.pad(jnp.tile(bounds, (1, 1, 2)), ((0, 0), (0, 5), (0, 0)))
    last = (chip * T + T + KB - 1) // KB
    blocks = jnp.stack([starts[:, 0] // KB, jnp.full((MB,), last, jnp.int32)], axis=1)

    (
        wa, wm, kv_all, gu_all, ends_all, gains_all, n1_all, qt_all, mixed_all, lse_all, att_all,
        mid_all, n2_all, hid_all, x_all, sq_all,
    ) = forward(
        heads_half(core),
        heads_half(1 - core),
        feed_half(core),
        feed_half(1 - core),
        widen(ends[0].reshape(R, D)),
        small_in,
        cosine,
        sine,
        bounds,
    )
    wa = wa.reshape(2, 64, 16, CA)
    wm = wm.reshape(2, 64, 16, CM)
    kv_all = kv_all.reshape(2, 64, MB, T, 128)
    final_out = x_all[1]
    dout = ends_all[1]

    def columns_of(rows):
        turned = rows.reshape(MB, T, 8, 64).transpose(0, 3, 2, 1)
        return turned.at[:, :, 0].set(0).reshape(MB, 64, QS)

    def rows_of(columns):
        return columns.reshape(MB, 64, 8, T).transpose(0, 3, 2, 1).reshape(R, 8, 64)

    grads = [None, None]
    smalls = [None, None]
    for layer in (1, 0):
        gains, n1, kv, qt, mixed, lse, attended, mid, n2, gu, hid, sq = (
            member[layer]
            for member in (
                gains_all, n1_all, kv_all, qt_all, mixed_all, lse_all, att_all, mid_all, n2_all,
                gu_all, hid_all, sq_all,
            )
        )
        x = x_all[0] if layer == 1 else ends_all[0]
        dgu, dmid, da, datt, gain_two = mlp_back(layer, dout, gu, mid, gains, wa, wm)
        dot_ = jnp.pad(columns_of(datt), ((0, 0), (64, 0), (0, 0)))
        dqt, terms = attend_back(blocks, qt, dot_, kv, bounds, mixed, lse)
        own = scatter_tokens(terms.reshape(4, 4, 4, MB, T, 128)).reshape(R, 128)
        dqk = rows_of(dqt).at[:, 0].set(own[:, :64]).reshape(R, QS)
        dv = jnp.pad(own[:, 64:], ((0, 0), (0, QS - 64)))
        dx, dqk_low, dv_low, gain_one, bias_sum = project_back(
            layer, dqk, dv, x, dmid, gains, cosine, sine, wa
        )
        valid = lax.dynamic_slice_in_dim(valid_blocks, chip // 2, 1, 1).astype(jnp.float32)
        squares = jnp.where(valid > 0, sq[:MB, :3], 0.0)
        smalls[layer] = jnp.stack(
            [
                gain_one[0],
                gain_two[0],
                bias_sum[0],
                jnp.pad(squares.reshape(-1), (0, DP - 9)),
            ]
        )
        small = jnp.concatenate(smalls, axis=0) if layer == 0 else jnp.zeros((8, DP), jnp.float32)
        grads[layer], small_sum = weight_grads(
            layer == 0, n2, dgu, dout, hid, n1, dqk_low, dv_low, da, attended, small
        )
        dout = dx

    def with_bias(layer):
        return grads[layer].at[14, :QS].set(small_sum[4 * layer + 2, :QS]).at[
            14, QS : 2 * QS
        ].set(small_sum[4 * layer + 2, QS:])

    ready = [with_bias(0), with_bias(1)]
    here = jnp.where(core == 0, ready[0], ready[1])
    away = lax.ppermute(jnp.where(core == 0, ready[1], ready[0]), "section", [(0, 1), (1, 0)])
    lower = jnp.where(core == 0, here, away)
    upper = jnp.where(core == 0, away, here)
    sides = (lower, upper)

    def column(start, size):
        return [side[:14, start : start + size] for side in sides]

    grad_gu = jnp.concatenate(column(0, FFH) + column(C_UP, FFH), axis=1)
    grad_down = jnp.concatenate(column(C_DOWN, FFH), axis=1)
    grad_qkv = jnp.concatenate(
        column(C_QK + 64, 448) + column(C_QK, 64) + column(C_VO, 64), axis=1
    )
    grad_out = jnp.concatenate(column(C_VO + 64, 448), axis=1)
    bias_rows = [side[14] for side in sides]
    grad_bias = jnp.concatenate(
        [row[64:QS] for row in bias_rows]
        + [row[:64] for row in bias_rows]
        + [row[QS : QS + 64] for row in bias_rows]
    )
    own_small = lax.dynamic_slice_in_dim(small_sum, 4 * core, 4, 0)
    grad_gain = own_small[:2].reshape(2, 64, 16)[:, :, :14].reshape(2, D)
    counts = jnp.sum(valid_blocks, axis=1).astype(jnp.float32) * 128 * D
    rms = jnp.sqrt(own_small[3, :9].reshape(MB, 3) / counts[:, None])
    ends_out = jnp.where(core == 0, dout, final_out)
    boundary = nt(ends_out, spread).astype(jnp.bfloat16).reshape(1, MB, T, D)
    return (
        boundary,
        grad_qkv[None],
        grad_bias[None],
        grad_out[None],
        grad_gu[None],
        grad_down[None],
        grad_gain[None],
        rms[None],
    )


def solution(mesh):
    in_specs = (
        P("section", None, "dp", None),
        P(),
        P(),
        P("section", "dp", None),
        P("section", None),
        P("section", "dp", None),
        P("section", "dp", None),
        P("section", "dp", None),
        P("section", None, None),
    )
    out_specs = (
        P("section", None, "dp", None),
        P("section", "dp", None),
        P("section", None),
        P("section", "dp", None),
        P("section", "dp", None),
        P("section", "dp", None),
        P("section", None, None),
        P("section", None, None),
    )
    return jax.shard_map(shards, mesh=mesh, in_specs=in_specs, out_specs=out_specs, check_vma=False)
```

```python
import functools
import math

import jax
import jax.numpy as jnp
from jax import lax
from jax.experimental import pallas as pl
from jax.experimental.pallas import tpu as pltpu
from jax.sharding import PartitionSpec as P

MESH = pl.DeviceIdType.MESH
EPS = 1e-06
THETA = 1000000.0
MASKED = -1e30

MB = 3
T = 64
R = MB * T
D = 896
DP = 1024
FFH = 2432
QS = 512
C_UP, C_DOWN, C_QK, C_VO, C = FFH, 2 * FFH, 3 * FFH, 3 * FFH + QS, 3 * FFH + 2 * QS
KB = 512
SEQ = 4096
MIB = 1024 * 1024

THIRDS = ((0, 22 * 128), (22 * 128, 22 * 128), (44 * 128, 21 * 128))
ORDERS = (("z", "y", "x"), ("y", "x", "z"), ("x", "z", "y"))
CM, CA = 3 * FFH, 2 * QS
M_THIRDS = ((0, FFH), (FFH, FFH), (2 * FFH, FFH))
A_THIRDS = ((0, 384), (384, 384), (768, 256))
FF_CHUNKS = ((0, 512), (512, 512), (1024, 512), (1536, 512), (2048, 384))


def position():
    chip = lax.axis_index("dp")
    return {"x": chip // 16, "y": (chip // 4) % 4, "z": chip % 4}


def moved(place, axis, distance):
    other = dict(place)
    other[axis] = (place[axis] + distance + 4) % 4
    return other


def chip_id(place):
    return {"dp": place["x"] * 16 + place["y"] * 4 + place["z"]}


def other_core():
    return {"section": 1 - lax.axis_index("section")}


def meet(place, core=False, chips=True, far=False):
    barrier = pltpu.get_barrier_semaphore()
    count = 0
    if chips:
        for axis in "xyz":
            for distance in (1, -1, 2) if far else (1, -1):
                pl.semaphore_signal(
                    barrier,
                    inc=1,
                    device_id=chip_id(moved(place, axis, distance)),
                    device_id_type=MESH,
                )
                count += 1
    if core:
        pl.semaphore_signal(barrier, inc=1, device_id=other_core(), device_id_type=MESH)
        count += 1
    pl.semaphore_wait(barrier, count)


def send(src, dst, send_sem, recv_sem, device):
    return pltpu.make_async_remote_copy(
        src, dst, send_sem, recv_sem, device_id=device, device_id_type=MESH
    )


def cube(done, place):
    return tuple(slice(None) if axis in done else place[axis] for axis in "xyz")


def gather_stages(view, place, send_sems, recv_sems):
    pending = []

    def copy(j, phase, k, whose, part, distance):
        ref = view(cube(ORDERS[j][:phase], whose), j, part)
        return send(
            ref,
            ref,
            send_sems.at[j, phase, k],
            recv_sems.at[j, phase, k],
            chip_id(moved(place, ORDERS[j][phase], distance)),
        )

    def first(phase):
        for j in range(3):
            for k, distance in ((0, 1), (1, -1)):
                one = copy(j, phase, k, place, None, distance)
                one.start()
                pending.append(one)

    def second(phase):
        for j in range(3):
            for k, distance in ((0, 1), (1, -1)):
                whose = moved(place, ORDERS[j][phase], -distance)
                copy(j, phase, k, whose, None, distance).wait_recv()
                one = copy(j, phase, 2 + k, whose, k, distance)
                one.start()
                pending.append(one)

    def third(phase):
        for j in range(3):
            for k, distance in ((0, 1), (1, -1)):
                whose = moved(place, ORDERS[j][phase], 2)
                copy(j, phase, 2 + k, whose, k, distance).wait_recv()

    def finish():
        for one in pending:
            one.wait_send()

    stages = []
    for phase in range(3):
        stages.append(functools.partial(first, phase))
        stages.append(functools.partial(second, phase))
        stages.append(functools.partial(third, phase))
    stages.append(finish)
    return stages


def scatter_stages(view, halves, wholes, place, send_sems, recv_sems, final, begin=0):
    pending = []

    def half_copy(j, phase, k, distance):
        far = moved(place, back_axis(j, phase), 2)
        return send(
            view(back_chips(j, phase, far), j, k),
            halves[phase](j, k),
            send_sems.at[j, phase, k],
            recv_sems.at[j, phase, k],
            chip_id(moved(place, back_axis(j, phase), distance)),
        )

    def whole_copy(j, phase, k, distance):
        near = moved(place, back_axis(j, phase), distance)
        return send(
            view(back_chips(j, phase, near), j, None),
            wholes[phase](j, k),
            send_sems.at[j, phase, 2 + k],
            recv_sems.at[j, phase, 2 + k],
            chip_id(near),
        )

    def first(phase):
        for j in range(3):
            for k, distance in ((0, 1), (1, -1)):
                one = half_copy(j, phase, k, distance)
                one.start()
                pending.append(one)

    def second(phase):
        for j in range(3):
            for k, distance in ((0, 1), (1, -1)):
                half_copy(j, phase, k, distance).wait_recv()
                near = moved(place, back_axis(j, phase), distance)
                mine = view(back_chips(j, phase, near), j, k)
                add(mine, mine, halves[phase](j, k))
                one = whole_copy(j, phase, k, distance)
                one.start()
                pending.append(one)

    def third(phase):
        for j in range(3):
            for k, distance in ((0, 1), (1, -1)):
                whole_copy(j, phase, k, distance).wait_recv()
            mine = view(back_chips(j, phase, place), j, None)
            if phase < 2:
                add(mine, mine, wholes[phase](j, 0), wholes[phase](j, 1))
            else:
                final(j, mine, wholes[phase](j, 0), wholes[phase](j, 1))

    def finish():
        for one in pending:
            one.wait_send()

    stages = []
    for phase in range(begin, 3):
        stages.append(functools.partial(first, phase))
        stages.append(functools.partial(second, phase))
        stages.append(functools.partial(third, phase))
    stages.append(finish)
    return stages


def back_axis(j, phase):
    return ORDERS[j][2 - phase]


def back_chips(j, phase, whose):
    return cube(ORDERS[j][: 2 - phase], whose)


def add(dst, *terms):
    dst[...] = sum(term[...].astype(jnp.float32) for term in terms).astype(dst.dtype)


def half_of(size, part):
    half = size // 256 * 128
    return (0, half) if part == 0 else (half, size - half)


def scatter_large_stages(
    source, slab, got_half, got_whole, spare, inner_halves, inner_wholes, place,
    hs, hr, os_, or_, ws, wr, ls, ss, rs, final,
):
    pending = []
    turns = [(j, k, (1, -1)[k]) for j in range(3) for k in range(2)]

    def half_ref(j, k):
        return got_half.at[j, k, :, :, :, pl.ds(0, half_of(FFH, k)[1])]

    def whole_ref(j, k, part):
        return got_whole.at[j, k, :, :, :, pl.ds(*half_of(FFH, part))]

    def near(j, distance):
        return moved(place, back_axis(j, 0), distance)

    def half_copy(j, k, distance):
        return send(
            source(back_chips(j, 0, near(j, 2)), j, k),
            half_ref(j, k),
            hs.at[j, k],
            hr.at[j, k],
            chip_id(near(j, distance)),
        )

    def other_copy(j, k, distance):
        return send(
            source(back_chips(j, 0, near(j, distance)), j, 1 - k),
            whole_ref(j, k, 1 - k),
            os_.at[j, k],
            or_.at[j, k],
            chip_id(near(j, distance)),
        )

    def summed_copy(j, k, distance):
        return send(
            half_ref(j, k),
            whole_ref(j, k, k),
            ws.at[j, k],
            wr.at[j, k],
            chip_id(near(j, distance)),
        )

    def own_load(index):
        j, k, distance = turns[index]
        return pltpu.make_async_copy(
            source(back_chips(j, 0, near(j, distance)), j, k),
            spare.at[index % 2, :, :, :, pl.ds(0, half_of(FFH, k)[1])],
            ls.at[index],
        )

    def slab_load(j):
        return pltpu.make_async_copy(
            source(back_chips(j, 0, place), j, None), slab.at[j], ls.at[6 + j]
        )

    def first():
        for j, k, distance in turns:
            one = half_copy(j, k, distance)
            one.start()
            pending.append(one)
        for j, k, distance in turns:
            one = other_copy(j, k, distance)
            one.start()
            pending.append(one)
        for j in range(3):
            slab_load(j).start()
        own_load(0).start()
        own_load(1).start()

    def second():
        for index, (j, k, distance) in enumerate(turns):
            half_copy(j, k, distance).wait_recv()
            own_load(index).wait()
            size = half_of(FFH, k)[1]
            add(half_ref(j, k), half_ref(j, k), spare.at[index % 2, :, :, :, pl.ds(0, size)])
            one = summed_copy(j, k, distance)
            one.start()
            pending.append(one)
            if index < 4:
                own_load(index + 2).start()

    def third():
        for j in range(3):
            slab_load(j).wait()
            for k in range(2):
                distance = (1, -1)[k]
                other_copy(j, k, distance).wait_recv()
                summed_copy(j, k, distance).wait_recv()
            add(slab.at[j], slab.at[j], got_whole.at[j, 0], got_whole.at[j, 1])

    def view(chips, j, part):
        rest = tuple(index for axis, index in zip("xyz", chips) if axis != back_axis(j, 0))
        cols = slice(None) if part is None else pl.ds(*half_of(FFH, part))
        return slab.at[(j,) + rest + (slice(None), cols)]

    inner = scatter_stages(
        view, inner_halves, inner_wholes, place, ss, rs, final, begin=1
    )

    def finish():
        for one in pending:
            one.wait_send()
        inner[-1]()

    return [first, second, third] + inner[:-1] + [finish]


def weight_view(ref, thirds=THIRDS):
    def view(chips, j, part):
        start, size = thirds[j]
        if part is not None:
            half = size // 256 * 128
            start, size = (start, half) if part == 0 else (start + half, size - half)
        return ref.at[tuple(chips) + (slice(None), pl.ds(start, size))]

    return view


def token_view(ref):
    def view(chips, j, part):
        rows = slice(None) if part is None else pl.ds(part * 32, 32)
        return ref.at[tuple(chips) + (j, rows, slice(None))]

    return view


def params(collective_id=None, vmem=56):
    if collective_id is None:
        return pltpu.CompilerParams(vmem_limit_bytes=vmem * MIB)
    return pltpu.CompilerParams(
        collective_id=collective_id, has_side_effects=True, vmem_limit_bytes=vmem * MIB
    )


ANY = pl.BlockSpec(memory_space=pl.ANY)
VMEM = pl.BlockSpec(memory_space=pltpu.VMEM)
SMEM = pl.BlockSpec(memory_space=pltpu.SMEM)
DMA = pltpu.SemaphoreType.DMA


def shape(dims, dtype):
    return jax.ShapeDtypeStruct(dims, dtype)


def nn(left, right):
    return jnp.dot(left, right, preferred_element_type=jnp.float32)


def nt(left, right):
    return lax.dot_general(
        left, right, (((1,), (1,)), ((), ())), preferred_element_type=jnp.float32
    )


def tn(left, right):
    return lax.dot_general(
        left, right, (((0,), (0,)), ((), ())), preferred_element_type=jnp.float32
    )


def pair_mask(base, bounds):
    keys = base + lax.broadcasted_iota(jnp.int32, (KB, 128), 0)
    start, end, own = bounds[0:1, :], bounds[1:2, :], bounds[2:3, :]
    allowed = ((keys >= start) & (keys < end)) | (keys == own)
    bias = jnp.where(allowed, 0.0, MASKED)
    return jnp.concatenate([bias] * 4, axis=1)


def mean_of(values):
    return jnp.sum(values, axis=-1, keepdims=True) * (1.0 / D)


def turn(values, cosine, sine):
    lane = lax.broadcasted_iota(jnp.int32, values.shape, 1) % 64
    swapped = jnp.where(lane < 32, pltpu.roll(values, QS - 32, 1), pltpu.roll(values, 32, 1))
    return values * cosine + swapped * sine


def tiled(table):
    wide = jnp.concatenate([table] * 4, axis=1)
    return jnp.concatenate([wide] * MB, axis=0)


def to_columns(rows):
    turned = rows.T
    return jnp.concatenate([turned[64 * h : 64 * h + 64] for h in range(8)], axis=1)


def to_rows(columns):
    pairs = []
    for pair in range(4):
        turned = columns[:, 128 * pair : 128 * pair + 128].T
        pairs.append(jnp.concatenate([turned[:64], turned[64:]], axis=1))
    return jnp.concatenate(pairs, axis=1)


def without_first_slot(rows):
    lane = lax.broadcasted_iota(jnp.int32, rows.shape, 1)
    return jnp.where(lane < 64, 0.0, rows)


def forward_kernel(
    mat, tat, mml, tml, ends, small, cosine, sine, bounds,
    wa, wm, kv, gu, cot, gains, n1, qt, mixed, lse, att, mid, n2, hid, xs_, sq,
    ends_v, small_v, stage_a, stage_m, wat, wml, kvb, gu_v, mine, theirs,
    lsem, ssem, rsem, a_s, a_r, m_s, m_r, k_s, k_r, osem, wsem, xsem, xrsem,
):
    place = position()
    core = lax.axis_index("section")
    chip = lax.axis_index("dp")
    here = (place["x"], place["y"], place["z"])
    meet(place, core=True)

    traded = ((mat, tat, stage_a), (mml, tml, stage_m), (ends, ends, ends_v), (small, small, small_v))
    trades = []
    for index, (keep, give, dst) in enumerate(traded):
        local = pltpu.make_async_copy(keep, dst.at[core], lsem.at[index])
        out = send(give, dst.at[core], ssem.at[index], rsem.at[index], other_core())
        back = send(give, dst.at[1 - core], ssem.at[index], rsem.at[index], other_core())
        local.start()
        out.start()
        trades.append((local, out, back))

    def arrive(index):
        local, out, back = trades[index]
        local.wait()
        back.wait_recv()
        out.wait_send()

    arrive(0)
    into = [
        pltpu.make_async_copy(stage_a.at[layer], wat.at[(layer,) + here], lsem.at[4 + layer])
        for layer in range(2)
    ]
    for one in into:
        one.start()
    for one in into:
        one.wait()
    attn = [
        gather_stages(weight_view(wat.at[layer], A_THIRDS), place, a_s.at[layer], a_r.at[layer])
        for layer in range(2)
    ]
    feed = [
        gather_stages(weight_view(wml, M_THIRDS), place, m_s.at[0], m_r.at[0]),
        gather_stages(weight_view(wm.at[1], M_THIRDS), place, m_s.at[1], m_r.at[1]),
    ]
    keys = [
        gather_stages(token_view(kvb.at[layer]), place, k_s.at[layer], k_r.at[layer])
        for layer in range(2)
    ]
    attn[0][0]()
    arrive(1)
    into = [
        pltpu.make_async_copy(stage_m.at[0], wml.at[here], lsem.at[4]),
        pltpu.make_async_copy(stage_m.at[1], wm.at[(1,) + here], lsem.at[5]),
    ]
    for one in into:
        one.start()
    for one in into:
        one.wait()
    feed[0][0]()
    attn[0][1]()
    feed[0][1]()
    attn[0][2]()
    attn[0][3]()
    feed[0][2]()
    feed[0][3]()
    attn[0][4]()
    attn[0][5]()
    attn[0][6]()
    attn[0][7]()
    arrive(2)
    arrive(3)
    cot[...] = ends_v[...]
    for layer in range(2):
        gains[layer] = small_v[layer, 0:8, :].astype(jnp.float32)
    attn[0][8]()

    outs = []

    def store(src, dst, index):
        one = pltpu.make_async_copy(src, dst, osem.at[index])
        one.start()
        outs.append(one)

    def rows_of(layer):
        return ends_v[0] if layer == 0 else xs_[0]

    def project(layer):
        rows = rows_of(layer).astype(jnp.float32)
        gain = gains[layer, 2:3, :]
        bias = jnp.where(core == 0, gains[layer, 0:1, :], gains[layer, 1:2, :])
        normed = (rows * lax.rsqrt(mean_of(rows * rows) + EPS) * gain).astype(jnp.bfloat16)
        n1[layer] = normed
        weights = wat[layer].reshape(DP, CA)
        projected = nn(normed, weights[:, : QS + 128]) + bias[:, : QS + 128]
        turned = turn(projected[:, :QS], tiled(cosine[...]), tiled(sine[...]))
        own = jnp.concatenate([turned[:, :64], projected[:, QS : QS + 64]], axis=1)
        kvb[(layer,) + here] = own.astype(jnp.bfloat16).reshape(MB, T, 128)
        heads = without_first_slot(turned).astype(jnp.bfloat16).astype(jnp.float32) * 0.125
        for batch in range(MB):
            columns = to_columns(heads[batch * T : (batch + 1) * T]).astype(jnp.bfloat16)
            qt[layer, batch] = jnp.concatenate([columns, jnp.zeros_like(columns)], axis=0)

    def attend(layer, batch):
        queries = qt[layer, batch]
        limits = bounds[batch]

        def step(index, carry):
            top, total, sums = carry
            rows = kvb[layer, index // 2, pl.ds(index % 2 * 2, 2), :, batch].reshape(KB, 128)
            scores = nn(rows, queries) + pair_mask(index * KB, limits)
            new_top = jnp.maximum(top, jnp.max(scores, axis=0, keepdims=True))
            shrink = jnp.exp(top - new_top)
            probs = jnp.exp(scores - new_top)
            total = total * shrink + jnp.sum(probs, axis=0, keepdims=True)
            sums = sums * shrink + tn(rows, probs.astype(jnp.bfloat16))
            return new_top, total, sums

        top, total, sums = lax.fori_loop(
            0,
            (chip * T + T + KB - 1) // KB,
            step,
            (
                jnp.full((1, QS), MASKED, jnp.float32),
                jnp.zeros((1, QS), jnp.float32),
                jnp.zeros((128, QS), jnp.float32),
            ),
        )
        result = (sums / total)[64:, :]
        mixed[layer, batch] = result
        lse[layer, batch] = jnp.broadcast_to(top + jnp.log(total), (8, QS))
        att[layer, pl.ds(batch * T, T), :] = without_first_slot(to_rows(result)).astype(
            jnp.bfloat16
        )

    def swap(slot):
        return send(mine.at[slot], theirs.at[slot], xsem.at[slot], xrsem.at[slot], other_core())

    def branch_of(layer):
        mine[0] = nt(att[layer], wat[layer, :, :, :, :, QS:].reshape(DP, QS))
        one = swap(0)
        one.start()
        one.wait()
        branch = mine[0] + theirs[0]
        middle = rows_of(layer).astype(jnp.float32) + branch
        mid[layer] = middle
        scale = lax.rsqrt(mean_of(middle * middle) + EPS)
        n2[layer] = (middle * scale * gains[layer, 3:4, :]).astype(jnp.bfloat16)
        return branch

    def feed_forward(layer, branch, hooks):
        normed = n2[layer]
        sums = jnp.zeros((R, DP), jnp.float32)
        for index, (start, size) in enumerate(FF_CHUNKS):
            hooks[index]()

            def weights(first, start=start, size=size):
                return wml[:, :, :, :, pl.ds(first + start, size)].reshape(DP, size)

            gate = nn(normed, weights(0))
            up = nn(normed, weights(FFH))
            gu_v[:, pl.ds(start, size)] = gate
            gu_v[:, pl.ds(FFH + start, size)] = up
            hidden = (gate * jax.nn.sigmoid(gate) * up).astype(jnp.bfloat16)
            hid[layer, :, pl.ds(start, size)] = hidden
            sums = sums + nt(hidden, weights(2 * FFH))
        store(gu_v, gu.at[layer], 4 + layer)
        mine[1] = sums
        one = swap(1)
        one.start()
        one.wait()
        result = mine[1] + theirs[1]
        middle = mid[layer]
        xs_[layer] = (middle + result).astype(jnp.bfloat16)
        rows = rows_of(layer).astype(jnp.float32)
        row = lax.broadcasted_iota(jnp.int32, (8, 128), 0)
        lane = lax.broadcasted_iota(jnp.int32, (8, 128), 1)
        table = jnp.zeros((8, 128), jnp.float32)
        for kind, values in enumerate((rows, branch, result)):
            squares = jnp.sum(values * values, axis=1, keepdims=True)
            for batch in range(MB):
                one = jnp.sum(squares[batch * T : (batch + 1) * T], axis=0, keepdims=True)
                table = jnp.where((row == batch) & (lane == kind), one, table)
        sq[layer] = table

    def nothing():
        pass

    project(0)
    keys[0][0]()
    attn[1][0]()
    feed[0][4]()
    keys[0][1]()
    attn[1][1]()
    keys[0][2]()
    keys[0][3]()
    attn[1][2]()
    attn[1][3]()
    feed[0][5]()
    keys[0][4]()
    attn[1][4]()
    keys[0][5]()
    keys[0][6]()
    attn[1][5]()
    attn[1][6]()
    keys[0][7]()
    feed[0][6]()
    feed[1][0]()
    keys[0][8]()
    store(kvb.at[0], kv.at[0], 0)
    attend(0, 0)
    feed[1][1]()
    attn[1][7]()
    attend(0, 1)
    feed[0][7]()
    feed[1][2]()
    feed[1][3]()
    attend(0, 2)
    feed[1][4]()
    attn[1][8]()
    store(wat, wa, 1)
    branch = branch_of(0)
    feed[1][5]()
    feed[0][8]()
    feed[1][6]()
    store(wml, wm.at[0], 2)
    feed_forward(0, branch, [nothing] * 5)
    project(1)
    for stage in keys[1][:8]:
        stage()
    feed[1][7]()
    keys[1][8]()
    store(kvb.at[1], kv.at[1], 3)
    for batch in range(MB):
        attend(1, batch)
    branch = branch_of(1)
    feed[1][8]()
    feed[0][9]()
    outs[2].wait()
    outs[3].wait()
    loads = []
    for index, (start, size) in enumerate(FF_CHUNKS):
        for part in range(3):
            cols = pl.ds(part * FFH + start, size)
            loads.append(
                pltpu.make_async_copy(
                    wm.at[1, :, :, :, :, cols],
                    wml.at[:, :, :, :, cols],
                    wsem.at[3 * index + part],
                )
            )
    for one in loads:
        one.start()

    def ready(index):
        for one in loads[3 * index : 3 * index + 3]:
            one.wait()

    feed_forward(1, branch, [functools.partial(ready, index) for index in range(5)])
    for index, one in enumerate(outs):
        if index not in (2, 3):
            one.wait()
    for stages in attn + feed[1:] + keys:
        stages[9]()


def forward(mat, tat, mml, tml, ends, small, cosine, sine, bounds):
    low, full = jnp.bfloat16, jnp.float32
    return pl.pallas_call(
        forward_kernel,
        out_shape=(
            shape((2, 4, 4, 4, 16, CA), low),
            shape((2, 4, 4, 4, 16, CM), low),
            shape((2, 4, 4, 4, MB, T, 128), low),
            shape((2, R, 2 * FFH), full),
            shape((2, R, DP), low),
            shape((2, 8, DP), full),
            shape((2, R, DP), low),
            shape((2, MB, 128, QS), low),
            shape((2, MB, 64, QS), full),
            shape((2, MB, 8, QS), full),
            shape((2, R, QS), low),
            shape((2, R, DP), full),
            shape((2, R, DP), low),
            shape((2, R, FFH), low),
            shape((2, R, DP), low),
            shape((2, 8, 128), full),
        ),
        in_specs=[ANY] * 6 + [VMEM] * 3,
        out_specs=(ANY,) * 4 + (VMEM,) * 12,
        scratch_shapes=[
            pltpu.VMEM((2, R, DP), low),
            pltpu.VMEM((2, 16, DP), low),
            pltpu.VMEM((2, 16, CA), low),
            pltpu.VMEM((2, 16, CM), low),
            pltpu.VMEM((2, 4, 4, 4, 16, CA), low),
            pltpu.VMEM((4, 4, 4, 16, CM), low),
            pltpu.VMEM((2, 4, 4, 4, MB, T, 128), low),
            pltpu.VMEM((R, 2 * FFH), full),
            pltpu.VMEM((2, R, DP), full),
            pltpu.VMEM((2, R, DP), full),
            DMA((6,)),
            DMA((4,)),
            DMA((4,)),
            DMA((2, 3, 3, 4)),
            DMA((2, 3, 3, 4)),
            DMA((2, 3, 3, 4)),
            DMA((2, 3, 3, 4)),
            DMA((2, 3, 3, 4)),
            DMA((2, 3, 3, 4)),
            DMA((6,)),
            DMA((15,)),
            DMA((2,)),
            DMA((2,)),
        ],
        compiler_params=params(0, vmem=60),
        name="forward",
    )(mat, tat, mml, tml, ends, small, cosine, sine, bounds)


def norm_back(grad, rows, gain):
    scale = lax.rsqrt(mean_of(rows * rows) + EPS)
    scaled = grad * gain
    back = scale * scaled - rows * (scale * scale * scale) * mean_of(scaled * rows)
    return back, jnp.sum(grad * rows * scale, axis=0, keepdims=True)


SLOT = 256
FF_SLOTS = tuple((start, min(SLOT, FFH - start)) for start in range(0, FFH, SLOT))
A_SLOTS = ((0, 3), (3, 3), (6, 2))


def slot_view(pool):
    def view(chips, j, part):
        lanes = slice(None) if part is None else pl.ds(part * 128, 128)
        return pool.at[(pl.ds(*A_SLOTS[j]),) + tuple(chips) + (slice(None), lanes)]

    return view


def backward_kernel(
    wa, wm, kv, gu, cot, x0, x1, gains, n1, qt, mixed, lse, att, mid, n2, squares, cosine, sine,
    bounds,
    grads, dx, kept, other, small_out,
    pool, gbuf, n2t, dmt, wat, mine, theirs, dout, dmid, da, dot_, dqk, low, vlow, kvb, own,
    kh0, kh1, kh2, kw0, kw1, kw2, slab, got_half, got_whole, spare, mh1, mh2, mw1, mw2,
    ah0, ah1, ah2, aw0, aw1, aw2, outv, sbuf,
    lsem, psem, gsem, usem, xsem, xrsem, ks, kr, hs, hr, os_, or_, ws, wr, ls, ms, mr, as_, ar,
    bs, br, fs, fr, credit,
):
    place = position()
    core = lax.axis_index("section")
    chip = lax.axis_index("dp")
    meet(place, core=True, far=True)
    steps = (chip * T + T + KB - 1) // KB

    def heads_load(layer):
        return pltpu.make_async_copy(wa.at[layer], wat, lsem.at[2 * layer])

    def keys_load(layer):
        return pltpu.make_async_copy(kv.at[layer], kvb, lsem.at[2 * layer + 1])

    heads_load(1).start()
    keys_load(1).start()
    dout[...] = cot[...].astype(jnp.float32)
    small = [[None] * 4, [None] * 4]
    stored = {}

    def swap(slot):
        return send(mine.at[slot], theirs.at[slot], xsem.at[slot], xrsem.at[slot], other_core())

    def back_feed(layer, hooks):
        def loads(index):
            start, size = FF_SLOTS[index]
            slot = index % 2
            copies = []
            for part in range(3):
                copies.append(
                    pltpu.make_async_copy(
                        wm.at[layer, :, :, :, :, pl.ds(part * FFH + start, size)],
                        pool.at[3 * slot + part, :, :, :, :, pl.ds(0, size)],
                        psem.at[slot, part],
                    )
                )
            for part in range(2):
                copies.append(
                    pltpu.make_async_copy(
                        gu.at[layer, :, pl.ds(part * FFH + start, size)],
                        gbuf.at[slot, part, :, pl.ds(0, size)],
                        usem.at[slot, part],
                    )
                )
            return copies

        for index in range(2):
            for one in loads(index):
                one.start()
        grad_in = dout[...]
        grad_low = grad_in.astype(jnp.bfloat16)
        n2t[...] = n2[layer].astype(jnp.float32).T.astype(jnp.bfloat16)
        dmt[...] = grad_low.astype(jnp.float32).T.astype(jnp.bfloat16)
        mine[0] = jnp.zeros((R, DP), jnp.float32)
        for index, (start, size) in enumerate(FF_SLOTS):
            slot = index % 2
            hooks.get(index, lambda: None)()
            for one in loads(index):
                one.wait()

            def weights(part, slot=slot, size=size):
                return pool[3 * slot + part, :, :, :, :, :size].reshape(DP, size)

            grad_hidden = nn(grad_low, weights(2))
            gate = gbuf[slot, 0, :, :size]
            up = gbuf[slot, 1, :, :size]
            sigma = jax.nn.sigmoid(gate)
            hidden = (gate * sigma * up).astype(jnp.bfloat16)
            grad_gate = grad_hidden * up * sigma * (1.0 + gate * (1.0 - sigma))
            grad_gate = grad_gate.astype(jnp.bfloat16)
            grad_up = (grad_hidden * gate * sigma).astype(jnp.bfloat16)
            mine[0] += nt(grad_gate, weights(0)) + nt(grad_up, weights(1))
            if index + 2 < len(FF_SLOTS):
                for one in loads(index + 2):
                    one.start()
            products = ((n2t, grad_gate), (n2t, grad_up), (dmt, hidden))
            for part, (left, right) in enumerate(products):
                held = 6 + 3 * slot + part
                if held in stored:
                    stored.pop(held).wait()
                pool[held, :, :, :, :, :size] = (
                    nn(left[...], right).astype(jnp.bfloat16).reshape(4, 4, 4, 16, size)
                )
                stored[held] = pltpu.make_async_copy(
                    pool.at[held, :, :, :, :, pl.ds(0, size)],
                    grads.at[layer, :, :, :, :, pl.ds(part * FFH + start, size)],
                    gsem.at[slot, part],
                )
                stored[held].start()
        one = swap(0)
        one.start()
        one.wait()
        back, gain_row = norm_back(mine[0] + theirs[0], mid[layer], gains[layer, 3:4, :])
        small[layer][1] = gain_row
        middle = grad_in + back
        dmid[...] = middle
        middle_low = middle.astype(jnp.bfloat16)
        da[layer] = middle_low
        heads_load(layer).wait()
        turned = nn(middle_low, wat[:, :, :, :, QS:].reshape(DP, QS))
        turned = without_first_slot(turned.astype(jnp.bfloat16).astype(jnp.float32))
        for batch in range(MB):
            columns = to_columns(turned[batch * T : (batch + 1) * T]).astype(jnp.bfloat16)
            dot_[batch] = jnp.concatenate([jnp.zeros_like(columns), columns], axis=0)
        for held in list(stored):
            stored.pop(held).wait()

    def back_attend(layer, batch):
        if batch == 0:
            keys_load(layer).wait()
        queries, slopes_out = qt[layer, batch], dot_[batch]
        limits = bounds[batch]
        log_total = lse[layer, batch, 0:1, :]
        inner = jnp.sum(
            mixed[layer, batch] * slopes_out[64:, :].astype(jnp.float32), axis=0, keepdims=True
        )

        def step(index, sums):
            spot = (index // 2, pl.ds(index % 2 * 2, 2), slice(None), batch)
            rows = kvb[spot].reshape(KB, 128)
            scores = nn(rows, queries) + pair_mask(index * KB, limits)
            probs = jnp.exp(scores - log_total)
            slopes = (probs * (nn(rows, slopes_out) - inner)).astype(jnp.bfloat16)
            both = nt(slopes, queries) + nt(probs.astype(jnp.bfloat16), slopes_out)
            kvb[spot] = both.astype(jnp.bfloat16).reshape(2, 4, T, 128)
            return sums + tn(rows, slopes)

        sums = lax.fori_loop(0, steps, step, jnp.zeros((128, QS), jnp.float32))

        def clear(index, nothing):
            kvb[index // 2, pl.ds(index % 2 * 2, 2), :, batch] = jnp.zeros(
                (2, 4, T, 128), jnp.bfloat16
            )
            return nothing

        lax.fori_loop(steps, SEQ // KB, clear, 0)
        dqk[pl.ds(batch * T, T), :] = to_rows(sums[:64, :] * 0.125)

    def back_project(layer):
        key_grads = own[...].reshape(R, 128)
        whole = jnp.concatenate([key_grads[:, :64], dqk[:, 64:]], axis=1)
        turned = turn(whole, tiled(cosine[...]), -tiled(sine[...])).astype(jnp.bfloat16)
        values = jnp.concatenate(
            [key_grads[:, 64:], jnp.zeros((R, QS - 64), jnp.float32)], axis=1
        ).astype(jnp.bfloat16)
        low[layer] = turned
        vlow[layer] = values
        small[layer][2] = jnp.concatenate(
            [
                jnp.sum(turned.astype(jnp.float32), axis=0, keepdims=True),
                jnp.sum(values.astype(jnp.float32), axis=0, keepdims=True),
            ],
            axis=1,
        )
        mine[1] = nt(turned, wat[:, :, :, :, :QS].reshape(DP, QS)) + nt(
            values, wat[:, :, :, :, QS:].reshape(DP, QS)
        )
        one = swap(1)
        one.start()
        one.wait()
        rows = (x0 if layer == 0 else x1)[...].astype(jnp.float32)
        back, gain_row = norm_back(mine[1] + theirs[1], rows, gains[layer, 2:3, :])
        small[layer][0] = gain_row
        small[layer][3] = squares[layer : layer + 1, :]
        result = (dmid[...] + back).astype(jnp.bfloat16)
        if layer == 0:
            dx[...] = result
        else:
            dout[...] = result.astype(jnp.float32)

    def heads_products(layer):
        first = tn(n1[layer], low[layer])
        second = tn(n1[layer], vlow[layer]) + tn(da[layer], att[layer])
        for side, product in enumerate((first, second)):
            for part in range(2):
                pool[4 * layer + 2 * side + part] = (
                    product[:, part * SLOT : (part + 1) * SLOT]
                    .astype(jnp.bfloat16)
                    .reshape(4, 4, 4, 16, SLOT)
                )

    def key_final(j, mine_, left, right):
        own[j] = (
            mine_[...].astype(jnp.float32)
            + left[...].astype(jnp.float32)
            + right[...].astype(jnp.float32)
        )

    key_halves = [lambda j, k, ref=ref: ref.at[j, k] for ref in (kh0, kh1, kh2)]
    key_wholes = [lambda j, k, ref=ref: ref.at[j, k] for ref in (kw0, kw1, kw2)]
    keys = [
        scatter_stages(
            token_view(kvb), key_halves, key_wholes, place, ks.at[layer], kr.at[layer], key_final
        )
        for layer in range(2)
    ]

    def feed_final(layer):
        def final(j, mine_, left, right):
            outv[layer, :, pl.ds(j * FFH, FFH)] = (
                mine_[...].astype(jnp.float32)
                + left[...].astype(jnp.float32)
                + right[...].astype(jnp.float32)
            )

        return final

    def lanes(ref, size):
        return lambda j, k: ref.at[
            (j, k) + (slice(None),) * (len(ref.shape) - 3) + (pl.ds(0, size(k)),)
        ]

    inner_halves = [None] + [lanes(ref, lambda k: half_of(FFH, k)[1]) for ref in (mh1, mh2)]
    inner_wholes = [None] + [lanes(ref, lambda k: FFH) for ref in (mw1, mw2)]
    feed = [
        scatter_large_stages(
            weight_view(grads.at[layer], M_THIRDS), slab, got_half, got_whole, spare,
            inner_halves, inner_wholes, place, hs.at[layer], hr.at[layer], os_.at[layer],
            or_.at[layer], ws.at[layer], wr.at[layer], ls.at[layer], ms.at[layer], mr.at[layer],
            feed_final(layer),
        )
        for layer in range(2)
    ]

    def slots(ref):
        return lambda j, k: ref.at[j, k, pl.ds(0, A_SLOTS[j][1])]

    def heads_final(j, mine_, left, right):
        begin, count = A_SLOTS[j]
        for index in range(count):
            layer, spot = divmod(begin + index, 4)
            outv[layer, :, pl.ds(CM + spot * SLOT, SLOT)] = (
                mine_[index].astype(jnp.float32)
                + left[index].astype(jnp.float32)
                + right[index].astype(jnp.float32)
            )

    heads = scatter_stages(
        slot_view(pool), [slots(ref) for ref in (ah0, ah1, ah2)],
        [slots(ref) for ref in (aw0, aw1, aw2)], place, as_, ar, heads_final,
    )

    def total_small(phase, axis):
        copies = [
            send(
                sbuf.at[4 * phase],
                sbuf.at[4 * phase + k],
                bs.at[phase, k - 1],
                br.at[phase, k - 1],
                chip_id(moved(place, axis, distance)),
            )
            for k, distance in ((1, 1), (2, -1), (3, 2))
        ]

        def begin():
            for one in copies:
                one.start()

        def end():
            for one in copies:
                one.wait()
            total = (
                sbuf[4 * phase] + sbuf[4 * phase + 1] + sbuf[4 * phase + 2] + sbuf[4 * phase + 3]
            )
            if phase < 2:
                sbuf[4 * phase + 4] = total
            else:
                small_out[...] = total

        return begin, end

    back_feed(1, {})
    feed[1][0]()
    for batch in range(MB):
        back_attend(1, batch)
    for stage in keys[1][:8]:
        stage()
    feed[1][1]()
    keys[1][8]()
    keys[1][9]()
    keys_load(0).start()
    back_project(1)
    heads_load(0).start()
    back_feed(
        0,
        {
            3: lambda: (feed[1][2](), feed[1][3]()),
            5: lambda: feed[1][4](),
            7: lambda: (feed[1][5](), feed[1][6]()),
            9: lambda: feed[1][7](),
        },
    )
    feed[1][8]()
    feed[1][9]()
    for axis in "xyz":
        for distance in (1, -1):
            pl.semaphore_signal(
                credit, inc=1, device_id=chip_id(moved(place, axis, distance)), device_id_type=MESH
            )
    pl.semaphore_wait(credit, 6)
    feed[0][0]()
    for batch in range(MB):
        back_attend(0, batch)
    heads_products(1)
    for stage in keys[0][:8]:
        stage()
    feed[0][1]()
    keys[0][8]()
    keys[0][9]()
    back_project(0)
    heads_products(0)
    sbuf[0] = jnp.concatenate(small[0] + small[1], axis=0)
    sums = [total_small(phase, axis) for phase, axis in enumerate("xyz")]
    sums[0][0]()
    heads[0]()
    feed[0][2]()
    feed[0][3]()
    sums[0][1]()
    sums[1][0]()
    heads[1]()
    feed[0][4]()
    heads[2]()
    heads[3]()
    sums[1][1]()
    sums[2][0]()
    feed[0][5]()
    feed[0][6]()
    heads[4]()
    heads[5]()
    heads[6]()
    sums[2][1]()
    feed[0][7]()
    heads[7]()
    feed[0][8]()
    heads[8]()
    for layer in range(2):
        outv[layer, 14:15, pl.ds(CM, CA)] = small_out[4 * layer + 2 : 4 * layer + 3, :]
    trade = send(outv.at[1 - core], other, fs, fr, other_core())
    trade.start()
    kept[...] = outv[core]
    feed[0][9]()
    heads[9]()
    trade.wait()


def backward(*arrays):
    low, full = jnp.bfloat16, jnp.float32
    half = FFH - FFH // 256 * 128

    def ring(last, phase, kind=low):
        return pltpu.VMEM((3, 2) + (4,) * (2 - phase) + last, kind)

    return pl.pallas_call(
        backward_kernel,
        out_shape=(
            shape((2, 4, 4, 4, 16, CM), low),
            shape((R, DP), low),
            shape((16, C), full),
            shape((16, C), full),
            shape((8, DP), full),
        ),
        in_specs=[ANY] * 4 + [VMEM] * 15,
        out_specs=(ANY,) + (VMEM,) * 4,
        scratch_shapes=[
            pltpu.VMEM((12, 4, 4, 4, 16, SLOT), low),
            pltpu.VMEM((2, 2, R, SLOT), full),
            pltpu.VMEM((DP, R), low),
            pltpu.VMEM((DP, R), low),
            pltpu.VMEM((4, 4, 4, 16, CA), low),
            pltpu.VMEM((2, R, DP), full),
            pltpu.VMEM((2, R, DP), full),
            pltpu.VMEM((R, DP), full),
            pltpu.VMEM((R, DP), full),
            pltpu.VMEM((2, R, DP), low),
            pltpu.VMEM((MB, 128, QS), low),
            pltpu.VMEM((R, QS), full),
            pltpu.VMEM((2, R, QS), low),
            pltpu.VMEM((2, R, QS), low),
            pltpu.VMEM((4, 4, 4, MB, T, 128), low),
            pltpu.VMEM((MB, T, 128), full),
        ]
        + [ring((T // 2, 128), phase) for phase in range(3)]
        + [ring((T, 128), phase) for phase in range(3)]
        + [
            pltpu.VMEM((3, 4, 4, 16, FFH), low),
            pltpu.VMEM((3, 2, 4, 4, 16, half), low),
            pltpu.VMEM((3, 2, 4, 4, 16, FFH), low),
            pltpu.VMEM((2, 4, 4, 16, half), low),
        ]
        + [ring((16, half), phase) for phase in (1, 2)]
        + [ring((16, FFH), phase) for phase in (1, 2)]
        + [
            pltpu.VMEM((3, 2, 3) + (4,) * (2 - phase) + (16, wide), low)
            for wide in (128, SLOT)
            for phase in range(3)
        ]
        + [
            pltpu.VMEM((2, 16, C), full),
            pltpu.VMEM((12, 8, DP), full),
            DMA((4,)),
            DMA((2, 3)),
            DMA((2, 3)),
            DMA((2, 2)),
            DMA((2,)),
            DMA((2,)),
            DMA((2, 3, 3, 4)),
            DMA((2, 3, 3, 4)),
            DMA((2, 3, 2)),
            DMA((2, 3, 2)),
            DMA((2, 3, 2)),
            DMA((2, 3, 2)),
            DMA((2, 3, 2)),
            DMA((2, 3, 2)),
            DMA((2, 9)),
            DMA((2, 3, 3, 4)),
            DMA((2, 3, 3, 4)),
            DMA((3, 3, 4)),
            DMA((3, 3, 4)),
            DMA((3, 3)),
            DMA((3, 3)),
            DMA,
            DMA,
            pltpu.SemaphoreType.REGULAR,
        ],
        compiler_params=params(1, vmem=63),
        name="backward",
    )(*arrays)


def shards(
    ends,
    segment_ids,
    valid_blocks,
    qkv_weight,
    qkv_bias,
    out_weight,
    gate_up_weight,
    down_weight,
    norm_gains,
):
    core = lax.axis_index("section")
    chip = lax.axis_index("dp")
    ff = 2 * FFH

    feature = jnp.arange(D, dtype=jnp.int32)
    spread = (
        (feature // 14 * 16 + feature % 14)[:, None] == jnp.arange(DP, dtype=jnp.int32)[None, :]
    ).astype(jnp.bfloat16)

    def widen(rows):
        return nn(rows, spread).astype(jnp.bfloat16)

    def feed_half(index):
        pieces = (
            lax.dynamic_slice_in_dim(gate_up_weight[0], index * FFH, FFH, 1),
            lax.dynamic_slice_in_dim(gate_up_weight[0], ff + index * FFH, FFH, 1),
            lax.dynamic_slice_in_dim(down_weight[0], index * FFH, FFH, 1),
        )
        return jnp.pad(jnp.concatenate(pieces, axis=1), ((0, 2), (0, 0)))

    def heads_half(index):
        pieces = (
            lax.dynamic_slice_in_dim(qkv_weight[0], D + index * 64, 64, 1),
            lax.dynamic_slice_in_dim(qkv_weight[0], index * 448, 448, 1),
            lax.dynamic_slice_in_dim(qkv_weight[0], D + 128 + index * 64, 64, 1),
            lax.dynamic_slice_in_dim(out_weight[0], index * 448, 448, 1),
        )
        return jnp.pad(jnp.concatenate(pieces, axis=1), ((0, 2), (0, 0)))

    def bias_half(index):
        row = qkv_bias[0]
        pieces = (
            row[D + index * 64 : D + index * 64 + 64],
            row[index * 448 : index * 448 + 448],
            row[D + 128 + index * 64 : D + 128 + index * 64 + 64],
            jnp.zeros((448,), row.dtype),
        )
        return jnp.concatenate(pieces)[None]

    small_in = jnp.concatenate([bias_half(0), bias_half(1), widen(norm_gains[0])], axis=0)
    small_in = jnp.pad(small_in, ((0, 12), (0, 0)))

    places = chip * T + jnp.arange(T, dtype=jnp.int32)
    frequency = THETA ** (-jnp.arange(32, dtype=jnp.float32) * 2.0 / 64)
    angles = places.astype(jnp.float32)[:, None] * frequency[None, :]
    cosine = jnp.tile(jnp.cos(angles), (1, 4))
    sine = jnp.sin(angles)
    sine = jnp.tile(jnp.concatenate([-sine, sine], axis=1), (1, 2))

    own_ids = lax.dynamic_slice_in_dim(segment_ids, chip * T, T, 1)
    starts = jnp.sum(
        (segment_ids[:, None, :] < own_ids[:, :, None]).astype(jnp.int32), axis=2
    )
    lengths = jnp.sum(valid_blocks, axis=1) * 128
    finish = jnp.minimum(places[None, :] + 1, lengths[:, None])
    bounds = jnp.stack([starts, finish, jnp.broadcast_to(places[None], (MB, T))], axis=1)
    bounds = jnp.pad(jnp.tile(bounds, (1, 1, 2)), ((0, 0), (0, 5), (0, 0)))
    (
        wa, wm, kv_all, gu_all, ends_all, gains_all, n1_all, qt_all, mixed_all, lse_all, att_all,
        mid_all, n2_all, hid_all, x_all, sq_all,
    ) = forward(
        heads_half(core),
        heads_half(1 - core),
        feed_half(core),
        feed_half(1 - core),
        widen(ends[0].reshape(R, D)),
        small_in,
        cosine,
        sine,
        bounds,
    )
    valid = lax.dynamic_slice_in_dim(valid_blocks, chip // 2, 1, 1) > 0
    squares = jnp.where(valid[None], sq_all[:, :MB, :3], 0.0).reshape(2, 9)
    squares = jnp.pad(squares, ((0, 6), (0, DP - 9)))
    _, dx, kept, other, small_sum = backward(
        wa, wm, kv_all, gu_all, ends_all[1], ends_all[0], x_all[0], gains_all, n1_all, qt_all,
        mixed_all, lse_all, att_all, mid_all, n2_all, squares, cosine, sine, bounds,
    )
    sides = (jnp.where(core == 0, kept, other), jnp.where(core == 0, other, kept))

    def column(start, size):
        return [side[:14, start : start + size] for side in sides]

    grad_gu = jnp.concatenate(column(0, FFH) + column(C_UP, FFH), axis=1)
    grad_down = jnp.concatenate(column(C_DOWN, FFH), axis=1)
    grad_qkv = jnp.concatenate(
        column(C_QK + 64, 448) + column(C_QK, 64) + column(C_VO, 64), axis=1
    )
    grad_out = jnp.concatenate(column(C_VO + 64, 448), axis=1)
    bias_rows = [side[14, CM:] for side in sides]
    grad_bias = jnp.concatenate(
        [row[64:QS] for row in bias_rows]
        + [row[:64] for row in bias_rows]
        + [row[QS : QS + 64] for row in bias_rows]
    )
    own_small = lax.dynamic_slice_in_dim(small_sum, 4 * core, 4, 0)
    grad_gain = own_small[:2].reshape(2, 64, 16)[:, :, :14].reshape(2, D)
    counts = jnp.sum(valid_blocks, axis=1).astype(jnp.float32) * 128 * D
    rms = jnp.sqrt(own_small[3, :9].reshape(MB, 3) / counts[:, None])
    ends_out = jnp.where(core == 0, dx, x_all[1])
    boundary = nt(ends_out, spread).astype(jnp.bfloat16).reshape(1, MB, T, D)
    return (
        boundary,
        grad_qkv[None],
        grad_bias[None],
        grad_out[None],
        grad_gu[None],
        grad_down[None],
        grad_gain[None],
        rms[None],
    )


def solution(mesh):
    in_specs = (
        P("section", None, "dp", None),
        P(),
        P(),
        P("section", "dp", None),
        P("section", None),
        P("section", "dp", None),
        P("section", "dp", None),
        P("section", "dp", None),
        P("section", None, None),
    )
    out_specs = (
        P("section", None, "dp", None),
        P("section", "dp", None),
        P("section", None),
        P("section", "dp", None),
        P("section", "dp", None),
        P("section", "dp", None),
        P("section", None, None),
        P("section", None, None),
    )
    return jax.shard_map(shards, mesh=mesh, in_specs=in_specs, out_specs=out_specs, check_vma=False)
```

```python
import functools
import math

import jax
import jax.numpy as jnp
from jax import lax
from jax.experimental import pallas as pl
from jax.experimental.pallas import tpu as pltpu
from jax.sharding import PartitionSpec as P

MESH = pl.DeviceIdType.MESH
EPS = 1e-06
THETA = 1000000.0
MASKED = -1e30

MB = 3
T = 64
R = MB * T
D = 896
DP = 1024
FFH = 2432
QS = 512
C_UP, C_DOWN, C_QK, C_VO, C = FFH, 2 * FFH, 3 * FFH, 3 * FFH + QS, 3 * FFH + 2 * QS
KB = 1024
SEQ = 4096
MIB = 1024 * 1024

BLOCK = 128

THIRDS = ((0, 22 * 128), (22 * 128, 22 * 128), (44 * 128, 21 * 128))
ORDERS = (("z", "y", "x"), ("y", "x", "z"), ("x", "z", "y"))
CM, CA = 3 * FFH, 2 * QS
M_THIRDS = ((0, FFH), (FFH, FFH), (2 * FFH, FFH))
A_THIRDS = ((0, 384), (384, 384), (768, 256))
FF_CHUNKS = ((0, 512), (512, 512), (1024, 512), (1536, 512), (2048, 384))


def position():
    chip = lax.axis_index("dp")
    return {"x": chip // 16, "y": (chip // 4) % 4, "z": chip % 4}


def moved(place, axis, distance):
    other = dict(place)
    other[axis] = (place[axis] + distance + 4) % 4
    return other


def chip_id(place):
    return {"dp": place["x"] * 16 + place["y"] * 4 + place["z"]}


def other_core():
    return {"section": 1 - lax.axis_index("section")}


def greet(place, core=False, chips=True, far=False):
    barrier = pltpu.get_barrier_semaphore()
    count = 0
    if chips:
        for axis in "xyz":
            for distance in (1, -1, 2) if far else (1, -1):
                pl.semaphore_signal(
                    barrier,
                    inc=1,
                    device_id=chip_id(moved(place, axis, distance)),
                    device_id_type=MESH,
                )
                count += 1
    if core:
        pl.semaphore_signal(barrier, inc=1, device_id=other_core(), device_id_type=MESH)
        count += 1
    return count


def settle(count):
    pl.semaphore_wait(pltpu.get_barrier_semaphore(), count)


def send(src, dst, send_sem, recv_sem, device):
    return pltpu.make_async_remote_copy(
        src, dst, send_sem, recv_sem, device_id=device, device_id_type=MESH
    )


def cube(done, place):
    return tuple(slice(None) if axis in done else place[axis] for axis in "xyz")


DIRECT = ((0, 1), (1, -1), (2, 2))


def gather_stages(view, place, send_sems, recv_sems, direct=(0, 1)):
    pending = []

    def copy(j, phase, k, whose, part, distance):
        ref = view(cube(ORDERS[j][:phase], whose), j, part)
        return send(
            ref,
            ref,
            send_sems.at[j, phase, k],
            recv_sems.at[j, phase, k],
            chip_id(moved(place, ORDERS[j][phase], distance)),
        )

    def first(phase):
        for j in range(3):
            for k, distance in DIRECT if phase in direct else DIRECT[:2]:
                one = copy(j, phase, k, place, None, distance)
                one.start()
                pending.append(one)

    def second(phase):
        if phase in direct:
            return
        for j in range(3):
            for k, distance in DIRECT[:2]:
                whose = moved(place, ORDERS[j][phase], -distance)
                copy(j, phase, k, whose, None, distance).wait_recv()
                one = copy(j, phase, 2 + k, whose, k, distance)
                one.start()
                pending.append(one)

    def third(phase):
        for j in range(3):
            if phase in direct:
                for k, distance in DIRECT:
                    whose = moved(place, ORDERS[j][phase], -distance)
                    copy(j, phase, k, whose, None, distance).wait_recv()
            else:
                for k, distance in DIRECT[:2]:
                    whose = moved(place, ORDERS[j][phase], 2)
                    copy(j, phase, 2 + k, whose, k, distance).wait_recv()

    def finish():
        for one in pending:
            one.wait_send()

    stages = []
    for phase in range(3):
        stages.append(functools.partial(first, phase))
        stages.append(functools.partial(second, phase))
        stages.append(functools.partial(third, phase))
    stages.append(finish)
    return stages


PARTS = (
    ((0, 256), (256, 256), (512, 256), (768, 384)),
    ((1152, 256), (1408, 256), (1664, 384), (2048, 384)),
)
ROUNDS = 4
TURNS = tuple((j, k, (1, -1)[k]) for j in range(3) for k in range(2))


class LargeGather:
    def __init__(self, ref, place, send_sems, recv_sems, part_sems, pass_sems):
        self.ref, self.place = ref, place
        self.part_sems, self.pass_sems = part_sems, pass_sems
        stages = gather_stages(
            weight_view(ref, M_THIRDS), place, send_sems, recv_sems, direct=(0,)
        )
        self.phases, self.done = stages[:6], stages[9]
        self.pending = []

    def slab(self, j, whose, half, r):
        start, size = PARTS[half][r]
        chips = cube(ORDERS[j][:2], whose)
        return self.ref.at[chips + (slice(None), pl.ds(j * FFH + start, size))]

    def whose(self, j, distance):
        return moved(self.place, ORDERS[j][2], distance)

    def part(self, j, k, distance, half, r, whose):
        ref = self.slab(j, whose, half, r)
        sems = [side.at[j, k, half, r] for side in self.part_sems]
        return send(ref, ref, *sems, chip_id(self.whose(j, distance)))

    def passed(self, j, k, distance, r, whose):
        ref = self.slab(j, whose, k, r)
        sems = [side.at[j, k, r] for side in self.pass_sems]
        return send(ref, ref, *sems, chip_id(self.whose(j, distance)))

    def start(self, one):
        one.start()
        self.pending.append(one)

    def ahead(self, r):
        for j, k, distance in TURNS:
            self.start(self.part(j, k, distance, k, r, self.place))

    def rest(self, r):
        for j, k, distance in TURNS:
            self.start(self.part(j, k, distance, 1 - k, r, self.place))

    def pass_on(self, r):
        for j, k, distance in TURNS:
            back = self.whose(j, -distance)
            self.part(j, k, distance, k, r, back).wait_recv()
            self.start(self.passed(j, k, distance, r, back))

    def last(self):
        for j, k, distance in TURNS:
            for r in range(ROUNDS):
                self.part(j, k, distance, 1 - k, r, self.whose(j, -distance)).wait_recv()
                self.passed(j, k, distance, r, self.whose(j, 2)).wait_recv()

    def finish(self):
        self.done()
        for one in self.pending:
            one.wait_send()


def scatter_stages(
    view, halves, wholes, place, send_sems, recv_sems, final, begin=0, direct=(1, 2)
):
    pending = []

    def half_copy(j, phase, k, distance):
        far = moved(place, back_axis(j, phase), 2)
        return send(
            view(back_chips(j, phase, far), j, k),
            halves[phase](j, k),
            send_sems.at[j, phase, k],
            recv_sems.at[j, phase, k],
            chip_id(moved(place, back_axis(j, phase), distance)),
        )

    def whole_copy(j, phase, k, distance):
        near = moved(place, back_axis(j, phase), distance)
        slot = k if phase in direct else 2 + k
        return send(
            view(back_chips(j, phase, near), j, None),
            wholes[phase](j, k),
            send_sems.at[j, phase, slot],
            recv_sems.at[j, phase, slot],
            chip_id(near),
        )

    def first(phase):
        for j in range(3):
            for k, distance in DIRECT if phase in direct else DIRECT[:2]:
                one = (whole_copy if phase in direct else half_copy)(j, phase, k, distance)
                one.start()
                pending.append(one)

    def second(phase):
        if phase in direct:
            return
        for j in range(3):
            for k, distance in DIRECT[:2]:
                half_copy(j, phase, k, distance).wait_recv()
                near = moved(place, back_axis(j, phase), distance)
                mine = view(back_chips(j, phase, near), j, k)
                add(mine, mine, halves[phase](j, k))
                one = whole_copy(j, phase, k, distance)
                one.start()
                pending.append(one)

    def third(phase):
        turns = DIRECT if phase in direct else DIRECT[:2]
        for j in range(3):
            for k, distance in turns:
                whole_copy(j, phase, k, distance).wait_recv()
            mine = view(back_chips(j, phase, place), j, None)
            terms = [wholes[phase](j, k) for k, distance in turns]
            if phase < 2:
                add(mine, mine, *terms)
            else:
                final(j, mine, *terms)

    def finish():
        for one in pending:
            one.wait_send()

    stages = []
    for phase in range(begin, 3):
        stages.append(functools.partial(first, phase))
        stages.append(functools.partial(second, phase))
        stages.append(functools.partial(third, phase))
    stages.append(finish)
    return stages


def back_axis(j, phase):
    return ORDERS[j][2 - phase]


def back_chips(j, phase, whose):
    return cube(ORDERS[j][: 2 - phase], whose)


def add(dst, *terms):
    dst[...] = sum(term[...].astype(jnp.float32) for term in terms).astype(dst.dtype)


def half_of(size, part):
    half = size // 256 * 128
    return (0, half) if part == 0 else (half, size - half)


class LargeScatter:
    def __init__(
        self, source, slab, got_half, got_whole, spare, inner_halves, inner_wholes, place,
        half_sems, rest_sems, pass_sems, load_sems, send_sems, recv_sems, final,
    ):
        self.source, self.slab, self.place = source, slab, place
        self.got_half, self.got_whole, self.spare = got_half, got_whole, spare
        self.half_sems, self.rest_sems, self.pass_sems = half_sems, rest_sems, pass_sems
        self.load_sems = load_sems
        self.pending = []

        def view(chips, j, part):
            rest = tuple(index for axis, index in zip("xyz", chips) if axis != back_axis(j, 0))
            cols = slice(None) if part is None else pl.ds(*half_of(FFH, part))
            return slab.at[(j,) + rest + (slice(None), cols)]

        stages = scatter_stages(
            view, inner_halves, inner_wholes, place, send_sems, recv_sems, final, begin=1, direct=(2,)
        )
        self.phases, self.done = stages[:-1], stages[-1]

    def terms(self, j, whose, cols):
        chips = back_chips(j, 0, whose)
        return self.source.at[chips + (slice(None), pl.ds(j * FFH + cols[0], cols[1]))]

    def near(self, j, distance):
        return moved(self.place, back_axis(j, 0), distance)

    def half_ref(self, j, k, r):
        start, size = PARTS[k][r]
        return self.got_half.at[j, k, :, :, :, pl.ds(start - PARTS[k][0][0], size)]

    def copy(self, src, dst, sems, j, k, distance, r):
        return send(
            src, dst, sems[0].at[j, k, r], sems[1].at[j, k, r], chip_id(self.near(j, distance))
        )

    def half_copy(self, j, k, distance, r):
        src = self.terms(j, self.near(j, 2), PARTS[k][r])
        return self.copy(src, self.half_ref(j, k, r), self.half_sems, j, k, distance, r)

    def rest_copy(self, j, k, distance, r):
        cols = PARTS[1 - k][r]
        src = self.terms(j, self.near(j, distance), cols)
        dst = self.got_whole.at[j, k, :, :, :, pl.ds(*cols)]
        return self.copy(src, dst, self.rest_sems, j, k, distance, r)

    def pass_copy(self, j, k, distance, r):
        dst = self.got_whole.at[j, k, :, :, :, pl.ds(*PARTS[k][r])]
        return self.copy(self.half_ref(j, k, r), dst, self.pass_sems, j, k, distance, r)

    def own_load(self, j, k, distance, r):
        return pltpu.make_async_copy(
            self.terms(j, self.near(j, distance), PARTS[k][r]),
            self.spare.at[j, k, :, :, :, pl.ds(0, PARTS[k][r][1])],
            self.load_sems.at[2 * j + k],
        )

    def slab_load(self, j):
        return pltpu.make_async_copy(
            self.terms(j, self.place, (0, FFH)), self.slab.at[j], self.load_sems.at[6 + j]
        )

    def start(self, one):
        one.start()
        self.pending.append(one)

    def ahead(self, r):
        for j, k, distance in TURNS:
            self.start(self.half_copy(j, k, distance, r))
        if r == 0:
            for j, k, distance in TURNS:
                self.own_load(j, k, distance, 0).start()
            for j in range(3):
                self.slab_load(j).start()

    def rest(self, r):
        for j, k, distance in TURNS:
            self.start(self.rest_copy(j, k, distance, r))

    def pass_on(self, r):
        for j, k, distance in TURNS:
            self.half_copy(j, k, distance, r).wait_recv()
            self.own_load(j, k, distance, r).wait()
            own = self.spare.at[j, k, :, :, :, pl.ds(0, PARTS[k][r][1])]
            add(self.half_ref(j, k, r), self.half_ref(j, k, r), own)
            self.start(self.pass_copy(j, k, distance, r))
            if r + 1 < ROUNDS:
                self.own_load(j, k, distance, r + 1).start()

    def third(self):
        for j in range(3):
            self.slab_load(j).wait()
            for k in range(2):
                for r in range(ROUNDS):
                    self.rest_copy(j, k, (1, -1)[k], r).wait_recv()
                    self.pass_copy(j, k, (1, -1)[k], r).wait_recv()
            add(self.slab.at[j], self.slab.at[j], self.got_whole.at[j, 0], self.got_whole.at[j, 1])

    def finish(self):
        self.done()
        for one in self.pending:
            one.wait_send()


def weight_view(ref, thirds=THIRDS):
    def view(chips, j, part):
        start, size = thirds[j]
        if part is not None:
            half = size // 256 * 128
            start, size = (start, half) if part == 0 else (start + half, size - half)
        return ref.at[tuple(chips) + (slice(None), pl.ds(start, size))]

    return view


def token_view(ref):
    def view(chips, j, part):
        rows = slice(None) if part is None else pl.ds(part * 32, 32)
        return ref.at[tuple(chips) + (j, rows, slice(None))]

    return view


def params(collective_id=None, vmem=56):
    if collective_id is None:
        return pltpu.CompilerParams(vmem_limit_bytes=vmem * MIB)
    return pltpu.CompilerParams(
        collective_id=collective_id, has_side_effects=True, vmem_limit_bytes=vmem * MIB
    )


ANY = pl.BlockSpec(memory_space=pl.ANY)
VMEM = pl.BlockSpec(memory_space=pltpu.VMEM)
SMEM = pl.BlockSpec(memory_space=pltpu.SMEM)
DMA = pltpu.SemaphoreType.DMA


def shape(dims, dtype):
    return jax.ShapeDtypeStruct(dims, dtype)


def nn(left, right):
    return jnp.dot(left, right, preferred_element_type=jnp.float32)


def nt(left, right):
    return lax.dot_general(
        left, right, (((1,), (1,)), ((), ())), preferred_element_type=jnp.float32
    )


def tn(left, right):
    return lax.dot_general(
        left, right, (((0,), (0,)), ((), ())), preferred_element_type=jnp.float32
    )


DEAD = 4


def key_marks(segments, lengths, chip):
    rows = lax.broadcasted_iota(jnp.int32, (8, SEQ), 0)
    keys = lax.broadcasted_iota(jnp.int32, (8, SEQ), 1)
    groups = []
    for batch in range(MB):
        same = (rows < DEAD) & (segments[batch : batch + 1, :] == rows)
        dead = (keys >= chip * T) | (keys.astype(jnp.float32) >= lengths[batch])
        groups.append(jnp.where(same | ((rows == DEAD) & dead), 1.0, 0.0))
    groups.append(jnp.zeros((128 - 8 * MB, SEQ), jnp.float32))
    return jnp.concatenate(groups, axis=0).T.astype(jnp.bfloat16)


def query_marks(ids, batch, dead):
    place = lax.broadcasted_iota(jnp.int32, (128, 128), 0) - 8 * batch
    hit = (place >= 0) & (place < DEAD) & (place != ids)
    if dead:
        hit = hit | (place == DEAD)
    return jnp.where(hit, MASKED, 0.0).astype(jnp.bfloat16)


def own_bias(full):
    key = lax.broadcasted_iota(jnp.int32, (T, 128), 0)
    query = lax.broadcasted_iota(jnp.int32, (T, 128), 1) % T
    allowed = (key == query) | ((key <= query) & (full > 0.0))
    return jnp.where(allowed, 0.0, MASKED)


def all_heads(two):
    return jnp.concatenate([two] * 4, axis=1)


def mean_of(values):
    return jnp.sum(values, axis=-1, keepdims=True) * (1.0 / D)


def turn(values, cosine, sine):
    lane = lax.broadcasted_iota(jnp.int32, values.shape, 1) % 64
    swapped = jnp.where(lane < 32, pltpu.roll(values, QS - 32, 1), pltpu.roll(values, 32, 1))
    return values * cosine + swapped * sine


def tiled(table):
    wide = jnp.concatenate([table] * 4, axis=1)
    return jnp.concatenate([wide] * MB, axis=0)


def to_columns(rows):
    turned = rows.T
    return jnp.concatenate([turned[64 * h : 64 * h + 64] for h in range(8)], axis=1)


def to_rows(columns):
    pairs = []
    for pair in range(4):
        turned = columns[:, 128 * pair : 128 * pair + 128].T
        pairs.append(jnp.concatenate([turned[:64], turned[64:]], axis=1))
    return jnp.concatenate(pairs, axis=1)


def without_first_slot(rows):
    lane = lax.broadcasted_iota(jnp.int32, rows.shape, 1)
    return jnp.where(lane < 64, 0.0, rows)


def spread_matrix():
    row = lax.broadcasted_iota(jnp.int32, (D, DP), 0)
    column = lax.broadcasted_iota(jnp.int32, (1, DP), 1)
    spot = column % 16
    target = jnp.where(spot < 14, column // 16 * 14 + spot, -1)
    return jnp.where(row == target, 1.0, 0.0).astype(jnp.bfloat16)


def forward_kernel(
    gate_up, down, qkv, out_w, bias_in, gains_in, ends, segments, valid, cosine, sine,
    wa, wm, kv, gu, cot, gains, n1, qt, mixed, lse, att, mid, n2, hid, xs_, sq, km, qm, ob,
    ends_v, small_v, give_a, give_m, stage_a, stage_m, wat, wml, kvb, gu_v, mine, theirs,
    lsem, ssem, rsem, a_s, a_r, m_s, m_r, mp_s, mp_r, mq_s, mq_r, k_s, k_r, osem, wsem, xsem,
    xrsem,
):
    place = position()
    core = lax.axis_index("section")
    chip = lax.axis_index("dp")
    here = (place["x"], place["y"], place["z"])
    partners = greet(place, core=True, far=True)

    def heads_half(half):
        wide = qkv[...].astype(jnp.float32)
        outs_ = out_w[...].astype(jnp.float32)
        return jnp.concatenate(
            [
                wide[:, D + 64 * half : D + 64 * half + 64],
                wide[:, 448 * half : 448 * half + 448],
                wide[:, D + 128 + 64 * half : D + 192 + 64 * half],
                outs_[:, 448 * half : 448 * half + 448],
            ],
            axis=1,
        )

    def bias_half(half):
        wide = bias_in[...].astype(jnp.float32)
        return jnp.concatenate(
            [
                wide[:, D + 64 * half : D + 64 * half + 64],
                wide[:, 448 * half : 448 * half + 448],
                wide[:, D + 128 + 64 * half : D + 192 + 64 * half],
                jnp.zeros((1, 448), jnp.float32),
            ],
            axis=1,
        )

    halves = [heads_half(0), heads_half(1)]
    for dst, side in ((stage_a.at[core], 0), (give_a, 1)):
        dst[...] = jnp.zeros((16, CA), jnp.bfloat16)
        dst[0:14, :] = jnp.where(core == side, halves[0], halves[1]).astype(jnp.bfloat16)
    for dst, index in ((stage_m.at[core], core), (give_m, 1 - core)):
        dst[...] = jnp.zeros((16, CM), jnp.bfloat16)
        start = pl.multiple_of(index * FFH, 128)
        dst[0:14, 0:FFH] = gate_up[:, pl.ds(start, FFH)]
        dst[0:14, FFH : 2 * FFH] = gate_up[:, pl.ds(pl.multiple_of(start + 2 * FFH, 128), FFH)]
        dst[0:14, 2 * FFH : CM] = down[:, pl.ds(start, FFH)]
    settle(partners)

    trades = []

    def trade(index, give, dst):
        out = send(give, dst.at[core], ssem.at[index], rsem.at[index], other_core())
        back = send(give, dst.at[1 - core], ssem.at[index], rsem.at[index], other_core())
        out.start()
        trades.append((out, back))

    trade(0, give_a, stage_a)
    trade(1, give_m, stage_m)

    def arrive(index):
        out, back = trades[index]
        back.wait_recv()
        out.wait_send()

    arrive(0)
    into = [
        pltpu.make_async_copy(stage_a.at[layer], wat.at[(layer,) + here], lsem.at[layer])
        for layer in range(2)
    ]
    for one in into:
        one.start()
    for one in into:
        one.wait()
    attn = [
        gather_stages(weight_view(wat.at[layer], A_THIRDS), place, a_s.at[layer], a_r.at[layer])
        for layer in range(2)
    ]
    feed = [
        LargeGather(
            ref,
            place,
            m_s.at[layer],
            m_r.at[layer],
            (mp_s.at[layer], mp_r.at[layer]),
            (mq_s.at[layer], mq_r.at[layer]),
        )
        for layer, ref in enumerate((wml, wm.at[1]))
    ]
    early, late = feed
    keys = [
        gather_stages(token_view(kvb.at[layer]), place, k_s.at[layer], k_r.at[layer])
        for layer in range(2)
    ]
    attn[0][0]()
    attn[1][0]()
    arrive(1)
    into = [
        pltpu.make_async_copy(stage_m.at[0], wml.at[here], lsem.at[2]),
        pltpu.make_async_copy(stage_m.at[1], wm.at[(1,) + here], lsem.at[3]),
    ]
    for one in into:
        one.start()
    for one in into:
        one.wait()
    early.phases[0]()
    spread = spread_matrix()
    ends_v[core] = nn(ends[...], spread).astype(jnp.bfloat16)
    small_v[core] = jnp.zeros((8, DP), jnp.float32)
    small_v[core, 0:1, :] = bias_half(0)
    small_v[core, 1:2, :] = bias_half(1)
    small_v[core, 2:4, :] = nn(gains_in[...], spread)
    trade(2, ends_v.at[core], ends_v)
    trade(3, small_v.at[core], small_v)
    attn[0][1]()
    attn[1][1]()
    early.phases[1]()
    lengths = [
        jnp.sum(valid[batch : batch + 1, :].astype(jnp.float32), axis=1, keepdims=True) * BLOCK
        for batch in range(MB)
    ]
    km[...] = key_marks(segments, lengths, chip)
    pair = segments[:, pl.ds(pl.multiple_of(chip // 2 * 128, 128), 128)]
    ids = jnp.where(chip % 2 == 0, pair[:, :64], pair[:, 64:])
    ids = jnp.concatenate([ids, ids], axis=1)
    first_key = (chip * T).astype(jnp.float32)
    for batch in range(MB):
        for kind in range(2):
            qm[kind, batch] = query_marks(ids[batch : batch + 1, :], batch, kind == 0)
        full = jnp.where(first_key < lengths[batch], 1.0, 0.0)
        ob[batch] = own_bias(full)
    for index in range(2, 8):
        attn[0][index]()
        attn[1][index]()
    early.phases[2]()
    early.phases[3]()
    arrive(2)
    arrive(3)
    cot[...] = ends_v[...]
    gains[...] = small_v[...]
    attn[0][8]()

    outs = []

    def store(src, dst, index):
        one = pltpu.make_async_copy(src, dst, osem.at[index])
        one.start()
        outs.append(one)

    def rows_of(layer):
        return ends_v[0] if layer == 0 else xs_[0]

    def project(layer):
        rows = rows_of(layer).astype(jnp.float32)
        gain = gains[layer, 2:3, :]
        bias = jnp.where(core == 0, gains[layer, 0:1, :], gains[layer, 1:2, :])
        normed = (rows * lax.rsqrt(mean_of(rows * rows) + EPS) * gain).astype(jnp.bfloat16)
        n1[layer] = normed
        weights = wat[layer].reshape(DP, CA)
        projected = nn(normed, weights[:, : QS + 128]) + bias[:, : QS + 128]
        turned = turn(projected[:, :QS], tiled(cosine[...]), tiled(sine[...]))
        own = jnp.concatenate([turned[:, :64], projected[:, QS : QS + 64]], axis=1)
        kvb[(layer,) + here] = own.astype(jnp.bfloat16).reshape(MB, T, 128)
        heads = without_first_slot(turned).astype(jnp.bfloat16).astype(jnp.float32) * 0.125
        for batch in range(MB):
            columns = to_columns(heads[batch * T : (batch + 1) * T]).astype(jnp.bfloat16)
            qt[layer, batch] = jnp.concatenate([columns, jnp.zeros_like(columns)], axis=0)

    def attend(layer, batch):
        queries = jnp.concatenate([qt[layer, batch], all_heads(qm[0, batch])], axis=0)
        own_queries = jnp.concatenate([qt[layer, batch], all_heads(qm[1, batch])], axis=0)
        rows = kvb[(layer,) + here + (batch,)]
        marks = km[pl.ds(pl.multiple_of(chip * T, T), T), :]
        scores = nn(jnp.concatenate([rows, marks], axis=1), own_queries) + all_heads(ob[batch])
        top = jnp.max(scores, axis=0, keepdims=True)
        probs = jnp.exp(scores - top)
        total = jnp.sum(probs, axis=0, keepdims=True)
        sums = tn(rows, probs.astype(jnp.bfloat16))

        def step(index, carry):
            top, total, sums = carry
            rows = kvb[layer, index, :, :, batch].reshape(KB, 128)
            marks = km[pl.ds(pl.multiple_of(index * KB, KB), KB), :]
            scores = nn(jnp.concatenate([rows, marks], axis=1), queries)
            new_top = jnp.maximum(top, jnp.max(scores, axis=0, keepdims=True))
            shrink = jnp.exp(top - new_top)
            probs = jnp.exp(scores - new_top)
            total = total * shrink + jnp.sum(probs, axis=0, keepdims=True)
            sums = sums * shrink + tn(rows, probs.astype(jnp.bfloat16))
            return new_top, total, sums

        top, total, sums = lax.fori_loop(0, (chip + 15) // 16, step, (top, total, sums))
        result = (sums / total)[64:, :]
        mixed[layer, batch] = result
        lse[layer, batch] = jnp.broadcast_to(top + jnp.log(total), (8, QS))
        att[layer, pl.ds(batch * T, T), :] = without_first_slot(to_rows(result)).astype(
            jnp.bfloat16
        )

    def swap(slot):
        return send(mine.at[slot], theirs.at[slot], xsem.at[slot], xrsem.at[slot], other_core())

    def branch_of(layer):
        mine[0] = nt(att[layer], wat[layer, :, :, :, :, QS:].reshape(DP, QS))
        one = swap(0)
        one.start()
        one.wait()
        branch = mine[0] + theirs[0]
        middle = rows_of(layer).astype(jnp.float32) + branch
        mid[layer] = middle
        scale = lax.rsqrt(mean_of(middle * middle) + EPS)
        n2[layer] = (middle * scale * gains[layer, 3:4, :]).astype(jnp.bfloat16)
        return branch

    def feed_forward(layer, branch, hooks):
        normed = n2[layer]
        sums = jnp.zeros((R, DP), jnp.float32)
        for index, (start, size) in enumerate(FF_CHUNKS):
            hooks[index]()

            def weights(first, start=start, size=size):
                return wml[:, :, :, :, pl.ds(first + start, size)].reshape(DP, size)

            gate = nn(normed, weights(0))
            up = nn(normed, weights(FFH))
            gu_v[:, pl.ds(start, size)] = gate
            gu_v[:, pl.ds(FFH + start, size)] = up
            hidden = (gate * jax.nn.sigmoid(gate) * up).astype(jnp.bfloat16)
            hid[layer, :, pl.ds(start, size)] = hidden
            sums = sums + nt(hidden, weights(2 * FFH))
        store(gu_v, gu.at[layer], 4 + layer)
        mine[1] = sums
        one = swap(1)
        one.start()
        one.wait()
        result = mine[1] + theirs[1]
        middle = mid[layer]
        xs_[layer] = (middle + result).astype(jnp.bfloat16)
        rows = rows_of(layer).astype(jnp.float32)
        lane = lax.broadcasted_iota(jnp.int32, (8, 128), 1)
        table = jnp.zeros((8, 128), jnp.float32)
        for kind, values in enumerate((rows, branch, result)):
            squares = jnp.sum(values * values, axis=1, keepdims=True)
            for batch in range(MB):
                one = jnp.sum(squares[batch * T : (batch + 1) * T], axis=0, keepdims=True)
                one = jnp.where(first_key < lengths[batch], one, 0.0)
                table = jnp.where(lane == 3 * batch + kind, one, table)
        sq[layer] = table

    def nothing():
        pass

    def beside(stages, rounds):
        rounds = iter(rounds)
        for index in range(8):
            stages[index]()
            if index not in (2, 5):
                next(rounds)()

    def calls(method, *numbers):
        return [functools.partial(method, r) for r in numbers]

    def rounds_of(*methods):
        for method in methods:
            for r in range(ROUNDS):
                method(r)

    project(0)
    beside(
        keys[0],
        [
            early.phases[4],
            nothing,
            lambda: (early.phases[5](), early.ahead(0)),
            *calls(early.ahead, 1, 2, 3),
        ],
    )
    keys[0][8]()
    rounds_of(early.rest)
    store(kvb.at[0], kv.at[0], 0)
    attend(0, 0)
    early.pass_on(0)
    early.pass_on(1)
    attend(0, 1)
    early.pass_on(2)
    early.pass_on(3)
    late.phases[0]()
    attend(0, 2)
    late.phases[1]()
    branch = branch_of(0)
    early.last()
    store(wml, wm.at[0], 2)
    late.phases[2]()
    late.phases[3]()
    feed_forward(0, branch, [nothing] * 3 + [late.phases[4], nothing])
    late.phases[5]()
    late.ahead(0)
    late.ahead(1)
    attn[1][8]()
    store(wat, wa, 1)
    project(1)
    beside(
        keys[1], [nothing, nothing, *calls(late.ahead, 2, 3), *calls(late.rest, 0, 1)]
    )
    keys[1][8]()
    late.rest(2)
    late.rest(3)
    store(kvb.at[1], kv.at[1], 3)
    attend(1, 0)
    late.pass_on(0)
    late.pass_on(1)
    attend(1, 1)
    late.pass_on(2)
    late.pass_on(3)
    attend(1, 2)
    branch = branch_of(1)
    late.last()
    early.finish()
    outs[1].wait()
    outs[2].wait()
    loads = []
    for index, (start, size) in enumerate(FF_CHUNKS):
        for part in range(3):
            cols = pl.ds(part * FFH + start, size)
            loads.append(
                pltpu.make_async_copy(
                    wm.at[1, :, :, :, :, cols],
                    wml.at[:, :, :, :, cols],
                    wsem.at[3 * index + part],
                )
            )
    for one in loads:
        one.start()

    def ready(index):
        for one in loads[3 * index : 3 * index + 3]:
            one.wait()

    feed_forward(1, branch, [functools.partial(ready, index) for index in range(5)])
    for index, one in enumerate(outs):
        if index not in (1, 2):
            one.wait()
    late.finish()
    for stages in attn + keys:
        stages[9]()


def forward(*arrays):
    low, full = jnp.bfloat16, jnp.float32
    return pl.pallas_call(
        forward_kernel,
        out_shape=(
            shape((2, 4, 4, 4, 16, CA), low),
            shape((2, 4, 4, 4, 16, CM), low),
            shape((2, 4, 4, 4, MB, T, 128), low),
            shape((2, R, 2 * FFH), full),
            shape((2, R, DP), low),
            shape((2, 8, DP), full),
            shape((2, R, DP), low),
            shape((2, MB, 128, QS), low),
            shape((2, MB, 64, QS), full),
            shape((2, MB, 8, QS), full),
            shape((2, R, QS), low),
            shape((2, R, DP), full),
            shape((2, R, DP), low),
            shape((2, R, FFH), low),
            shape((2, R, DP), low),
            shape((2, 8, 128), full),
            shape((SEQ, 128), low),
            shape((2, MB, 128, 128), low),
            shape((MB, T, 128), full),
        ),
        in_specs=[VMEM] * 11,
        out_specs=(ANY,) * 4 + (VMEM,) * 15,
        scratch_shapes=[
            pltpu.VMEM((2, R, DP), low),
            pltpu.VMEM((2, 8, DP), full),
            pltpu.VMEM((16, CA), low),
            pltpu.VMEM((16, CM), low),
            pltpu.VMEM((2, 16, CA), low),
            pltpu.VMEM((2, 16, CM), low),
            pltpu.VMEM((2, 4, 4, 4, 16, CA), low),
            pltpu.VMEM((4, 4, 4, 16, CM), low),
            pltpu.VMEM((2, 4, 4, 4, MB, T, 128), low),
            pltpu.VMEM((R, 2 * FFH), full),
            pltpu.VMEM((2, R, DP), full),
            pltpu.VMEM((2, R, DP), full),
            DMA((4,)),
            DMA((4,)),
            DMA((4,)),
            DMA((2, 3, 3, 4)),
            DMA((2, 3, 3, 4)),
            DMA((2, 3, 3, 4)),
            DMA((2, 3, 3, 4)),
            DMA((2, 3, 2, 2, ROUNDS)),
            DMA((2, 3, 2, 2, ROUNDS)),
            DMA((2, 3, 2, ROUNDS)),
            DMA((2, 3, 2, ROUNDS)),
            DMA((2, 3, 3, 4)),
            DMA((2, 3, 3, 4)),
            DMA((6,)),
            DMA((15,)),
            DMA((2,)),
            DMA((2,)),
        ],
        compiler_params=params(0, vmem=60),
        name="forward",
    )(*arrays)


def norm_back(grad, rows, gain):
    scale = lax.rsqrt(mean_of(rows * rows) + EPS)
    scaled = grad * gain
    back = scale * scaled - rows * (scale * scale * scale) * mean_of(scaled * rows)
    return back, jnp.sum(grad * rows * scale, axis=0, keepdims=True)


SLOT = 256
FF_SLOTS = tuple((start, min(SLOT, FFH - start)) for start in range(0, FFH, SLOT))
A_SLOTS = ((0, 3), (3, 3), (6, 2))


def slot_view(pool):
    def view(chips, j, part):
        lanes = slice(None) if part is None else pl.ds(part * 128, 128)
        return pool.at[(pl.ds(*A_SLOTS[j]),) + tuple(chips) + (slice(None), lanes)]

    return view


def backward_kernel(
    wa, wm, kv, gu, ends, xs_, gains, n1, qt, mixed, lse, att, mid, n2, squares, cosine, sine,
    km, qm, ob,
    grads, dx, outv, other, small_out,
    pool, gbuf, n2t, dmt, wat, mine, theirs, dout, dmid, da, dot_, dqk, low, vlow, kvb, own,
    kh0, kw0, kw1, kw2, slab, got_half, got_whole, spare, mh1, mw1, mw2, ah0, aw0, aw1, aw2,
    sbuf,
    lsem, psem, gsem, usem, xsem, xrsem, ks, kr, hs, hr, os_, or_, ws, wr, ls, ms, mr, as_, ar,
    bs, br, fs, fr, credit,
):
    place = position()
    core = lax.axis_index("section")
    chip = lax.axis_index("dp")
    here = (place["x"], place["y"], place["z"])
    partners = greet(place, core=True, far=True)
    steps = (chip + 15) // 16

    def heads_load(layer):
        return pltpu.make_async_copy(wa.at[layer], wat, lsem.at[2 * layer])

    def keys_load(layer):
        return pltpu.make_async_copy(kv.at[layer], kvb, lsem.at[2 * layer + 1])

    heads_load(1).start()
    keys_load(1).start()
    dout[...] = ends[1].astype(jnp.float32)
    settle(partners)
    small = [[None] * 4, [None] * 4]
    stored = {}

    def swap(slot):
        return send(mine.at[slot], theirs.at[slot], xsem.at[slot], xrsem.at[slot], other_core())

    def back_feed(layer, hooks):
        def loads(index):
            start, size = FF_SLOTS[index]
            slot = index % 2
            copies = []
            for part in range(3):
                copies.append(
                    pltpu.make_async_copy(
                        wm.at[layer, :, :, :, :, pl.ds(part * FFH + start, size)],
                        pool.at[3 * slot + part, :, :, :, :, pl.ds(0, size)],
                        psem.at[slot, part],
                    )
                )
            for part in range(2):
                copies.append(
                    pltpu.make_async_copy(
                        gu.at[layer, :, pl.ds(part * FFH + start, size)],
                        gbuf.at[slot, part, :, pl.ds(0, size)],
                        usem.at[slot, part],
                    )
                )
            return copies

        for index in range(2):
            for one in loads(index):
                one.start()
        grad_in = dout[...]
        grad_low = grad_in.astype(jnp.bfloat16)
        n2t[...] = n2[layer].astype(jnp.float32).T.astype(jnp.bfloat16)
        dmt[...] = grad_low.astype(jnp.float32).T.astype(jnp.bfloat16)
        mine[0] = jnp.zeros((R, DP), jnp.float32)
        for index, (start, size) in enumerate(FF_SLOTS):
            slot = index % 2
            hooks.get(index, lambda: None)()
            for one in loads(index):
                one.wait()

            def weights(part, slot=slot, size=size):
                return pool[3 * slot + part, :, :, :, :, :size].reshape(DP, size)

            grad_hidden = nn(grad_low, weights(2))
            gate = gbuf[slot, 0, :, :size]
            up = gbuf[slot, 1, :, :size]
            sigma = jax.nn.sigmoid(gate)
            hidden = (gate * sigma * up).astype(jnp.bfloat16)
            grad_gate = grad_hidden * up * sigma * (1.0 + gate * (1.0 - sigma))
            grad_gate = grad_gate.astype(jnp.bfloat16)
            grad_up = (grad_hidden * gate * sigma).astype(jnp.bfloat16)
            mine[0] += nt(grad_gate, weights(0)) + nt(grad_up, weights(1))
            if index + 2 < len(FF_SLOTS):
                for one in loads(index + 2):
                    one.start()
            products = ((n2t, grad_gate), (n2t, grad_up), (dmt, hidden))
            for part, (left, right) in enumerate(products):
                held = 6 + 3 * slot + part
                if held in stored:
                    stored.pop(held).wait()
                pool[held, :, :, :, :, :size] = (
                    nn(left[...], right).astype(jnp.bfloat16).reshape(4, 4, 4, 16, size)
                )
                stored[held] = pltpu.make_async_copy(
                    pool.at[held, :, :, :, :, pl.ds(0, size)],
                    grads.at[layer, :, :, :, :, pl.ds(part * FFH + start, size)],
                    gsem.at[slot, part],
                )
                stored[held].start()
        one = swap(0)
        one.start()
        one.wait()
        back, gain_row = norm_back(mine[0] + theirs[0], mid[layer], gains[layer, 3:4, :])
        small[layer][1] = gain_row
        middle = grad_in + back
        dmid[...] = middle
        middle_low = middle.astype(jnp.bfloat16)
        da[layer] = middle_low
        heads_load(layer).wait()
        turned = nn(middle_low, wat[:, :, :, :, QS:].reshape(DP, QS))
        turned = without_first_slot(turned.astype(jnp.bfloat16).astype(jnp.float32))
        for batch in range(MB):
            columns = to_columns(turned[batch * T : (batch + 1) * T]).astype(jnp.bfloat16)
            dot_[batch] = jnp.concatenate([jnp.zeros_like(columns), columns], axis=0)
        for held in list(stored):
            stored.pop(held).wait()

    def back_attend(layer, batch):
        if batch == 0:
            keys_load(layer).wait()
        slopes_out = dot_[batch]
        queries = qt[layer, batch]
        marked = jnp.concatenate([queries, all_heads(qm[0, batch])], axis=0)
        log_total = lse[layer, batch, 0:1, :]
        inner = jnp.sum(
            mixed[layer, batch] * slopes_out[64:, :].astype(jnp.float32), axis=0, keepdims=True
        )

        def terms(rows, scores):
            probs = jnp.exp(scores - log_total)
            slopes = (probs * (nn(rows, slopes_out) - inner)).astype(jnp.bfloat16)
            both = nt(slopes, queries) + nt(probs.astype(jnp.bfloat16), slopes_out)
            return both.astype(jnp.bfloat16), tn(rows, slopes)

        own_rows = kvb[here + (batch,)]
        marks = km[pl.ds(pl.multiple_of(chip * T, T), T), :]
        scores = nn(
            jnp.concatenate([own_rows, marks], axis=1),
            jnp.concatenate([queries, all_heads(qm[1, batch])], axis=0),
        )
        own_both, sums = terms(own_rows, scores + all_heads(ob[batch]))

        def step(index, sums):
            rows = kvb[index, :, :, batch].reshape(KB, 128)
            marks = km[pl.ds(pl.multiple_of(index * KB, KB), KB), :]
            both, more = terms(rows, nn(jnp.concatenate([rows, marks], axis=1), marked))
            kvb[index, :, :, batch] = both.reshape(4, 4, T, 128)
            return sums + more

        sums = lax.fori_loop(0, steps, step, sums)

        def clear(index, nothing):
            kvb[index, :, :, batch] = jnp.zeros((4, 4, T, 128), jnp.bfloat16)
            return nothing

        lax.fori_loop(steps, 4, clear, 0)
        kvb[here + (batch,)] = own_both
        dqk[pl.ds(batch * T, T), :] = to_rows(sums[:64, :] * 0.125)

    def back_project(layer):
        key_grads = own[...].reshape(R, 128)
        whole = jnp.concatenate([key_grads[:, :64], dqk[:, 64:]], axis=1)
        turned = turn(whole, tiled(cosine[...]), -tiled(sine[...])).astype(jnp.bfloat16)
        values = jnp.concatenate(
            [key_grads[:, 64:], jnp.zeros((R, QS - 64), jnp.float32)], axis=1
        ).astype(jnp.bfloat16)
        low[layer] = turned
        vlow[layer] = values
        small[layer][2] = jnp.concatenate(
            [
                jnp.sum(turned.astype(jnp.float32), axis=0, keepdims=True),
                jnp.sum(values.astype(jnp.float32), axis=0, keepdims=True),
            ],
            axis=1,
        )
        mine[1] = nt(turned, wat[:, :, :, :, :QS].reshape(DP, QS)) + nt(
            values, wat[:, :, :, :, QS:].reshape(DP, QS)
        )
        one = swap(1)
        one.start()
        one.wait()
        rows = (ends[0] if layer == 0 else xs_[0]).astype(jnp.float32)
        back, gain_row = norm_back(mine[1] + theirs[1], rows, gains[layer, 2:3, :])
        small[layer][0] = gain_row
        small[layer][3] = jnp.concatenate(
            [squares[layer, 0:1, :], jnp.zeros((1, DP - 128), jnp.float32)], axis=1
        )
        result = (dmid[...] + back).astype(jnp.bfloat16)
        if layer == 0:
            dx[...] = result
        else:
            dout[...] = result.astype(jnp.float32)

    def heads_products(layer):
        first = tn(n1[layer], low[layer])
        second = tn(n1[layer], vlow[layer]) + tn(da[layer], att[layer])
        for side, product in enumerate((first, second)):
            for part in range(2):
                pool[4 * layer + 2 * side + part] = (
                    product[:, part * SLOT : (part + 1) * SLOT]
                    .astype(jnp.bfloat16)
                    .reshape(4, 4, 4, 16, SLOT)
                )

    def total(terms):
        return sum(term[...].astype(jnp.float32) for term in terms)

    def key_final(j, *terms):
        own[j] = total(terms)

    key_halves = [lambda j, k, ref=ref: ref.at[j, k] for ref in (kh0,)]
    key_wholes = [lambda j, k, ref=ref: ref.at[j, k] for ref in (kw0, kw1, kw2)]
    keys = [
        scatter_stages(
            token_view(kvb), key_halves, key_wholes, place, ks.at[layer], kr.at[layer], key_final
        )
        for layer in range(2)
    ]

    def feed_final(layer):
        def final(j, *terms):
            outv[layer, :, pl.ds(j * FFH, FFH)] = total(terms)

        return final

    def lanes(ref, size):
        return lambda j, k: ref.at[
            (j, k) + (slice(None),) * (len(ref.shape) - 3) + (pl.ds(0, size(k)),)
        ]

    inner_halves = [None, lanes(mh1, lambda k: half_of(FFH, k)[1])]
    inner_wholes = [None] + [lanes(ref, lambda k: FFH) for ref in (mw1, mw2)]
    feed = [
        LargeScatter(
            grads.at[layer], slab, got_half, got_whole, spare, inner_halves, inner_wholes, place,
            (hs.at[layer], hr.at[layer]), (os_.at[layer], or_.at[layer]),
            (ws.at[layer], wr.at[layer]), ls.at[layer], ms.at[layer], mr.at[layer],
            feed_final(layer),
        )
        for layer in range(2)
    ]
    late, early = feed

    def slots(ref):
        return lambda j, k: ref.at[j, k, pl.ds(0, A_SLOTS[j][1])]

    def heads_final(j, *terms):
        begin, count = A_SLOTS[j]
        for index in range(count):
            layer, spot = divmod(begin + index, 4)
            outv[layer, :, pl.ds(CM + spot * SLOT, SLOT)] = total(
                [term.at[index] for term in terms]
            )

    heads = scatter_stages(
        slot_view(pool), [slots(ah0)],
        [slots(ref) for ref in (aw0, aw1, aw2)], place, as_, ar, heads_final,
    )

    def total_small(phase, axis):
        copies = [
            send(
                sbuf.at[4 * phase],
                sbuf.at[4 * phase + k],
                bs.at[phase, k - 1],
                br.at[phase, k - 1],
                chip_id(moved(place, axis, distance)),
            )
            for k, distance in ((1, 1), (2, -1), (3, 2))
        ]

        def begin():
            for one in copies:
                one.start()

        def end():
            for one in copies:
                one.wait()
            total = (
                sbuf[4 * phase] + sbuf[4 * phase + 1] + sbuf[4 * phase + 2] + sbuf[4 * phase + 3]
            )
            if phase < 2:
                sbuf[4 * phase + 4] = total
            else:
                small_out[...] = total

        return begin, end

    def beside(stages, rounds):
        rounds = iter(rounds)
        for index in range(8):
            stages[index]()
            if index not in (2, 5):
                next(rounds)()

    def calls(method, *numbers):
        return [functools.partial(method, r) for r in numbers]

    def nothing():
        pass

    def rounds_of(*methods):
        for method in methods:
            for r in range(ROUNDS):
                method(r)

    back_feed(1, {})
    rounds_of(early.ahead, early.rest)
    for batch in range(MB):
        back_attend(1, batch)
    for stage in keys[1][:8]:
        stage()
    rounds_of(early.pass_on)
    keys[1][8]()
    keys[1][9]()
    keys_load(0).start()
    back_project(1)
    heads_load(0).start()
    back_feed(
        0,
        {
            2: lambda: (early.third(), early.phases[0]()),
            4: early.phases[1],
            6: lambda: (early.phases[2](), early.phases[3]()),
            9: early.phases[5],
        },
    )
    early.finish()
    for axis in "xyz":
        for distance in (1, -1, 2):
            pl.semaphore_signal(
                credit, inc=1, device_id=chip_id(moved(place, axis, distance)), device_id_type=MESH
            )
    pl.semaphore_wait(credit, 9)
    rounds_of(late.ahead)
    back_attend(0, 0)
    late.pass_on(0)
    late.pass_on(1)
    back_attend(0, 1)
    late.pass_on(2)
    late.pass_on(3)
    late.rest(0)
    back_attend(0, 2)
    beside(
        keys[0],
        [nothing, *calls(late.rest, 1, 2, 3), functools.partial(heads_products, 1), nothing],
    )
    keys[0][8]()
    keys[0][9]()
    late.third()
    late.phases[0]()
    back_project(0)
    heads_products(0)
    sbuf[0] = jnp.concatenate(small[0] + small[1], axis=0)
    sums = [total_small(phase, axis) for phase, axis in enumerate("xyz")]
    sums[0][0]()
    heads[0]()
    late.phases[1]()
    sums[0][1]()
    sums[1][0]()
    heads[1]()
    late.phases[2]()
    late.phases[3]()
    heads[2]()
    heads[3]()
    sums[1][1]()
    sums[2][0]()
    late.phases[5]()
    heads[5]()
    heads[6]()
    sums[2][1]()
    heads[8]()
    for layer in range(2):
        outv[layer, 14:15, pl.ds(CM, CA)] = small_out[4 * layer + 2 : 4 * layer + 3, :]
    trade = send(outv.at[1 - core], other, fs, fr, other_core())
    trade.start()
    late.finish()
    heads[9]()
    trade.wait()


def backward(*arrays):
    low, full = jnp.bfloat16, jnp.float32
    half = FFH - FFH // 256 * 128

    def ring(last, phase, count=2):
        return pltpu.VMEM((3, count) + last[:-2] + (4,) * (2 - phase) + last[-2:], low)

    return pl.pallas_call(
        backward_kernel,
        out_shape=(
            shape((2, 4, 4, 4, 16, CM), low),
            shape((R, DP), low),
            shape((2, 16, C), full),
            shape((16, C), full),
            shape((8, DP), full),
        ),
        in_specs=[ANY] * 4 + [VMEM] * 16,
        out_specs=(ANY,) + (VMEM,) * 4,
        scratch_shapes=[
            pltpu.VMEM((12, 4, 4, 4, 16, SLOT), low),
            pltpu.VMEM((2, 2, R, SLOT), full),
            pltpu.VMEM((DP, R), low),
            pltpu.VMEM((DP, R), low),
            pltpu.VMEM((4, 4, 4, 16, CA), low),
            pltpu.VMEM((2, R, DP), full),
            pltpu.VMEM((2, R, DP), full),
            pltpu.VMEM((R, DP), full),
            pltpu.VMEM((R, DP), full),
            pltpu.VMEM((2, R, DP), low),
            pltpu.VMEM((MB, 128, QS), low),
            pltpu.VMEM((R, QS), full),
            pltpu.VMEM((2, R, QS), low),
            pltpu.VMEM((2, R, QS), low),
            pltpu.VMEM((4, 4, 4, MB, T, 128), low),
            pltpu.VMEM((MB, T, 128), full),
        ]
        + [
            ring((T // 2, 128), 0),
            ring((T, 128), 0),
            ring((T, 128), 1, 3),
            ring((T, 128), 2, 3),
            pltpu.VMEM((3, 4, 4, 16, FFH), low),
            ring((16, half), 0),
            ring((16, FFH), 0),
            ring((16, 384), 0),
            ring((16, half), 1),
            ring((16, FFH), 1),
            ring((16, FFH), 2, 3),
            ring((3, 16, 128), 0),
            ring((3, 16, SLOT), 0),
            ring((3, 16, SLOT), 1, 3),
            ring((3, 16, SLOT), 2, 3),
        ]
        + [
            pltpu.VMEM((12, 8, DP), full),
            DMA((4,)),
            DMA((2, 3)),
            DMA((2, 3)),
            DMA((2, 2)),
            DMA((2,)),
            DMA((2,)),
            DMA((2, 3, 3, 4)),
            DMA((2, 3, 3, 4)),
            DMA((2, 3, 2, ROUNDS)),
            DMA((2, 3, 2, ROUNDS)),
            DMA((2, 3, 2, ROUNDS)),
            DMA((2, 3, 2, ROUNDS)),
            DMA((2, 3, 2, ROUNDS)),
            DMA((2, 3, 2, ROUNDS)),
            DMA((2, 9)),
            DMA((2, 3, 3, 4)),
            DMA((2, 3, 3, 4)),
            DMA((3, 3, 4)),
            DMA((3, 3, 4)),
            DMA((3, 3)),
            DMA((3, 3)),
            DMA,
            DMA,
            pltpu.SemaphoreType.REGULAR,
        ],
        compiler_params=params(1, vmem=63),
        name="backward",
    )(*arrays)


def assemble_kernel(
    kept, other, dx, xs_, sums, valid, boundary, grad_qkv, grad_bias, grad_out, grad_gu, grad_down,
    grad_gain, rms,
):
    core = lax.axis_index("section")
    own, far = jnp.where(core == 0, kept[0], kept[1]), other[...]
    sides = (jnp.where(core == 0, own, far), jnp.where(core == 0, far, own))

    def column(start, size):
        return [side[:, start : start + size] for side in sides]

    qkv = jnp.concatenate(column(CM + 64, 448) + column(CM, 64) + column(CM + QS, 64), axis=1)
    out = jnp.concatenate(column(CM + QS + 64, 448), axis=1)
    gate_up = jnp.concatenate(column(0, FFH) + column(FFH, FFH), axis=1)
    down = jnp.concatenate(column(2 * FFH, FFH), axis=1)
    for row in range(14):
        grad_qkv[row] = qkv[row : row + 1, :]
        grad_out[row] = out[row : row + 1, :]
        grad_gu[row] = gate_up[row : row + 1, :]
        grad_down[row] = down[row : row + 1, :]
    rows = [side[14:15, CM:] for side in sides]
    grad_bias[...] = jnp.concatenate(
        [row[:, 64:QS] for row in rows]
        + [row[:, :64] for row in rows]
        + [row[:, QS : QS + 64] for row in rows],
        axis=1,
    )
    mine = jnp.where(core == 0, sums[0:4, :], sums[4:8, :])
    rest = jnp.concatenate([mine, jnp.zeros((12, DP), jnp.float32)], axis=0)
    terms = []
    for _ in range(3):
        term = rest.astype(jnp.bfloat16)
        rest = rest - term.astype(jnp.float32)
        terms.append(term)
    result = jnp.where(core == 0, dx[...].astype(jnp.float32), xs_[1].astype(jnp.float32))
    narrow = nt(
        jnp.concatenate([result.astype(jnp.bfloat16)] + terms, axis=0), spread_matrix()
    )
    boundary[...] = narrow[:R].astype(jnp.bfloat16)
    grad_gain[...] = narrow[R : R + 2] + narrow[R + 16 : R + 18] + narrow[R + 32 : R + 34]
    for batch in range(MB):
        count = jnp.sum(valid[batch : batch + 1, :].astype(jnp.float32), axis=1, keepdims=True)
        rms[batch] = jnp.sqrt(mine[3:4, 3 * batch : 3 * batch + 3] / (count * float(BLOCK * D)))


def assemble(*arrays):
    full = jnp.float32
    return pl.pallas_call(
        assemble_kernel,
        out_shape=(
            shape((R, D), jnp.bfloat16),
            shape((14, 1, D + 256), full),
            shape((1, D + 256), full),
            shape((14, 1, D), full),
            shape((14, 1, 4 * FFH), full),
            shape((14, 1, 2 * FFH), full),
            shape((2, D), full),
            shape((MB, 1, MB), full),
        ),
        in_specs=[VMEM] * 6,
        out_specs=(VMEM,) * 8,
        compiler_params=params(),
        name="assemble",
    )(*arrays)


def shards(
    ends,
    segment_ids,
    valid_blocks,
    qkv_weight,
    qkv_bias,
    out_weight,
    gate_up_weight,
    down_weight,
    norm_gains,
):
    chip = lax.axis_index("dp")
    places = chip * T + jnp.arange(T, dtype=jnp.int32)
    frequency = THETA ** (-(jnp.arange(128) % 32).astype(jnp.float32) * 2.0 / 64)
    sign = jnp.where(jnp.arange(128) % 64 < 32, -1.0, 1.0)
    angles = places.astype(jnp.float32)[:, None] * frequency[None, :]
    cosine = jnp.cos(angles)
    sine = jnp.sin(angles) * sign[None, :]

    (
        wa, wm, kv, gu, ends_all, gains, n1, qt, mixed, lse, att, mid, n2, _, xs_, sq, km, qm, ob,
    ) = forward(
        gate_up_weight[0],
        down_weight[0],
        qkv_weight[0],
        out_weight[0],
        qkv_bias,
        norm_gains[0],
        ends.reshape(R, D),
        segment_ids,
        valid_blocks,
        cosine,
        sine,
    )
    _, dx, kept, other, sums = backward(
        wa, wm, kv, gu, ends_all, xs_, gains, n1, qt, mixed, lse, att, mid, n2, sq, cosine, sine,
        km, qm, ob,
    )
    boundary, *grads, rms = assemble(kept, other, dx, xs_, sums, valid_blocks)
    grad_qkv, grad_bias, grad_out, grad_gu, grad_down, grad_gain = grads
    return (
        boundary.reshape(1, MB, T, D),
        grad_qkv.transpose(1, 0, 2),
        grad_bias,
        grad_out.transpose(1, 0, 2),
        grad_gu.transpose(1, 0, 2),
        grad_down.transpose(1, 0, 2),
        grad_gain[None],
        rms.transpose(1, 0, 2),
    )


def solution(mesh):
    in_specs = (
        P("section", None, "dp", None),
        P(),
        P(),
        P("section", "dp", None),
        P("section", None),
        P("section", "dp", None),
        P("section", "dp", None),
        P("section", "dp", None),
        P("section", None, None),
    )
    out_specs = (
        P("section", None, "dp", None),
        P("section", "dp", None),
        P("section", None),
        P("section", "dp", None),
        P("section", "dp", None),
        P("section", "dp", None),
        P("section", None, None),
        P("section", None, None),
    )
    return jax.shard_map(shards, mesh=mesh, in_specs=in_specs, out_specs=out_specs, check_vma=False)
```

```python
import functools
import math

import jax
import jax.numpy as jnp
from jax import lax
from jax.experimental import pallas as pl
from jax.experimental.pallas import tpu as pltpu
from jax.sharding import PartitionSpec as P

MESH = pl.DeviceIdType.MESH
EPS = 1e-06
THETA = 1000000.0
MASKED = -1e30

MB = 3
T = 64
R = MB * T
D = 896
DP = 1024
FFH = 2432
QS = 512
C_UP, C_DOWN, C_QK, C_VO, C = FFH, 2 * FFH, 3 * FFH, 3 * FFH + QS, 3 * FFH + 2 * QS
KB = 1024
SEQ = 4096
MIB = 1024 * 1024

BLOCK = 128

THIRDS = ((0, 22 * 128), (22 * 128, 22 * 128), (44 * 128, 21 * 128))
ORDERS = (("z", "y", "x"), ("y", "x", "z"), ("x", "z", "y"))
CM, CA = 3 * FFH, 2 * QS
M_THIRDS = ((0, FFH), (FFH, FFH), (2 * FFH, FFH))
A_THIRDS = ((0, 384), (384, 384), (768, 256))
FF_CHUNKS = ((0, 512), (512, 512), (1024, 512), (1536, 512), (2048, 384))


def position():
    chip = lax.axis_index("dp")
    return {"x": chip // 16, "y": (chip // 4) % 4, "z": chip % 4}


def moved(place, axis, distance):
    other = dict(place)
    other[axis] = (place[axis] + distance + 4) % 4
    return other


def chip_id(place):
    return {"dp": place["x"] * 16 + place["y"] * 4 + place["z"]}


def other_core():
    return {"section": 1 - lax.axis_index("section")}


def greet(place, core=False, chips=True, far=False):
    barrier = pltpu.get_barrier_semaphore()
    count = 0
    if chips:
        for axis in "xyz":
            for distance in (1, -1, 2) if far else (1, -1):
                pl.semaphore_signal(
                    barrier,
                    inc=1,
                    device_id=chip_id(moved(place, axis, distance)),
                    device_id_type=MESH,
                )
                count += 1
    if core:
        pl.semaphore_signal(barrier, inc=1, device_id=other_core(), device_id_type=MESH)
        count += 1
    return count


def settle(count):
    pl.semaphore_wait(pltpu.get_barrier_semaphore(), count)


def send(src, dst, send_sem, recv_sem, device):
    return pltpu.make_async_remote_copy(
        src, dst, send_sem, recv_sem, device_id=device, device_id_type=MESH
    )


def cube(done, place):
    return tuple(slice(None) if axis in done else place[axis] for axis in "xyz")


DIRECT = ((0, 1), (1, -1), (2, 2))


def gather_stages(view, place, send_sems, recv_sems, direct=(0, 1)):
    pending = []

    def copy(j, phase, k, whose, part, distance):
        ref = view(cube(ORDERS[j][:phase], whose), j, part)
        return send(
            ref,
            ref,
            send_sems.at[j, phase, k],
            recv_sems.at[j, phase, k],
            chip_id(moved(place, ORDERS[j][phase], distance)),
        )

    def first(phase):
        for j in range(3):
            for k, distance in DIRECT if phase in direct else DIRECT[:2]:
                one = copy(j, phase, k, place, None, distance)
                one.start()
                pending.append(one)

    def second(phase):
        if phase in direct:
            return
        for j in range(3):
            for k, distance in DIRECT[:2]:
                whose = moved(place, ORDERS[j][phase], -distance)
                copy(j, phase, k, whose, None, distance).wait_recv()
                one = copy(j, phase, 2 + k, whose, k, distance)
                one.start()
                pending.append(one)

    def third(phase):
        for j in range(3):
            if phase in direct:
                for k, distance in DIRECT:
                    whose = moved(place, ORDERS[j][phase], -distance)
                    copy(j, phase, k, whose, None, distance).wait_recv()
            else:
                for k, distance in DIRECT[:2]:
                    whose = moved(place, ORDERS[j][phase], 2)
                    copy(j, phase, 2 + k, whose, k, distance).wait_recv()

    def finish():
        for one in pending:
            one.wait_send()

    stages = []
    for phase in range(3):
        stages.append(functools.partial(first, phase))
        stages.append(functools.partial(second, phase))
        stages.append(functools.partial(third, phase))
    stages.append(finish)
    return stages


PARTS = (
    ((0, 256), (256, 256), (512, 256), (768, 384)),
    ((1152, 256), (1408, 256), (1664, 384), (2048, 384)),
)
ROUNDS = 4
TURNS = tuple((j, k, (1, -1)[k]) for j in range(3) for k in range(2))


class LargeGather:
    def __init__(self, ref, place, send_sems, recv_sems, part_sems, pass_sems):
        self.ref, self.place = ref, place
        self.part_sems, self.pass_sems = part_sems, pass_sems
        stages = gather_stages(
            weight_view(ref, M_THIRDS), place, send_sems, recv_sems, direct=(0,)
        )
        self.phases, self.done = stages[:6], stages[9]
        self.pending = []

    def slab(self, j, whose, half, r):
        start, size = PARTS[half][r]
        chips = cube(ORDERS[j][:2], whose)
        return self.ref.at[chips + (slice(None), pl.ds(j * FFH + start, size))]

    def whose(self, j, distance):
        return moved(self.place, ORDERS[j][2], distance)

    def part(self, j, k, distance, half, r, whose):
        ref = self.slab(j, whose, half, r)
        sems = [side.at[j, k, half, r] for side in self.part_sems]
        return send(ref, ref, *sems, chip_id(self.whose(j, distance)))

    def passed(self, j, k, distance, r, whose):
        ref = self.slab(j, whose, k, r)
        sems = [side.at[j, k, r] for side in self.pass_sems]
        return send(ref, ref, *sems, chip_id(self.whose(j, distance)))

    def start(self, one):
        one.start()
        self.pending.append(one)

    def ahead(self, r):
        for j, k, distance in TURNS:
            self.start(self.part(j, k, distance, k, r, self.place))

    def rest(self, r):
        for j, k, distance in TURNS:
            self.start(self.part(j, k, distance, 1 - k, r, self.place))

    def pass_on(self, r):
        for j, k, distance in TURNS:
            back = self.whose(j, -distance)
            self.part(j, k, distance, k, r, back).wait_recv()
            self.start(self.passed(j, k, distance, r, back))

    def last(self):
        for j, k, distance in TURNS:
            for r in range(ROUNDS):
                self.part(j, k, distance, 1 - k, r, self.whose(j, -distance)).wait_recv()
                self.passed(j, k, distance, r, self.whose(j, 2)).wait_recv()

    def finish(self):
        self.done()
        for one in self.pending:
            one.wait_send()


def scatter_stages(
    view, halves, wholes, place, send_sems, recv_sems, final, begin=0, direct=(1, 2)
):
    pending = []

    def half_copy(j, phase, k, distance):
        far = moved(place, back_axis(j, phase), 2)
        return send(
            view(back_chips(j, phase, far), j, k),
            halves[phase](j, k),
            send_sems.at[j, phase, k],
            recv_sems.at[j, phase, k],
            chip_id(moved(place, back_axis(j, phase), distance)),
        )

    def whole_copy(j, phase, k, distance):
        near = moved(place, back_axis(j, phase), distance)
        slot = k if phase in direct else 2 + k
        return send(
            view(back_chips(j, phase, near), j, None),
            wholes[phase](j, k),
            send_sems.at[j, phase, slot],
            recv_sems.at[j, phase, slot],
            chip_id(near),
        )

    def first(phase):
        for j in range(3):
            for k, distance in DIRECT if phase in direct else DIRECT[:2]:
                one = (whole_copy if phase in direct else half_copy)(j, phase, k, distance)
                one.start()
                pending.append(one)

    def second(phase):
        if phase in direct:
            return
        for j in range(3):
            for k, distance in DIRECT[:2]:
                half_copy(j, phase, k, distance).wait_recv()
                near = moved(place, back_axis(j, phase), distance)
                mine = view(back_chips(j, phase, near), j, k)
                add(mine, mine, halves[phase](j, k))
                one = whole_copy(j, phase, k, distance)
                one.start()
                pending.append(one)

    def third(phase):
        turns = DIRECT if phase in direct else DIRECT[:2]
        for j in range(3):
            for k, distance in turns:
                whole_copy(j, phase, k, distance).wait_recv()
            mine = view(back_chips(j, phase, place), j, None)
            terms = [wholes[phase](j, k) for k, distance in turns]
            if phase < 2:
                add(mine, mine, *terms)
            else:
                final(j, mine, *terms)

    def finish():
        for one in pending:
            one.wait_send()

    stages = []
    for phase in range(begin, 3):
        stages.append(functools.partial(first, phase))
        stages.append(functools.partial(second, phase))
        stages.append(functools.partial(third, phase))
    stages.append(finish)
    return stages


def back_axis(j, phase):
    return ORDERS[j][2 - phase]


def back_chips(j, phase, whose):
    return cube(ORDERS[j][: 2 - phase], whose)


def add(dst, *terms):
    dst[...] = sum(term[...].astype(jnp.float32) for term in terms).astype(dst.dtype)


def half_of(size, part):
    half = size // 256 * 128
    return (0, half) if part == 0 else (half, size - half)


class LargeScatter:
    def __init__(
        self, source, slab, got_half, got_whole, spare, inner_halves, inner_wholes, place,
        half_sems, rest_sems, pass_sems, load_sems, send_sems, recv_sems, final,
    ):
        self.source, self.slab, self.place = source, slab, place
        self.got_half, self.got_whole, self.spare = got_half, got_whole, spare
        self.half_sems, self.rest_sems, self.pass_sems = half_sems, rest_sems, pass_sems
        self.load_sems = load_sems
        self.pending = []

        def view(chips, j, part):
            rest = tuple(index for axis, index in zip("xyz", chips) if axis != back_axis(j, 0))
            cols = slice(None) if part is None else pl.ds(*half_of(FFH, part))
            return slab.at[(j,) + rest + (slice(None), cols)]

        stages = scatter_stages(
            view, inner_halves, inner_wholes, place, send_sems, recv_sems, final, begin=1, direct=(2,)
        )
        self.phases, self.done = stages[:-1], stages[-1]

    def terms(self, j, whose, cols):
        chips = back_chips(j, 0, whose)
        return self.source.at[chips + (slice(None), pl.ds(j * FFH + cols[0], cols[1]))]

    def near(self, j, distance):
        return moved(self.place, back_axis(j, 0), distance)

    def half_ref(self, j, k, r):
        start, size = PARTS[k][r]
        return self.got_half.at[j, k, :, :, :, pl.ds(start - PARTS[k][0][0], size)]

    def copy(self, src, dst, sems, j, k, distance, r):
        return send(
            src, dst, sems[0].at[j, k, r], sems[1].at[j, k, r], chip_id(self.near(j, distance))
        )

    def half_copy(self, j, k, distance, r):
        src = self.terms(j, self.near(j, 2), PARTS[k][r])
        return self.copy(src, self.half_ref(j, k, r), self.half_sems, j, k, distance, r)

    def rest_copy(self, j, k, distance, r):
        cols = PARTS[1 - k][r]
        src = self.terms(j, self.near(j, distance), cols)
        dst = self.got_whole.at[j, k, :, :, :, pl.ds(*cols)]
        return self.copy(src, dst, self.rest_sems, j, k, distance, r)

    def pass_copy(self, j, k, distance, r):
        dst = self.got_whole.at[j, k, :, :, :, pl.ds(*PARTS[k][r])]
        return self.copy(self.half_ref(j, k, r), dst, self.pass_sems, j, k, distance, r)

    def own_load(self, j, k, distance, r):
        return pltpu.make_async_copy(
            self.terms(j, self.near(j, distance), PARTS[k][r]),
            self.spare.at[j, k, :, :, :, pl.ds(0, PARTS[k][r][1])],
            self.load_sems.at[2 * j + k],
        )

    def slab_load(self, j):
        return pltpu.make_async_copy(
            self.terms(j, self.place, (0, FFH)), self.slab.at[j], self.load_sems.at[6 + j]
        )

    def start(self, one):
        one.start()
        self.pending.append(one)

    def group(self, half, r):
        for j in range(3):
            self.start(self.half_copy(j, half, (1, -1)[half], r))
            self.start(self.rest_copy(j, 1 - half, (1, -1)[1 - half], r))

    def load(self):
        for j, k, distance in TURNS:
            self.own_load(j, k, distance, 0).start()
        for j in range(3):
            self.slab_load(j).start()

    def pass_on(self, r):
        for j, k, distance in TURNS:
            self.half_copy(j, k, distance, r).wait_recv()
            self.own_load(j, k, distance, r).wait()
            own = self.spare.at[j, k, :, :, :, pl.ds(0, PARTS[k][r][1])]
            add(self.half_ref(j, k, r), self.half_ref(j, k, r), own)
            self.start(self.pass_copy(j, k, distance, r))
            if r + 1 < ROUNDS:
                self.own_load(j, k, distance, r + 1).start()

    def third(self):
        for j in range(3):
            self.slab_load(j).wait()
            for k in range(2):
                for r in range(ROUNDS):
                    self.rest_copy(j, k, (1, -1)[k], r).wait_recv()
                    self.pass_copy(j, k, (1, -1)[k], r).wait_recv()
            add(self.slab.at[j], self.slab.at[j], self.got_whole.at[j, 0], self.got_whole.at[j, 1])

    def finish(self):
        self.done()
        for one in self.pending:
            one.wait_send()


def weight_view(ref, thirds=THIRDS):
    def view(chips, j, part):
        start, size = thirds[j]
        if part is not None:
            half = size // 256 * 128
            start, size = (start, half) if part == 0 else (start + half, size - half)
        return ref.at[tuple(chips) + (slice(None), pl.ds(start, size))]

    return view


def token_view(ref):
    def view(chips, j, part):
        rows = slice(None) if part is None else pl.ds(part * 32, 32)
        return ref.at[tuple(chips) + (j, rows, slice(None))]

    return view


def params(collective_id=None, vmem=56):
    if collective_id is None:
        return pltpu.CompilerParams(vmem_limit_bytes=vmem * MIB)
    return pltpu.CompilerParams(
        collective_id=collective_id, has_side_effects=True, vmem_limit_bytes=vmem * MIB
    )


ANY = pl.BlockSpec(memory_space=pl.ANY)
VMEM = pl.BlockSpec(memory_space=pltpu.VMEM)
SMEM = pl.BlockSpec(memory_space=pltpu.SMEM)
DMA = pltpu.SemaphoreType.DMA


def shape(dims, dtype):
    return jax.ShapeDtypeStruct(dims, dtype)


def nn(left, right):
    return jnp.dot(left, right, preferred_element_type=jnp.float32)


def nt(left, right):
    return lax.dot_general(
        left, right, (((1,), (1,)), ((), ())), preferred_element_type=jnp.float32
    )


def tn(left, right):
    return lax.dot_general(
        left, right, (((0,), (0,)), ((), ())), preferred_element_type=jnp.float32
    )


DEAD = 4


def key_marks(segments, lengths, chip):
    rows = lax.broadcasted_iota(jnp.int32, (8, SEQ), 0)
    keys = lax.broadcasted_iota(jnp.int32, (8, SEQ), 1)
    groups = []
    for batch in range(MB):
        same = (rows < DEAD) & (segments[batch : batch + 1, :] == rows)
        dead = (keys >= chip * T) | (keys.astype(jnp.float32) >= lengths[batch])
        groups.append(jnp.where(same | ((rows == DEAD) & dead), 1.0, 0.0))
    groups.append(jnp.zeros((128 - 8 * MB, SEQ), jnp.float32))
    marks = jnp.concatenate(groups, axis=0).T.astype(jnp.bfloat16)
    return marks.reshape(4, 4, 4, T, 128)


def query_marks(ids, batch, dead):
    place = lax.broadcasted_iota(jnp.int32, (128, 128), 0) - 8 * batch
    hit = (place >= 0) & (place < DEAD) & (place != ids)
    if dead:
        hit = hit | (place == DEAD)
    return jnp.where(hit, MASKED, 0.0).astype(jnp.bfloat16)


def own_bias(full):
    key = lax.broadcasted_iota(jnp.int32, (T, 128), 0)
    query = lax.broadcasted_iota(jnp.int32, (T, 128), 1) % T
    allowed = (key == query) | ((key <= query) & (full > 0.0))
    return jnp.where(allowed, 0.0, MASKED)


def all_heads(two):
    return jnp.concatenate([two] * 4, axis=1)


def mean_of(values):
    return jnp.sum(values, axis=-1, keepdims=True) * (1.0 / D)


def turn(values, cosine, sine):
    width = values.shape[1]
    lane = lax.broadcasted_iota(jnp.int32, values.shape, 1) % 64
    swapped = jnp.where(lane < 32, pltpu.roll(values, width - 32, 1), pltpu.roll(values, 32, 1))
    return values * cosine + swapped * sine


def tiled(table, columns=QS):
    wide = jnp.concatenate([table] * (columns // 128), axis=1)
    return jnp.concatenate([wide] * MB, axis=0)


def plane(batch, index):
    return tuple(index if axis == ORDERS[batch][2] else slice(None) for axis in "xyz")


def to_columns(rows):
    turned = rows.T
    return jnp.concatenate([turned[64 * h : 64 * h + 64] for h in range(8)], axis=1)


def to_rows(columns):
    pairs = []
    for pair in range(4):
        turned = columns[:, 128 * pair : 128 * pair + 128].T
        pairs.append(jnp.concatenate([turned[:64], turned[64:]], axis=1))
    return jnp.concatenate(pairs, axis=1)


def without_first_slot(rows):
    lane = lax.broadcasted_iota(jnp.int32, rows.shape, 1)
    return jnp.where(lane < 64, 0.0, rows)


def spread_matrix():
    row = lax.broadcasted_iota(jnp.int32, (D, DP), 0)
    column = lax.broadcasted_iota(jnp.int32, (1, DP), 1)
    spot = column % 16
    target = jnp.where(spot < 14, column // 16 * 14 + spot, -1)
    return jnp.where(row == target, 1.0, 0.0).astype(jnp.bfloat16)


def forward_kernel(
    gate_up, down, qkv, out_w, bias_in, gains_in, ends, segments, valid, cosine, sine,
    wa, wm, kv, gu, cot, gains, n1, qt, mixed, lse, att, mid, n2, hid, xs_, sq, km, qm, ob,
    ends_v, small_v, give_a, give_m, stage_a, stage_m, wat, wml, kvb, gu_v, mine, theirs,
    state, acc, lsem, ssem, rsem, a_s, a_r, m_s, m_r, mp_s, mp_r, mq_s, mq_r, k_s, k_r, osem, wsem, xsem,
    xrsem,
):
    place = position()
    core = lax.axis_index("section")
    chip = lax.axis_index("dp")
    here = (place["x"], place["y"], place["z"])
    partners = greet(place, core=True, far=True)

    def heads_half(half):
        wide = qkv[...].astype(jnp.float32)
        outs_ = out_w[...].astype(jnp.float32)
        return jnp.concatenate(
            [
                wide[:, D + 64 * half : D + 64 * half + 64],
                wide[:, 448 * half : 448 * half + 448],
                wide[:, D + 128 + 64 * half : D + 192 + 64 * half],
                outs_[:, 448 * half : 448 * half + 448],
            ],
            axis=1,
        )

    def bias_half(half):
        wide = bias_in[...].astype(jnp.float32)
        return jnp.concatenate(
            [
                wide[:, D + 64 * half : D + 64 * half + 64],
                wide[:, 448 * half : 448 * half + 448],
                wide[:, D + 128 + 64 * half : D + 192 + 64 * half],
                jnp.zeros((1, 448), jnp.float32),
            ],
            axis=1,
        )

    halves = [heads_half(0), heads_half(1)]
    for dst, side in ((stage_a.at[core], 0), (give_a, 1)):
        dst[...] = jnp.zeros((16, CA), jnp.bfloat16)
        dst[0:14, :] = jnp.where(core == side, halves[0], halves[1]).astype(jnp.bfloat16)
    for dst, index in ((stage_m.at[core], core), (give_m, 1 - core)):
        dst[...] = jnp.zeros((16, CM), jnp.bfloat16)
        start = pl.multiple_of(index * FFH, 128)
        dst[0:14, 0:FFH] = gate_up[:, pl.ds(start, FFH)]
        dst[0:14, FFH : 2 * FFH] = gate_up[:, pl.ds(pl.multiple_of(start + 2 * FFH, 128), FFH)]
        dst[0:14, 2 * FFH : CM] = down[:, pl.ds(start, FFH)]
    settle(partners)

    trades = []

    def trade(index, give, dst):
        out = send(give, dst.at[core], ssem.at[index], rsem.at[index], other_core())
        back = send(give, dst.at[1 - core], ssem.at[index], rsem.at[index], other_core())
        out.start()
        trades.append((out, back))

    trade(0, give_a, stage_a)
    trade(1, give_m, stage_m)

    def arrive(index):
        out, back = trades[index]
        back.wait_recv()
        out.wait_send()

    arrive(0)
    into = [
        pltpu.make_async_copy(stage_a.at[layer], wat.at[(layer,) + here], lsem.at[layer])
        for layer in range(2)
    ]
    for one in into:
        one.start()
    for one in into:
        one.wait()
    attn = [
        gather_stages(weight_view(wat.at[layer], A_THIRDS), place, a_s.at[layer], a_r.at[layer])
        for layer in range(2)
    ]
    feed = [
        LargeGather(
            ref,
            place,
            m_s.at[layer],
            m_r.at[layer],
            (mp_s.at[layer], mp_r.at[layer]),
            (mq_s.at[layer], mq_r.at[layer]),
        )
        for layer, ref in enumerate((wml, wm.at[1]))
    ]
    early, late = feed
    keys = [
        gather_stages(token_view(kvb.at[layer]), place, k_s.at[layer], k_r.at[layer])
        for layer in range(2)
    ]
    attn[0][0]()
    attn[1][0]()
    arrive(1)
    into = [
        pltpu.make_async_copy(stage_m.at[0], wml.at[here], lsem.at[2]),
        pltpu.make_async_copy(stage_m.at[1], wm.at[(1,) + here], lsem.at[3]),
    ]
    for one in into:
        one.start()
    for one in into:
        one.wait()
    early.phases[0]()
    spread = spread_matrix()
    ends_v[core] = nn(ends[...], spread).astype(jnp.bfloat16)
    small_v[core] = jnp.zeros((8, DP), jnp.float32)
    small_v[core, 0:1, :] = bias_half(0)
    small_v[core, 1:2, :] = bias_half(1)
    small_v[core, 2:4, :] = nn(gains_in[...], spread)
    trade(2, ends_v.at[core], ends_v)
    trade(3, small_v.at[core], small_v)
    attn[0][1]()
    attn[1][1]()
    early.phases[1]()
    lengths = [
        jnp.sum(valid[batch : batch + 1, :].astype(jnp.float32), axis=1, keepdims=True) * BLOCK
        for batch in range(MB)
    ]
    km[...] = key_marks(segments, lengths, chip)
    pair = segments[:, pl.ds(pl.multiple_of(chip // 2 * 128, 128), 128)]
    ids = jnp.where(chip % 2 == 0, pair[:, :64], pair[:, 64:])
    ids = jnp.concatenate([ids, ids], axis=1)
    first_key = (chip * T).astype(jnp.float32)
    for batch in range(MB):
        for kind in range(2):
            qm[kind, batch] = query_marks(ids[batch : batch + 1, :], batch, kind == 0)
        full = jnp.where(first_key < lengths[batch], 1.0, 0.0)
        ob[batch] = own_bias(full)
    for index in range(2, 8):
        attn[0][index]()
        attn[1][index]()
    early.phases[2]()
    early.phases[3]()
    arrive(2)
    arrive(3)
    cot[...] = ends_v[...]
    gains[...] = small_v[...]
    attn[0][8]()

    outs = []

    def store(src, dst, index):
        one = pltpu.make_async_copy(src, dst, osem.at[index])
        one.start()
        outs.append(one)

    def rows_of(layer):
        return ends_v[0] if layer == 0 else xs_[0]

    def bias_of(layer):
        return jnp.where(core == 0, gains[layer, 0:1, :], gains[layer, 1:2, :])

    def project_keys(layer):
        rows = rows_of(layer).astype(jnp.float32)
        gain = gains[layer, 2:3, :]
        normed = (rows * lax.rsqrt(mean_of(rows * rows) + EPS) * gain).astype(jnp.bfloat16)
        n1[layer] = normed
        bias = bias_of(layer)
        first = nn(normed, wat[layer, :, :, :, :, 0:128].reshape(DP, 128)) + bias[:, 0:128]
        values = nn(normed, wat[layer, :, :, :, :, QS : QS + 128].reshape(DP, 128))
        values = values + bias[:, QS : QS + 128]
        turned = turn(first, tiled(cosine[...], 128), tiled(sine[...], 128))
        own = jnp.concatenate([turned[:, :64], values[:, :64]], axis=1)
        kvb[(layer,) + here] = own.astype(jnp.bfloat16).reshape(MB, T, 128)

    def project_queries(layer):
        projected = nn(n1[layer], wat[layer, :, :, :, :, 0:QS].reshape(DP, QS))
        projected = projected + bias_of(layer)[:, 0:QS]
        turned = turn(projected, tiled(cosine[...]), tiled(sine[...]))
        heads = without_first_slot(turned).astype(jnp.bfloat16).astype(jnp.float32) * 0.125
        for batch in range(MB):
            columns = to_columns(heads[batch * T : (batch + 1) * T]).astype(jnp.bfloat16)
            qt[layer, batch] = jnp.concatenate([columns, jnp.zeros_like(columns)], axis=0)

    def attend_own(layer, batch):
        queries = jnp.concatenate([qt[layer, batch], all_heads(qm[1, batch])], axis=0)
        rows = kvb[(layer,) + here + (batch,)]
        scores = nn(jnp.concatenate([rows, km[here]], axis=1), queries) + all_heads(ob[batch])
        top = jnp.max(scores, axis=0, keepdims=True)
        probs = jnp.exp(scores - top)
        state[batch, 0:1, :] = top
        state[batch, 1:2, :] = jnp.sum(probs, axis=0, keepdims=True)
        acc[batch] = tn(rows, probs.astype(jnp.bfloat16))

    def fold(layer, batch, index, carry):
        top, total, sums = carry
        queries = jnp.concatenate([qt[layer, batch], all_heads(qm[0, batch])], axis=0)
        spot = plane(batch, index)
        rows = kvb[(layer,) + spot + (batch,)].reshape(KB, 128)
        scores = nn(jnp.concatenate([rows, km[spot].reshape(KB, 128)], axis=1), queries)
        new_top = jnp.maximum(top, jnp.max(scores, axis=0, keepdims=True))
        shrink = jnp.exp(top - new_top)
        probs = jnp.exp(scores - new_top)
        total = total * shrink + jnp.sum(probs, axis=0, keepdims=True)
        return new_top, total, sums * shrink + tn(rows, probs.astype(jnp.bfloat16))

    def held(batch):
        return state[batch, 0:1, :], state[batch, 1:2, :], acc[batch]

    def attend_near(layer, batch):
        top, total, sums = fold(layer, batch, place[ORDERS[batch][2]], held(batch))
        state[batch, 0:1, :] = top
        state[batch, 1:2, :] = total
        acc[batch] = sums

    def attend_far(layer, batch):
        def step(index, carry):
            return fold(layer, batch, (place[ORDERS[batch][2]] + index) % 4, carry)

        top, total, sums = lax.fori_loop(1, 4, step, held(batch))
        result = (sums / total)[64:, :]
        mixed[layer, batch] = result
        lse[layer, batch] = jnp.broadcast_to(top + jnp.log(total), (8, QS))
        att[layer, pl.ds(batch * T, T), :] = without_first_slot(to_rows(result)).astype(
            jnp.bfloat16
        )

    def swap(slot):
        return send(mine.at[slot], theirs.at[slot], xsem.at[slot], xrsem.at[slot], other_core())

    def branch_of(layer):
        mine[0] = nt(att[layer], wat[layer, :, :, :, :, QS:].reshape(DP, QS))
        one = swap(0)
        one.start()
        one.wait()
        branch = mine[0] + theirs[0]
        middle = rows_of(layer).astype(jnp.float32) + branch
        mid[layer] = middle
        scale = lax.rsqrt(mean_of(middle * middle) + EPS)
        n2[layer] = (middle * scale * gains[layer, 3:4, :]).astype(jnp.bfloat16)
        return branch

    def feed_forward(layer, branch, hooks):
        normed = n2[layer]
        sums = jnp.zeros((R, DP), jnp.float32)
        for index, (start, size) in enumerate(FF_CHUNKS):
            hooks[index]()

            def weights(first, start=start, size=size):
                return wml[:, :, :, :, pl.ds(first + start, size)].reshape(DP, size)

            gate = nn(normed, weights(0))
            up = nn(normed, weights(FFH))
            gu_v[:, pl.ds(start, size)] = gate
            gu_v[:, pl.ds(FFH + start, size)] = up
            hidden = (gate * jax.nn.sigmoid(gate) * up).astype(jnp.bfloat16)
            hid[layer, :, pl.ds(start, size)] = hidden
            sums = sums + nt(hidden, weights(2 * FFH))
        store(gu_v, gu.at[layer], 4 + layer)
        mine[1] = sums
        one = swap(1)
        one.start()
        one.wait()
        result = mine[1] + theirs[1]
        middle = mid[layer]
        xs_[layer] = (middle + result).astype(jnp.bfloat16)
        rows = rows_of(layer).astype(jnp.float32)
        lane = lax.broadcasted_iota(jnp.int32, (8, 128), 1)
        table = jnp.zeros((8, 128), jnp.float32)
        for kind, values in enumerate((rows, branch, result)):
            squares = jnp.sum(values * values, axis=1, keepdims=True)
            for batch in range(MB):
                one = jnp.sum(squares[batch * T : (batch + 1) * T], axis=0, keepdims=True)
                one = jnp.where(first_key < lengths[batch], one, 0.0)
                table = jnp.where(lane == 3 * batch + kind, one, table)
        sq[layer] = table

    def nothing():
        pass

    def calls(method, *numbers):
        return [functools.partial(method, r) for r in numbers]

    def rounds_of(*methods):
        for method in methods:
            for r in range(ROUNDS):
                method(r)

    project_keys(0)
    keys[0][0]()
    project_queries(0)
    early.phases[4]()
    keys[0][2]()
    keys[0][3]()
    for batch in range(MB):
        attend_own(0, batch)
    early.phases[5]()
    early.ahead(0)
    keys[0][5]()
    keys[0][6]()
    early.ahead(1)
    attend_near(0, 0)
    attend_near(0, 1)
    keys[0][7]()
    early.ahead(2)
    attend_near(0, 2)
    keys[0][8]()
    early.ahead(3)
    rounds_of(early.rest)
    store(kvb.at[0], kv.at[0], 0)
    early.pass_on(0)
    attend_far(0, 0)
    early.pass_on(1)
    early.pass_on(2)
    attend_far(0, 1)
    early.pass_on(3)
    late.phases[0]()
    attend_far(0, 2)
    late.phases[1]()
    branch = branch_of(0)
    early.last()
    store(wml, wm.at[0], 2)
    late.phases[2]()
    late.phases[3]()
    feed_forward(0, branch, [nothing] * 3 + [late.phases[4], nothing])
    late.phases[5]()
    late.ahead(0)
    attn[1][8]()
    store(wat, wa, 1)
    project_keys(1)
    keys[1][0]()
    late.ahead(1)
    project_queries(1)
    keys[1][2]()
    keys[1][3]()
    late.ahead(2)
    for batch in range(MB):
        attend_own(1, batch)
    keys[1][5]()
    keys[1][6]()
    late.ahead(3)
    attend_near(1, 0)
    attend_near(1, 1)
    keys[1][7]()
    late.rest(0)
    attend_near(1, 2)
    keys[1][8]()
    late.rest(1)
    late.rest(2)
    late.rest(3)
    store(kvb.at[1], kv.at[1], 3)
    late.pass_on(0)
    attend_far(1, 0)
    late.pass_on(1)
    late.pass_on(2)
    attend_far(1, 1)
    late.pass_on(3)
    attend_far(1, 2)
    branch = branch_of(1)
    late.last()
    early.finish()
    outs[1].wait()
    outs[2].wait()
    loads = []
    for index, (start, size) in enumerate(FF_CHUNKS):
        for part in range(3):
            cols = pl.ds(part * FFH + start, size)
            loads.append(
                pltpu.make_async_copy(
                    wm.at[1, :, :, :, :, cols],
                    wml.at[:, :, :, :, cols],
                    wsem.at[3 * index + part],
                )
            )
    for one in loads:
        one.start()

    def ready(index):
        for one in loads[3 * index : 3 * index + 3]:
            one.wait()

    feed_forward(1, branch, [functools.partial(ready, index) for index in range(5)])
    for index, one in enumerate(outs):
        if index not in (1, 2):
            one.wait()
    late.finish()
    for stages in attn + keys:
        stages[9]()


def forward(*arrays):
    low, full = jnp.bfloat16, jnp.float32
    return pl.pallas_call(
        forward_kernel,
        out_shape=(
            shape((2, 4, 4, 4, 16, CA), low),
            shape((2, 4, 4, 4, 16, CM), low),
            shape((2, 4, 4, 4, MB, T, 128), low),
            shape((2, R, 2 * FFH), full),
            shape((2, R, DP), low),
            shape((2, 8, DP), full),
            shape((2, R, DP), low),
            shape((2, MB, 128, QS), low),
            shape((2, MB, 64, QS), full),
            shape((2, MB, 8, QS), full),
            shape((2, R, QS), low),
            shape((2, R, DP), full),
            shape((2, R, DP), low),
            shape((2, R, FFH), low),
            shape((2, R, DP), low),
            shape((2, 8, 128), full),
            shape((4, 4, 4, T, 128), low),
            shape((2, MB, 128, 128), low),
            shape((MB, T, 128), full),
        ),
        in_specs=[VMEM] * 11,
        out_specs=(ANY,) * 4 + (VMEM,) * 15,
        scratch_shapes=[
            pltpu.VMEM((2, R, DP), low),
            pltpu.VMEM((2, 8, DP), full),
            pltpu.VMEM((16, CA), low),
            pltpu.VMEM((16, CM), low),
            pltpu.VMEM((2, 16, CA), low),
            pltpu.VMEM((2, 16, CM), low),
            pltpu.VMEM((2, 4, 4, 4, 16, CA), low),
            pltpu.VMEM((4, 4, 4, 16, CM), low),
            pltpu.VMEM((2, 4, 4, 4, MB, T, 128), low),
            pltpu.VMEM((R, 2 * FFH), full),
            pltpu.VMEM((2, R, DP), full),
            pltpu.VMEM((2, R, DP), full),
            pltpu.VMEM((MB, 8, QS), full),
            pltpu.VMEM((MB, 128, QS), full),
            DMA((4,)),
            DMA((4,)),
            DMA((4,)),
            DMA((2, 3, 3, 4)),
            DMA((2, 3, 3, 4)),
            DMA((2, 3, 3, 4)),
            DMA((2, 3, 3, 4)),
            DMA((2, 3, 2, 2, ROUNDS)),
            DMA((2, 3, 2, 2, ROUNDS)),
            DMA((2, 3, 2, ROUNDS)),
            DMA((2, 3, 2, ROUNDS)),
            DMA((2, 3, 3, 4)),
            DMA((2, 3, 3, 4)),
            DMA((6,)),
            DMA((15,)),
            DMA((2,)),
            DMA((2,)),
        ],
        compiler_params=params(0, vmem=60),
        name="forward",
    )(*arrays)


def norm_back(grad, rows, gain):
    scale = lax.rsqrt(mean_of(rows * rows) + EPS)
    scaled = grad * gain
    back = scale * scaled - rows * (scale * scale * scale) * mean_of(scaled * rows)
    return back, jnp.sum(grad * rows * scale, axis=0, keepdims=True)


SLOT = 256
FF_SLOTS = tuple((start, min(SLOT, FFH - start)) for start in range(0, FFH, SLOT))
A_SLOTS = ((0, 3), (3, 3), (6, 2))


def slot_view(pool):
    def view(chips, j, part):
        lanes = slice(None) if part is None else pl.ds(part * 128, 128)
        return pool.at[(pl.ds(*A_SLOTS[j]),) + tuple(chips) + (slice(None), lanes)]

    return view


def backward_kernel(
    wa, wm, kv, gu, ends, xs_, gains, n1, qt, mixed, lse, att, mid, n2, squares, cosine, sine,
    km, qm, ob,
    grads, dx, outv, other, small_out,
    pool, gbuf, n2t, dmt, wat, mine, theirs, dout, dmid, da, dot_, acc, low, vlow, kvb, own,
    kh0, kw0, kw1, kw2, slab, got_half, got_whole, spare, mh1, mw1, mw2, ah0, aw0, aw1, aw2,
    sbuf,
    lsem, psem, gsem, usem, xsem, xrsem, ks, kr, hs, hr, os_, or_, ws, wr, ls, ms, mr, as_, ar,
    bs, br, fs, fr, credit,
):
    place = position()
    core = lax.axis_index("section")
    chip = lax.axis_index("dp")
    here = (place["x"], place["y"], place["z"])
    partners = greet(place, core=True, far=True)

    def heads_load(layer):
        return pltpu.make_async_copy(wa.at[layer], wat, lsem.at[2 * layer])

    def keys_load(layer):
        return pltpu.make_async_copy(kv.at[layer], kvb, lsem.at[2 * layer + 1])

    heads_load(1).start()
    keys_load(1).start()
    dout[...] = ends[1].astype(jnp.float32)
    small = [[None] * 4, [None] * 4]
    stored = {}

    def swap(slot):
        return send(mine.at[slot], theirs.at[slot], xsem.at[slot], xrsem.at[slot], other_core())

    def feed_loads(layer, index):
        start, size = FF_SLOTS[index]
        slot = index % 2
        copies = []
        for part in range(3):
            copies.append(
                pltpu.make_async_copy(
                    wm.at[layer, :, :, :, :, pl.ds(part * FFH + start, size)],
                    pool.at[3 * slot + part, :, :, :, :, pl.ds(0, size)],
                    psem.at[slot, part],
                )
            )
        for part in range(2):
            copies.append(
                pltpu.make_async_copy(
                    gu.at[layer, :, pl.ds(part * FFH + start, size)],
                    gbuf.at[slot, part, :, pl.ds(0, size)],
                    usem.at[slot, part],
                )
            )
        return copies

    def feed_start(layer):
        for index in range(2):
            for one in feed_loads(layer, index):
                one.start()

    feed_start(1)

    def back_feed(layer, stream, hooks):
        sends = {
            2: ((0, 0),),
            3: ((0, 1),),
            4: ((0, 2),),
            6: ((0, 3),),
            7: ((1, 0),),
            8: ((1, 1),),
            9: ((1, 2),),
        }
        grad_in = dout[...]
        grad_low = grad_in.astype(jnp.bfloat16)
        n2t[...] = n2[layer].astype(jnp.float32).T.astype(jnp.bfloat16)
        dmt[...] = grad_low.astype(jnp.float32).T.astype(jnp.bfloat16)
        mine[0] = jnp.zeros((R, DP), jnp.float32)
        for index, (start, size) in enumerate(FF_SLOTS):
            slot = index % 2
            hooks.get(index, lambda: None)()
            for one in feed_loads(layer, index):
                one.wait()

            def weights(part, slot=slot, size=size):
                return pool[3 * slot + part, :, :, :, :, :size].reshape(DP, size)

            grad_hidden = nn(grad_low, weights(2))
            gate = gbuf[slot, 0, :, :size]
            up = gbuf[slot, 1, :, :size]
            sigma = jax.nn.sigmoid(gate)
            hidden = (gate * sigma * up).astype(jnp.bfloat16)
            grad_gate = grad_hidden * up * sigma * (1.0 + gate * (1.0 - sigma))
            grad_gate = grad_gate.astype(jnp.bfloat16)
            grad_up = (grad_hidden * gate * sigma).astype(jnp.bfloat16)
            mine[0] += nt(grad_gate, weights(0)) + nt(grad_up, weights(1))
            if index + 2 < len(FF_SLOTS):
                for one in feed_loads(layer, index + 2):
                    one.start()
            products = ((n2t, grad_gate), (n2t, grad_up), (dmt, hidden))
            for part, (left, right) in enumerate(products):
                held = 6 + 3 * slot + part
                if held in stored:
                    stored.pop(held).wait()
                pool[held, :, :, :, :, :size] = (
                    nn(left[...], right).astype(jnp.bfloat16).reshape(4, 4, 4, 16, size)
                )
                stored[held] = pltpu.make_async_copy(
                    pool.at[held, :, :, :, :, pl.ds(0, size)],
                    grads.at[layer, :, :, :, :, pl.ds(part * FFH + start, size)],
                    gsem.at[slot, part],
                )
                stored[held].start()
            for half, r in sends.get(index, ()):
                stream.group(half, r)
        for held in list(stored):
            stored.pop(held).wait()
        stream.group(1, 3)
        stream.load()
        one = swap(0)
        one.start()
        one.wait()
        back, gain_row = norm_back(mine[0] + theirs[0], mid[layer], gains[layer, 3:4, :])
        small[layer][1] = gain_row
        middle = grad_in + back
        dmid[...] = middle
        middle_low = middle.astype(jnp.bfloat16)
        da[layer] = middle_low
        heads_load(layer).wait()
        turned = nn(middle_low, wat[:, :, :, :, QS:].reshape(DP, QS))
        turned = without_first_slot(turned.astype(jnp.bfloat16).astype(jnp.float32))
        for batch in range(MB):
            columns = to_columns(turned[batch * T : (batch + 1) * T]).astype(jnp.bfloat16)
            dot_[batch] = jnp.concatenate([jnp.zeros_like(columns), columns], axis=0)

    def terms(layer, batch, rows, scores):
        slopes_out = dot_[batch]
        inner = jnp.sum(
            mixed[layer, batch] * slopes_out[64:, :].astype(jnp.float32), axis=0, keepdims=True
        )
        probs = jnp.exp(scores - lse[layer, batch, 0:1, :])
        slopes = (probs * (nn(rows, slopes_out) - inner)).astype(jnp.bfloat16)
        both = nt(slopes, qt[layer, batch]) + nt(probs.astype(jnp.bfloat16), slopes_out)
        return both.astype(jnp.bfloat16), tn(rows[:, :64], slopes)

    def back_plane(layer, batch, offset, begin=False):
        spot = plane(batch, (place[ORDERS[batch][2]] + offset) % 4)
        rows = kvb[spot + (batch,)].reshape(KB, 128)
        marked = jnp.concatenate([qt[layer, batch], all_heads(qm[0, batch])], axis=0)
        scores = nn(jnp.concatenate([rows, km[spot].reshape(KB, 128)], axis=1), marked)
        both, more = terms(layer, batch, rows, scores)
        kvb[spot + (batch,)] = both.reshape(4, 4, T, 128)
        acc[batch] = more if begin else acc[batch] + more

    def back_own(layer, batch):
        rows = kvb[here + (batch,)]
        back_plane(layer, batch, 0)
        marked = jnp.concatenate([qt[layer, batch], all_heads(qm[1, batch])], axis=0)
        scores = nn(jnp.concatenate([rows, km[here]], axis=1), marked) + all_heads(ob[batch])
        both, more = terms(layer, batch, rows, scores)
        kvb[here + (batch,)] = both
        acc[batch] += more

    def back_queries(layer):
        whole = jnp.concatenate([to_rows(acc[batch] * 0.125) for batch in range(MB)], axis=0)
        turned = turn(whole, tiled(cosine[...]), -tiled(sine[...])).astype(jnp.bfloat16)
        low[layer] = turned
        mine[1] = nt(turned, wat[:, :, :, :, 0:QS].reshape(DP, QS))

    def back_keys(layer):
        key_grads = own[...].reshape(R, 128)
        none = jnp.zeros((R, 64), jnp.float32)
        turned = turn(
            jnp.concatenate([key_grads[:, :64], none], axis=1),
            tiled(cosine[...], 128),
            -tiled(sine[...], 128),
        ).astype(jnp.bfloat16)
        values = jnp.concatenate([key_grads[:, 64:], none], axis=1).astype(jnp.bfloat16)
        low[layer, :, 0:128] = low[layer, :, 0:128] + turned
        vlow[layer] = values
        small[layer][2] = jnp.concatenate(
            [
                jnp.sum(low[layer].astype(jnp.float32), axis=0, keepdims=True),
                jnp.sum(values.astype(jnp.float32), axis=0, keepdims=True),
                jnp.zeros((1, QS - 128), jnp.float32),
            ],
            axis=1,
        )
        mine[1] += nt(turned, wat[:, :, :, :, 0:128].reshape(DP, 128)) + nt(
            values, wat[:, :, :, :, QS : QS + 128].reshape(DP, 128)
        )
        one = swap(1)
        one.start()
        one.wait()
        rows = (ends[0] if layer == 0 else xs_[0]).astype(jnp.float32)
        back, gain_row = norm_back(mine[1] + theirs[1], rows, gains[layer, 2:3, :])
        small[layer][0] = gain_row
        small[layer][3] = jnp.concatenate(
            [squares[layer, 0:1, :], jnp.zeros((1, DP - 128), jnp.float32)], axis=1
        )
        result = (dmid[...] + back).astype(jnp.bfloat16)
        if layer == 0:
            dx[...] = result
        else:
            dout[...] = result.astype(jnp.float32)

    def put(slot, start, product):
        wide = product.shape[1]
        pool[slot, :, :, :, :, pl.ds(start, wide)] = product.astype(jnp.bfloat16).reshape(
            4, 4, 4, 16, wide
        )

    def query_products(layer):
        first = tn(n1[layer], low[layer])
        second = tn(da[layer], att[layer])
        for side, product in enumerate((first, second)):
            put(4 * layer + 2 * side, 128, product[:, 128:SLOT])
            put(4 * layer + 2 * side + 1, 0, product[:, SLOT:])

    def key_products(layer):
        put(4 * layer, 0, tn(n1[layer], low[layer, :, 0:128]))
        put(
            4 * layer + 2,
            0,
            tn(n1[layer], vlow[layer]) + tn(da[layer], att[layer, :, 0:128]),
        )

    def total(terms):
        return sum(term[...].astype(jnp.float32) for term in terms)

    def key_final(j, *terms):
        own[j] = total(terms)

    key_halves = [lambda j, k, ref=ref: ref.at[j, k] for ref in (kh0,)]
    key_wholes = [lambda j, k, ref=ref: ref.at[j, k] for ref in (kw0, kw1, kw2)]
    keys = [
        scatter_stages(
            token_view(kvb), key_halves, key_wholes, place, ks.at[layer], kr.at[layer], key_final
        )
        for layer in range(2)
    ]

    def feed_final(layer):
        def final(j, *terms):
            outv[layer, :, pl.ds(j * FFH, FFH)] = total(terms)

        return final

    def lanes(ref, size):
        return lambda j, k: ref.at[
            (j, k) + (slice(None),) * (len(ref.shape) - 3) + (pl.ds(0, size(k)),)
        ]

    inner_halves = [None, lanes(mh1, lambda k: half_of(FFH, k)[1])]
    inner_wholes = [None] + [lanes(ref, lambda k: FFH) for ref in (mw1, mw2)]
    feed = [
        LargeScatter(
            grads.at[layer], slab, got_half, got_whole, spare, inner_halves, inner_wholes, place,
            (hs.at[layer], hr.at[layer]), (os_.at[layer], or_.at[layer]),
            (ws.at[layer], wr.at[layer]), ls.at[layer], ms.at[layer], mr.at[layer],
            feed_final(layer),
        )
        for layer in range(2)
    ]
    late, early = feed

    def slots(ref):
        return lambda j, k: ref.at[j, k, pl.ds(0, A_SLOTS[j][1])]

    def heads_final(j, *terms):
        begin, count = A_SLOTS[j]
        for index in range(count):
            layer, spot = divmod(begin + index, 4)
            outv[layer, :, pl.ds(CM + spot * SLOT, SLOT)] = total(
                [term.at[index] for term in terms]
            )

    heads = scatter_stages(
        slot_view(pool), [slots(ah0)],
        [slots(ref) for ref in (aw0, aw1, aw2)], place, as_, ar, heads_final,
    )

    def total_small(phase, axis):
        copies = [
            send(
                sbuf.at[4 * phase],
                sbuf.at[4 * phase + k],
                bs.at[phase, k - 1],
                br.at[phase, k - 1],
                chip_id(moved(place, axis, distance)),
            )
            for k, distance in ((1, 1), (2, -1), (3, 2))
        ]

        def begin():
            for one in copies:
                one.start()

        def end():
            for one in copies:
                one.wait()
            total = (
                sbuf[4 * phase] + sbuf[4 * phase + 1] + sbuf[4 * phase + 2] + sbuf[4 * phase + 3]
            )
            if phase < 2:
                sbuf[4 * phase + 4] = total
            else:
                small_out[...] = total

        return begin, end

    def rounds_of(*methods):
        for method in methods:
            for r in range(ROUNDS):
                method(r)

    def back_attend(layer, stream):
        keys_load(layer).wait()
        for batch in range(MB):
            back_plane(layer, batch, 2, True)
        keys[layer][0]()
        stream.pass_on(0)
        for batch in range(MB):
            back_plane(layer, batch, 1)
        stream.pass_on(1)
        for batch in range(MB):
            back_plane(layer, batch, 3)
        keys[layer][1]()
        stream.pass_on(2)
        for batch in range(MB):
            back_own(layer, batch)
        keys[layer][2]()
        keys[layer][3]()
        stream.pass_on(3)
        back_queries(layer)
        keys[layer][5]()
        keys[layer][6]()
        stream.third()
        stream.phases[0]()

    def settle_early():
        early.phases[5]()
        early.finish()
        for axis in "xyz":
            for distance in (1, -1, 2):
                pl.semaphore_signal(
                    credit,
                    inc=1,
                    device_id=chip_id(moved(place, axis, distance)),
                    device_id_type=MESH,
                )
        pl.semaphore_wait(credit, 9)

    back_feed(1, early, {1: lambda: settle(partners)})
    back_attend(1, early)
    feed_start(0)
    keys[1][8]()
    keys[1][9]()
    keys_load(0).start()
    back_keys(1)
    heads_load(0).start()
    back_feed(
        0,
        late,
        {
            0: early.phases[1],
            1: lambda: (early.phases[2](), early.phases[3]()),
            2: settle_early,
        },
    )
    back_attend(0, late)
    query_products(1)
    key_products(1)
    query_products(0)
    keys[0][8]()
    keys[0][9]()
    back_keys(0)
    key_products(0)
    sbuf[0] = jnp.concatenate(small[0] + small[1], axis=0)
    sums = [total_small(phase, axis) for phase, axis in enumerate("xyz")]
    sums[0][0]()
    heads[0]()
    late.phases[1]()
    sums[0][1]()
    sums[1][0]()
    heads[1]()
    late.phases[2]()
    late.phases[3]()
    heads[2]()
    heads[3]()
    sums[1][1]()
    sums[2][0]()
    late.phases[5]()
    heads[5]()
    heads[6]()
    sums[2][1]()
    heads[8]()
    for layer in range(2):
        outv[layer, 14:15, pl.ds(CM, CA)] = small_out[4 * layer + 2 : 4 * layer + 3, :]
    trade = send(outv.at[1 - core], other, fs, fr, other_core())
    trade.start()
    late.finish()
    heads[9]()
    trade.wait()


def backward(*arrays):
    low, full = jnp.bfloat16, jnp.float32
    half = FFH - FFH // 256 * 128

    def ring(last, phase, count=2):
        return pltpu.VMEM((3, count) + last[:-2] + (4,) * (2 - phase) + last[-2:], low)

    return pl.pallas_call(
        backward_kernel,
        out_shape=(
            shape((2, 4, 4, 4, 16, CM), low),
            shape((R, DP), low),
            shape((2, 16, C), full),
            shape((16, C), full),
            shape((8, DP), full),
        ),
        in_specs=[ANY] * 4 + [VMEM] * 16,
        out_specs=(ANY,) + (VMEM,) * 4,
        scratch_shapes=[
            pltpu.VMEM((12, 4, 4, 4, 16, SLOT), low),
            pltpu.VMEM((2, 2, R, SLOT), full),
            pltpu.VMEM((DP, R), low),
            pltpu.VMEM((DP, R), low),
            pltpu.VMEM((4, 4, 4, 16, CA), low),
            pltpu.VMEM((2, R, DP), full),
            pltpu.VMEM((2, R, DP), full),
            pltpu.VMEM((R, DP), full),
            pltpu.VMEM((R, DP), full),
            pltpu.VMEM((2, R, DP), low),
            pltpu.VMEM((MB, 128, QS), low),
            pltpu.VMEM((MB, 64, QS), full),
            pltpu.VMEM((2, R, QS), low),
            pltpu.VMEM((2, R, 128), low),
            pltpu.VMEM((4, 4, 4, MB, T, 128), low),
            pltpu.VMEM((MB, T, 128), full),
        ]
        + [
            ring((T // 2, 128), 0),
            ring((T, 128), 0),
            ring((T, 128), 1, 3),
            ring((T, 128), 2, 3),
            pltpu.VMEM((3, 4, 4, 16, FFH), low),
            ring((16, half), 0),
            ring((16, FFH), 0),
            ring((16, 384), 0),
            ring((16, half), 1),
            ring((16, FFH), 1),
            ring((16, FFH), 2, 3),
            ring((3, 16, 128), 0),
            ring((3, 16, SLOT), 0),
            ring((3, 16, SLOT), 1, 3),
            ring((3, 16, SLOT), 2, 3),
        ]
        + [
            pltpu.VMEM((12, 8, DP), full),
            DMA((4,)),
            DMA((2, 3)),
            DMA((2, 3)),
            DMA((2, 2)),
            DMA((2,)),
            DMA((2,)),
            DMA((2, 3, 3, 4)),
            DMA((2, 3, 3, 4)),
            DMA((2, 3, 2, ROUNDS)),
            DMA((2, 3, 2, ROUNDS)),
            DMA((2, 3, 2, ROUNDS)),
            DMA((2, 3, 2, ROUNDS)),
            DMA((2, 3, 2, ROUNDS)),
            DMA((2, 3, 2, ROUNDS)),
            DMA((2, 9)),
            DMA((2, 3, 3, 4)),
            DMA((2, 3, 3, 4)),
            DMA((3, 3, 4)),
            DMA((3, 3, 4)),
            DMA((3, 3)),
            DMA((3, 3)),
            DMA,
            DMA,
            pltpu.SemaphoreType.REGULAR,
        ],
        compiler_params=params(1, vmem=63),
        name="backward",
    )(*arrays)


def assemble_kernel(
    kept, other, dx, xs_, sums, valid, boundary, grad_qkv, grad_bias, grad_out, grad_gu, grad_down,
    grad_gain, rms,
):
    core = lax.axis_index("section")
    own, far = jnp.where(core == 0, kept[0], kept[1]), other[...]
    sides = (jnp.where(core == 0, own, far), jnp.where(core == 0, far, own))

    def column(start, size):
        return [side[:, start : start + size] for side in sides]

    qkv = jnp.concatenate(column(CM + 64, 448) + column(CM, 64) + column(CM + QS, 64), axis=1)
    out = jnp.concatenate(column(CM + QS + 64, 448), axis=1)
    gate_up = jnp.concatenate(column(0, FFH) + column(FFH, FFH), axis=1)
    down = jnp.concatenate(column(2 * FFH, FFH), axis=1)
    for row in range(14):
        grad_qkv[row] = qkv[row : row + 1, :]
        grad_out[row] = out[row : row + 1, :]
        grad_gu[row] = gate_up[row : row + 1, :]
        grad_down[row] = down[row : row + 1, :]
    rows = [side[14:15, CM:] for side in sides]
    grad_bias[...] = jnp.concatenate(
        [row[:, 64:QS] for row in rows]
        + [row[:, :64] for row in rows]
        + [row[:, QS : QS + 64] for row in rows],
        axis=1,
    )
    mine = jnp.where(core == 0, sums[0:4, :], sums[4:8, :])
    rest = jnp.concatenate([mine, jnp.zeros((12, DP), jnp.float32)], axis=0)
    terms = []
    for _ in range(3):
        term = rest.astype(jnp.bfloat16)
        rest = rest - term.astype(jnp.float32)
        terms.append(term)
    result = jnp.where(core == 0, dx[...].astype(jnp.float32), xs_[1].astype(jnp.float32))
    narrow = nt(
        jnp.concatenate([result.astype(jnp.bfloat16)] + terms, axis=0), spread_matrix()
    )
    boundary[...] = narrow[:R].astype(jnp.bfloat16)
    grad_gain[...] = narrow[R : R + 2] + narrow[R + 16 : R + 18] + narrow[R + 32 : R + 34]
    for batch in range(MB):
        count = jnp.sum(valid[batch : batch + 1, :].astype(jnp.float32), axis=1, keepdims=True)
        rms[batch] = jnp.sqrt(mine[3:4, 3 * batch : 3 * batch + 3] / (count * float(BLOCK * D)))


def assemble(*arrays):
    full = jnp.float32
    return pl.pallas_call(
        assemble_kernel,
        out_shape=(
            shape((R, D), jnp.bfloat16),
            shape((14, 1, D + 256), full),
            shape((1, D + 256), full),
            shape((14, 1, D), full),
            shape((14, 1, 4 * FFH), full),
            shape((14, 1, 2 * FFH), full),
            shape((2, D), full),
            shape((MB, 1, MB), full),
        ),
        in_specs=[VMEM] * 6,
        out_specs=(VMEM,) * 8,
        compiler_params=params(),
        name="assemble",
    )(*arrays)


def shards(
    ends,
    segment_ids,
    valid_blocks,
    qkv_weight,
    qkv_bias,
    out_weight,
    gate_up_weight,
    down_weight,
    norm_gains,
):
    chip = lax.axis_index("dp")
    places = chip * T + jnp.arange(T, dtype=jnp.int32)
    frequency = THETA ** (-(jnp.arange(128) % 32).astype(jnp.float32) * 2.0 / 64)
    sign = jnp.where(jnp.arange(128) % 64 < 32, -1.0, 1.0)
    angles = places.astype(jnp.float32)[:, None] * frequency[None, :]
    cosine = jnp.cos(angles)
    sine = jnp.sin(angles) * sign[None, :]

    (
        wa, wm, kv, gu, ends_all, gains, n1, qt, mixed, lse, att, mid, n2, _, xs_, sq, km, qm, ob,
    ) = forward(
        gate_up_weight[0],
        down_weight[0],
        qkv_weight[0],
        out_weight[0],
        qkv_bias,
        norm_gains[0],
        ends.reshape(R, D),
        segment_ids,
        valid_blocks,
        cosine,
        sine,
    )
    _, dx, kept, other, sums = backward(
        wa, wm, kv, gu, ends_all, xs_, gains, n1, qt, mixed, lse, att, mid, n2, sq, cosine, sine,
        km, qm, ob,
    )
    boundary, *grads, rms = assemble(kept, other, dx, xs_, sums, valid_blocks)
    grad_qkv, grad_bias, grad_out, grad_gu, grad_down, grad_gain = grads
    return (
        boundary.reshape(1, MB, T, D),
        grad_qkv.transpose(1, 0, 2),
        grad_bias,
        grad_out.transpose(1, 0, 2),
        grad_gu.transpose(1, 0, 2),
        grad_down.transpose(1, 0, 2),
        grad_gain[None],
        rms.transpose(1, 0, 2),
    )


def solution(mesh):
    in_specs = (
        P("section", None, "dp", None),
        P(),
        P(),
        P("section", "dp", None),
        P("section", None),
        P("section", "dp", None),
        P("section", "dp", None),
        P("section", "dp", None),
        P("section", None, None),
    )
    out_specs = (
        P("section", None, "dp", None),
        P("section", "dp", None),
        P("section", None),
        P("section", "dp", None),
        P("section", "dp", None),
        P("section", "dp", None),
        P("section", None, None),
        P("section", None, None),
    )
    return jax.shard_map(shards, mesh=mesh, in_specs=in_specs, out_specs=out_specs, check_vma=False)
```

```python
import functools
import math

import jax
import jax.numpy as jnp
from jax import lax
from jax.experimental import pallas as pl
from jax.experimental.pallas import tpu as pltpu
from jax.sharding import PartitionSpec as P

MESH = pl.DeviceIdType.MESH
EPS = 1e-06
THETA = 1000000.0
MASKED = -1e30

MB = 3
T = 64
R = MB * T
D = 896
DP = 1024
FFH = 2432
QS = 512
C_UP, C_DOWN, C_QK, C_VO, C = FFH, 2 * FFH, 3 * FFH, 3 * FFH + QS, 3 * FFH + 2 * QS
KB = 1024
SEQ = 4096
MIB = 1024 * 1024

BLOCK = 128

THIRDS = ((0, 22 * 128), (22 * 128, 22 * 128), (44 * 128, 21 * 128))
ORDERS = (("z", "y", "x"), ("y", "x", "z"), ("x", "z", "y"))
CM, CA = 3 * FFH, 2 * QS
M_THIRDS = ((0, FFH), (FFH, FFH), (2 * FFH, FFH))
A_THIRDS = ((0, 384), (384, 384), (768, 256))


def position():
    chip = lax.axis_index("dp")
    return {"x": chip // 16, "y": (chip // 4) % 4, "z": chip % 4}


def moved(place, axis, distance):
    other = dict(place)
    other[axis] = (place[axis] + distance + 4) % 4
    return other


def chip_id(place):
    return {"dp": place["x"] * 16 + place["y"] * 4 + place["z"]}


def other_core():
    return {"section": 1 - lax.axis_index("section")}


def greet(place, core=False, chips=True, far=False):
    barrier = pltpu.get_barrier_semaphore()
    count = 0
    if chips:
        for axis in "xyz":
            for distance in (1, -1, 2) if far else (1, -1):
                pl.semaphore_signal(
                    barrier,
                    inc=1,
                    device_id=chip_id(moved(place, axis, distance)),
                    device_id_type=MESH,
                )
                count += 1
    if core:
        pl.semaphore_signal(barrier, inc=1, device_id=other_core(), device_id_type=MESH)
        count += 1
    return count


def settle(count):
    pl.semaphore_wait(pltpu.get_barrier_semaphore(), count)


def send(src, dst, send_sem, recv_sem, device):
    return pltpu.make_async_remote_copy(
        src, dst, send_sem, recv_sem, device_id=device, device_id_type=MESH
    )


def cube(done, place):
    return tuple(slice(None) if axis in done else place[axis] for axis in "xyz")


DIRECT = ((0, 1), (1, -1), (2, 2))


def gather_stages(view, place, send_sems, recv_sems, direct=(0, 1)):
    pending = []

    def copy(j, phase, k, whose, part, distance):
        ref = view(cube(ORDERS[j][:phase], whose), j, part)
        return send(
            ref,
            ref,
            send_sems.at[j, phase, k],
            recv_sems.at[j, phase, k],
            chip_id(moved(place, ORDERS[j][phase], distance)),
        )

    def first(phase):
        for j in range(3):
            for k, distance in DIRECT if phase in direct else DIRECT[:2]:
                one = copy(j, phase, k, place, None, distance)
                one.start()
                pending.append(one)

    def second(phase):
        if phase in direct:
            return
        for j in range(3):
            for k, distance in DIRECT[:2]:
                whose = moved(place, ORDERS[j][phase], -distance)
                copy(j, phase, k, whose, None, distance).wait_recv()
                one = copy(j, phase, 2 + k, whose, k, distance)
                one.start()
                pending.append(one)

    def third(phase):
        for j in range(3):
            if phase in direct:
                for k, distance in DIRECT:
                    whose = moved(place, ORDERS[j][phase], -distance)
                    copy(j, phase, k, whose, None, distance).wait_recv()
            else:
                for k, distance in DIRECT[:2]:
                    whose = moved(place, ORDERS[j][phase], 2)
                    copy(j, phase, 2 + k, whose, k, distance).wait_recv()

    def finish():
        for one in pending:
            one.wait_send()

    stages = []
    for phase in range(3):
        stages.append(functools.partial(first, phase))
        stages.append(functools.partial(second, phase))
        stages.append(functools.partial(third, phase))
    stages.append(finish)
    return stages


PARTS = (
    ((0, 256), (256, 256), (512, 256), (768, 384)),
    ((1152, 256), (1408, 256), (1664, 384), (2048, 384)),
)
ROUNDS = 4
TURNS = tuple((j, k, (1, -1)[k]) for j in range(3) for k in range(2))


class LargeGather:
    def __init__(self, ref, place, send_sems, recv_sems, part_sems, pass_sems):
        self.ref, self.place = ref, place
        self.part_sems, self.pass_sems = part_sems, pass_sems
        stages = gather_stages(
            weight_view(ref, M_THIRDS), place, send_sems, recv_sems, direct=(0,)
        )
        self.phases, self.done = stages[:6], stages[9]
        self.pending = []

    def slab(self, j, whose, half, r):
        start, size = PARTS[half][r]
        chips = cube(ORDERS[j][:2], whose)
        return self.ref.at[chips + (slice(None), pl.ds(j * FFH + start, size))]

    def whose(self, j, distance):
        return moved(self.place, ORDERS[j][2], distance)

    def part(self, j, k, distance, half, r, whose):
        ref = self.slab(j, whose, half, r)
        sems = [side.at[j, k, half, r] for side in self.part_sems]
        return send(ref, ref, *sems, chip_id(self.whose(j, distance)))

    def passed(self, j, k, distance, r, whose):
        ref = self.slab(j, whose, k, r)
        sems = [side.at[j, k, r] for side in self.pass_sems]
        return send(ref, ref, *sems, chip_id(self.whose(j, distance)))

    def start(self, one):
        one.start()
        self.pending.append(one)

    def group(self, half, r):
        for j, k, distance in TURNS:
            self.start(self.part(j, k, distance, half, r, self.place))

    def pass_on(self, half, r):
        distance = (1, -1)[half]
        for j in range(3):
            back = self.whose(j, -distance)
            self.part(j, half, distance, half, r, back).wait_recv()
            self.start(self.passed(j, half, distance, r, back))

    def ready(self, half, r):
        for j in range(3):
            distance = (1, -1)[1 - half]
            self.part(j, 1 - half, distance, half, r, self.whose(j, -distance)).wait_recv()
            self.passed(j, half, (1, -1)[half], r, self.whose(j, 2)).wait_recv()

    def finish(self):
        self.done()
        for one in self.pending:
            one.wait_send()


def scatter_stages(
    view, halves, wholes, place, send_sems, recv_sems, final, begin=0, direct=(1, 2)
):
    pending = []

    def half_copy(j, phase, k, distance):
        far = moved(place, back_axis(j, phase), 2)
        return send(
            view(back_chips(j, phase, far), j, k),
            halves[phase](j, k),
            send_sems.at[j, phase, k],
            recv_sems.at[j, phase, k],
            chip_id(moved(place, back_axis(j, phase), distance)),
        )

    def whole_copy(j, phase, k, distance):
        near = moved(place, back_axis(j, phase), distance)
        slot = k if phase in direct else 2 + k
        return send(
            view(back_chips(j, phase, near), j, None),
            wholes[phase](j, k),
            send_sems.at[j, phase, slot],
            recv_sems.at[j, phase, slot],
            chip_id(near),
        )

    def first(phase):
        for j in range(3):
            for k, distance in DIRECT if phase in direct else DIRECT[:2]:
                one = (whole_copy if phase in direct else half_copy)(j, phase, k, distance)
                one.start()
                pending.append(one)

    def second(phase):
        if phase in direct:
            return
        for j in range(3):
            for k, distance in DIRECT[:2]:
                half_copy(j, phase, k, distance).wait_recv()
                near = moved(place, back_axis(j, phase), distance)
                mine = view(back_chips(j, phase, near), j, k)
                add(mine, mine, halves[phase](j, k))
                one = whole_copy(j, phase, k, distance)
                one.start()
                pending.append(one)

    def third(phase):
        turns = DIRECT if phase in direct else DIRECT[:2]
        for j in range(3):
            for k, distance in turns:
                whole_copy(j, phase, k, distance).wait_recv()
            mine = view(back_chips(j, phase, place), j, None)
            terms = [wholes[phase](j, k) for k, distance in turns]
            if phase < 2:
                add(mine, mine, *terms)
            else:
                final(j, mine, *terms)

    def finish():
        for one in pending:
            one.wait_send()

    stages = []
    for phase in range(begin, 3):
        stages.append(functools.partial(first, phase))
        stages.append(functools.partial(second, phase))
        stages.append(functools.partial(third, phase))
    stages.append(finish)
    return stages


def back_axis(j, phase):
    return ORDERS[j][2 - phase]


def back_chips(j, phase, whose):
    return cube(ORDERS[j][: 2 - phase], whose)


def add(dst, *terms):
    dst[...] = sum(term[...].astype(jnp.float32) for term in terms).astype(dst.dtype)


def half_of(size, part):
    half = size // 256 * 128
    return (0, half) if part == 0 else (half, size - half)


class LargeScatter:
    def __init__(
        self, source, slab, got_half, got_whole, spare, inner_halves, inner_wholes, place,
        half_sems, rest_sems, pass_sems, load_sems, send_sems, recv_sems, final,
    ):
        self.source, self.slab, self.place = source, slab, place
        self.got_half, self.got_whole, self.spare = got_half, got_whole, spare
        self.half_sems, self.rest_sems, self.pass_sems = half_sems, rest_sems, pass_sems
        self.load_sems = load_sems
        self.pending = []

        def view(chips, j, part):
            rest = tuple(index for axis, index in zip("xyz", chips) if axis != back_axis(j, 0))
            cols = slice(None) if part is None else pl.ds(*half_of(FFH, part))
            return slab.at[(j,) + rest + (slice(None), cols)]

        stages = scatter_stages(
            view, inner_halves, inner_wholes, place, send_sems, recv_sems, final, begin=1, direct=(2,)
        )
        self.phases, self.done = stages[:-1], stages[-1]

    def terms(self, j, whose, cols):
        chips = back_chips(j, 0, whose)
        return self.source.at[chips + (slice(None), pl.ds(j * FFH + cols[0], cols[1]))]

    def near(self, j, distance):
        return moved(self.place, back_axis(j, 0), distance)

    def half_ref(self, j, k, r):
        start, size = PARTS[k][r]
        return self.got_half.at[j, k, :, :, :, pl.ds(start - PARTS[k][0][0], size)]

    def copy(self, src, dst, sems, j, k, distance, r):
        return send(
            src, dst, sems[0].at[j, k, r], sems[1].at[j, k, r], chip_id(self.near(j, distance))
        )

    def half_copy(self, j, k, distance, r):
        src = self.terms(j, self.near(j, 2), PARTS[k][r])
        return self.copy(src, self.half_ref(j, k, r), self.half_sems, j, k, distance, r)

    def rest_copy(self, j, k, distance, r):
        cols = PARTS[1 - k][r]
        src = self.terms(j, self.near(j, distance), cols)
        dst = self.got_whole.at[j, k, :, :, :, pl.ds(*cols)]
        return self.copy(src, dst, self.rest_sems, j, k, distance, r)

    def pass_copy(self, j, k, distance, r):
        dst = self.got_whole.at[j, k, :, :, :, pl.ds(*PARTS[k][r])]
        return self.copy(self.half_ref(j, k, r), dst, self.pass_sems, j, k, distance, r)

    def own_load(self, j, k, distance, r):
        return pltpu.make_async_copy(
            self.terms(j, self.near(j, distance), PARTS[k][r]),
            self.spare.at[j, k, :, :, :, pl.ds(0, PARTS[k][r][1])],
            self.load_sems.at[2 * j + k],
        )

    def slab_load(self, j):
        return pltpu.make_async_copy(
            self.terms(j, self.place, (0, FFH)), self.slab.at[j], self.load_sems.at[6 + j]
        )

    def start(self, one):
        one.start()
        self.pending.append(one)

    def group(self, half, r):
        for j in range(3):
            self.start(self.half_copy(j, half, (1, -1)[half], r))
            self.start(self.rest_copy(j, 1 - half, (1, -1)[1 - half], r))

    def load(self):
        for j, k, distance in TURNS:
            self.own_load(j, k, distance, 0).start()
        for j in range(3):
            self.slab_load(j).start()

    def pass_on(self, r):
        for j, k, distance in TURNS:
            self.half_copy(j, k, distance, r).wait_recv()
            self.own_load(j, k, distance, r).wait()
            own = self.spare.at[j, k, :, :, :, pl.ds(0, PARTS[k][r][1])]
            add(self.half_ref(j, k, r), self.half_ref(j, k, r), own)
            self.start(self.pass_copy(j, k, distance, r))
            if r + 1 < ROUNDS:
                self.own_load(j, k, distance, r + 1).start()

    def third(self):
        for j in range(3):
            self.slab_load(j).wait()
            for k in range(2):
                for r in range(ROUNDS):
                    self.rest_copy(j, k, (1, -1)[k], r).wait_recv()
                    self.pass_copy(j, k, (1, -1)[k], r).wait_recv()
            add(self.slab.at[j], self.slab.at[j], self.got_whole.at[j, 0], self.got_whole.at[j, 1])

    def finish(self):
        self.done()
        for one in self.pending:
            one.wait_send()


def weight_view(ref, thirds=THIRDS):
    def view(chips, j, part):
        start, size = thirds[j]
        if part is not None:
            half = size // 256 * 128
            start, size = (start, half) if part == 0 else (start + half, size - half)
        return ref.at[tuple(chips) + (slice(None), pl.ds(start, size))]

    return view


def token_view(ref):
    def view(chips, j, part):
        rows = slice(None) if part is None else pl.ds(part * 32, 32)
        return ref.at[tuple(chips) + (j, rows, slice(None))]

    return view


def params(collective_id=None, vmem=56):
    if collective_id is None:
        return pltpu.CompilerParams(vmem_limit_bytes=vmem * MIB)
    return pltpu.CompilerParams(
        collective_id=collective_id, has_side_effects=True, vmem_limit_bytes=vmem * MIB
    )


ANY = pl.BlockSpec(memory_space=pl.ANY)
VMEM = pl.BlockSpec(memory_space=pltpu.VMEM)
SMEM = pl.BlockSpec(memory_space=pltpu.SMEM)
DMA = pltpu.SemaphoreType.DMA


def shape(dims, dtype):
    return jax.ShapeDtypeStruct(dims, dtype)


def nn(left, right):
    return jnp.dot(left, right, preferred_element_type=jnp.float32)


def nt(left, right):
    return lax.dot_general(
        left, right, (((1,), (1,)), ((), ())), preferred_element_type=jnp.float32
    )


def tn(left, right):
    return lax.dot_general(
        left, right, (((0,), (0,)), ((), ())), preferred_element_type=jnp.float32
    )


DEAD = 4


def key_marks(segments, lengths, chip):
    rows = lax.broadcasted_iota(jnp.int32, (8, SEQ), 0)
    keys = lax.broadcasted_iota(jnp.int32, (8, SEQ), 1)
    groups = []
    for batch in range(MB):
        same = (rows < DEAD) & (segments[batch : batch + 1, :] == rows)
        dead = (keys >= chip * T) | (keys.astype(jnp.float32) >= lengths[batch])
        groups.append(jnp.where(same | ((rows == DEAD) & dead), 1.0, 0.0))
    groups.append(jnp.zeros((128 - 8 * MB, SEQ), jnp.float32))
    marks = jnp.concatenate(groups, axis=0).T.astype(jnp.bfloat16)
    return marks.reshape(4, 4, 4, T, 128)


def query_marks(ids, batch, dead):
    place = lax.broadcasted_iota(jnp.int32, (128, 128), 0) - 8 * batch
    hit = (place >= 0) & (place < DEAD) & (place != ids)
    if dead:
        hit = hit | (place == DEAD)
    return jnp.where(hit, MASKED, 0.0).astype(jnp.bfloat16)


def own_bias(full):
    key = lax.broadcasted_iota(jnp.int32, (T, 128), 0)
    query = lax.broadcasted_iota(jnp.int32, (T, 128), 1) % T
    allowed = (key == query) | ((key <= query) & (full > 0.0))
    return jnp.where(allowed, 0.0, MASKED)


def all_heads(two):
    return jnp.concatenate([two] * 4, axis=1)


def mean_of(values):
    return jnp.sum(values, axis=-1, keepdims=True) * (1.0 / D)


def turn(values, cosine, sine):
    width = values.shape[1]
    lane = lax.broadcasted_iota(jnp.int32, values.shape, 1) % 64
    swapped = jnp.where(lane < 32, pltpu.roll(values, width - 32, 1), pltpu.roll(values, 32, 1))
    return values * cosine + swapped * sine


def tiled(table, columns=QS):
    wide = jnp.concatenate([table] * (columns // 128), axis=1)
    return jnp.concatenate([wide] * MB, axis=0)


def plane(batch, index):
    return tuple(index if axis == ORDERS[batch][2] else slice(None) for axis in "xyz")


def to_columns(rows):
    turned = rows.T
    return jnp.concatenate([turned[64 * h : 64 * h + 64] for h in range(8)], axis=1)


def to_rows(columns):
    pairs = []
    for pair in range(4):
        turned = columns[:, 128 * pair : 128 * pair + 128].T
        pairs.append(jnp.concatenate([turned[:64], turned[64:]], axis=1))
    return jnp.concatenate(pairs, axis=1)


def without_first_slot(rows):
    lane = lax.broadcasted_iota(jnp.int32, rows.shape, 1)
    return jnp.where(lane < 64, 0.0, rows)


def spread_matrix():
    row = lax.broadcasted_iota(jnp.int32, (D, DP), 0)
    column = lax.broadcasted_iota(jnp.int32, (1, DP), 1)
    spot = column % 16
    target = jnp.where(spot < 14, column // 16 * 14 + spot, -1)
    return jnp.where(row == target, 1.0, 0.0).astype(jnp.bfloat16)


def forward_kernel(
    gate_up, down, qkv, out_w, bias_in, gains_in, ends, segments, valid, cosine, sine,
    wa, wm, kv, gu, cot, gains, n1, qt, mixed, lse, att, mid, n2, xs_, sq, km, qm, ob,
    ends_v, small_v, give_a, give_m, stage_a, stage_m, wat, wml, kvb, gu_v, mine, theirs,
    state, acc, lsem, ssem, rsem, a_s, a_r, m_s, m_r, mp_s, mp_r, mq_s, mq_r, k_s, k_r, osem, wsem, xsem,
    xrsem,
):
    place = position()
    core = lax.axis_index("section")
    chip = lax.axis_index("dp")
    here = (place["x"], place["y"], place["z"])
    partners = greet(place, core=True, far=True)

    def heads_half(half):
        wide = qkv[...].astype(jnp.float32)
        outs_ = out_w[...].astype(jnp.float32)
        return jnp.concatenate(
            [
                wide[:, D + 64 * half : D + 64 * half + 64],
                wide[:, 448 * half : 448 * half + 448],
                wide[:, D + 128 + 64 * half : D + 192 + 64 * half],
                outs_[:, 448 * half : 448 * half + 448],
            ],
            axis=1,
        )

    def bias_half(half):
        wide = bias_in[...].astype(jnp.float32)
        return jnp.concatenate(
            [
                wide[:, D + 64 * half : D + 64 * half + 64],
                wide[:, 448 * half : 448 * half + 448],
                wide[:, D + 128 + 64 * half : D + 192 + 64 * half],
                jnp.zeros((1, 448), jnp.float32),
            ],
            axis=1,
        )

    halves = [heads_half(0), heads_half(1)]
    for dst, side in ((stage_a.at[core], 0), (give_a, 1)):
        dst[...] = jnp.zeros((16, CA), jnp.bfloat16)
        dst[0:14, :] = jnp.where(core == side, halves[0], halves[1]).astype(jnp.bfloat16)
    for dst, index in ((stage_m.at[core], core), (give_m, 1 - core)):
        dst[...] = jnp.zeros((16, CM), jnp.bfloat16)
        start = pl.multiple_of(index * FFH, 128)
        dst[0:14, 0:FFH] = gate_up[:, pl.ds(start, FFH)]
        dst[0:14, FFH : 2 * FFH] = gate_up[:, pl.ds(pl.multiple_of(start + 2 * FFH, 128), FFH)]
        dst[0:14, 2 * FFH : CM] = down[:, pl.ds(start, FFH)]
    settle(partners)

    trades = []

    def trade(index, give, dst):
        out = send(give, dst.at[core], ssem.at[index], rsem.at[index], other_core())
        back = send(give, dst.at[1 - core], ssem.at[index], rsem.at[index], other_core())
        out.start()
        trades.append((out, back))

    trade(0, give_a, stage_a)
    trade(1, give_m, stage_m)

    def arrive(index):
        out, back = trades[index]
        back.wait_recv()
        out.wait_send()

    arrive(0)
    into = [
        pltpu.make_async_copy(stage_a.at[layer], wat.at[(layer,) + here], lsem.at[layer])
        for layer in range(2)
    ]
    for one in into:
        one.start()
    for one in into:
        one.wait()
    attn = [
        gather_stages(weight_view(wat.at[layer], A_THIRDS), place, a_s.at[layer], a_r.at[layer])
        for layer in range(2)
    ]
    feed = [
        LargeGather(
            ref,
            place,
            m_s.at[layer],
            m_r.at[layer],
            (mp_s.at[layer], mp_r.at[layer]),
            (mq_s.at[layer], mq_r.at[layer]),
        )
        for layer, ref in enumerate((wml, wm.at[1]))
    ]
    early, late = feed
    keys = [
        gather_stages(token_view(kvb.at[layer]), place, k_s.at[layer], k_r.at[layer])
        for layer in range(2)
    ]
    attn[0][0]()
    attn[1][0]()
    arrive(1)
    into = [
        pltpu.make_async_copy(stage_m.at[0], wml.at[here], lsem.at[2]),
        pltpu.make_async_copy(stage_m.at[1], wm.at[(1,) + here], lsem.at[3]),
    ]
    for one in into:
        one.start()
    for one in into:
        one.wait()
    early.phases[0]()
    spread = spread_matrix()
    ends_v[core] = nn(ends[...], spread).astype(jnp.bfloat16)
    small_v[core] = jnp.zeros((8, DP), jnp.float32)
    small_v[core, 0:1, :] = bias_half(0)
    small_v[core, 1:2, :] = bias_half(1)
    small_v[core, 2:4, :] = nn(gains_in[...], spread)
    trade(2, ends_v.at[core], ends_v)
    trade(3, small_v.at[core], small_v)
    attn[0][1]()
    attn[1][1]()
    early.phases[1]()
    lengths = [
        jnp.sum(valid[batch : batch + 1, :].astype(jnp.float32), axis=1, keepdims=True) * BLOCK
        for batch in range(MB)
    ]
    km[...] = key_marks(segments, lengths, chip)
    pair = segments[:, pl.ds(pl.multiple_of(chip // 2 * 128, 128), 128)]
    ids = jnp.where(chip % 2 == 0, pair[:, :64], pair[:, 64:])
    ids = jnp.concatenate([ids, ids], axis=1)
    first_key = (chip * T).astype(jnp.float32)
    for batch in range(MB):
        for kind in range(2):
            qm[kind, batch] = query_marks(ids[batch : batch + 1, :], batch, kind == 0)
        full = jnp.where(first_key < lengths[batch], 1.0, 0.0)
        ob[batch] = own_bias(full)
    for index in range(2, 8):
        attn[0][index]()
        attn[1][index]()
        if index == 3:
            early.phases[2]()
            early.phases[3]()
    arrive(2)
    arrive(3)
    cot[...] = ends_v[...]
    gains[...] = small_v[...]
    attn[0][8]()

    outs = {}

    def store(src, dst, index):
        outs[index] = pltpu.make_async_copy(src, dst, osem.at[index])
        outs[index].start()

    def rows_of(layer):
        return ends_v[0] if layer == 0 else xs_[0]

    def bias_of(layer):
        return jnp.where(core == 0, gains[layer, 0:1, :], gains[layer, 1:2, :])

    def project_keys(layer):
        rows = rows_of(layer).astype(jnp.float32)
        gain = gains[layer, 2:3, :]
        normed = (rows * lax.rsqrt(mean_of(rows * rows) + EPS) * gain).astype(jnp.bfloat16)
        n1[layer] = normed
        bias = bias_of(layer)
        first = nn(normed, wat[layer, :, :, :, :, 0:128].reshape(DP, 128)) + bias[:, 0:128]
        values = nn(normed, wat[layer, :, :, :, :, QS : QS + 128].reshape(DP, 128))
        values = values + bias[:, QS : QS + 128]
        turned = turn(first, tiled(cosine[...], 128), tiled(sine[...], 128))
        own = jnp.concatenate([turned[:, :64], values[:, :64]], axis=1)
        kvb[(layer,) + here] = own.astype(jnp.bfloat16).reshape(MB, T, 128)

    def project_queries(layer):
        projected = nn(n1[layer], wat[layer, :, :, :, :, 0:QS].reshape(DP, QS))
        projected = projected + bias_of(layer)[:, 0:QS]
        turned = turn(projected, tiled(cosine[...]), tiled(sine[...]))
        heads = without_first_slot(turned).astype(jnp.bfloat16).astype(jnp.float32) * 0.125
        for batch in range(MB):
            columns = to_columns(heads[batch * T : (batch + 1) * T]).astype(jnp.bfloat16)
            qt[layer, batch] = jnp.concatenate([columns, jnp.zeros_like(columns)], axis=0)

    def attend_own(layer, batch):
        queries = jnp.concatenate([qt[layer, batch], all_heads(qm[1, batch])], axis=0)
        rows = kvb[(layer,) + here + (batch,)]
        scores = nn(jnp.concatenate([rows, km[here]], axis=1), queries) + all_heads(ob[batch])
        top = jnp.max(scores, axis=0, keepdims=True)
        probs = jnp.exp(scores - top)
        state[batch, 0:1, :] = top
        state[batch, 1:2, :] = jnp.sum(probs, axis=0, keepdims=True)
        acc[batch] = tn(rows, probs.astype(jnp.bfloat16))

    def fold(layer, batch, index, carry):
        top, total, sums = carry
        queries = jnp.concatenate([qt[layer, batch], all_heads(qm[0, batch])], axis=0)
        spot = plane(batch, index)
        rows = kvb[(layer,) + spot + (batch,)].reshape(KB, 128)
        scores = nn(jnp.concatenate([rows, km[spot].reshape(KB, 128)], axis=1), queries)
        new_top = jnp.maximum(top, jnp.max(scores, axis=0, keepdims=True))
        shrink = jnp.exp(top - new_top)
        probs = jnp.exp(scores - new_top)
        total = total * shrink + jnp.sum(probs, axis=0, keepdims=True)
        return new_top, total, sums * shrink + tn(rows, probs.astype(jnp.bfloat16))

    def held(batch):
        return state[batch, 0:1, :], state[batch, 1:2, :], acc[batch]

    def attend_near(layer, batch):
        top, total, sums = fold(layer, batch, place[ORDERS[batch][2]], held(batch))
        state[batch, 0:1, :] = top
        state[batch, 1:2, :] = total
        acc[batch] = sums

    def attend_far(layer, batch):
        def step(index, carry):
            return fold(layer, batch, (place[ORDERS[batch][2]] + index) % 4, carry)

        top, total, sums = lax.fori_loop(1, 4, step, held(batch))
        result = (sums / total)[64:, :]
        mixed[layer, batch] = result
        lse[layer, batch] = jnp.broadcast_to(top + jnp.log(total), (8, QS))
        att[layer, pl.ds(batch * T, T), :] = without_first_slot(to_rows(result)).astype(
            jnp.bfloat16
        )

    def swap(slot):
        return send(mine.at[slot], theirs.at[slot], xsem.at[slot], xrsem.at[slot], other_core())

    def branch_of(layer):
        mine[0] = nt(att[layer], wat[layer, :, :, :, :, QS:].reshape(DP, QS))
        one = swap(0)
        one.start()
        one.wait()
        branch = mine[0] + theirs[0]
        middle = rows_of(layer).astype(jnp.float32) + branch
        mid[layer] = middle
        scale = lax.rsqrt(mean_of(middle * middle) + EPS)
        n2[layer] = (middle * scale * gains[layer, 3:4, :]).astype(jnp.bfloat16)
        return branch

    def feed_forward(layer, branch, hooks):
        normed = n2[layer]
        sums = jnp.zeros((R, DP), jnp.float32)
        for index, (start, size) in enumerate(PARTS[0] + PARTS[1]):
            hooks[index]()

            def weights(first, start=start, size=size):
                return wml[:, :, :, :, pl.ds(first + start, size)].reshape(DP, size)

            gate = nn(normed, weights(0))
            up = nn(normed, weights(FFH))
            gu_v[:, pl.ds(start, size)] = gate
            gu_v[:, pl.ds(FFH + start, size)] = up
            hidden = (gate * jax.nn.sigmoid(gate) * up).astype(jnp.bfloat16)
            sums = sums + nt(hidden, weights(2 * FFH))
        store(gu_v, gu.at[layer], 4 + layer)
        mine[1] = sums
        one = swap(1)
        one.start()
        one.wait()
        result = mine[1] + theirs[1]
        middle = mid[layer]
        xs_[layer] = (middle + result).astype(jnp.bfloat16)
        rows = rows_of(layer).astype(jnp.float32)
        lane = lax.broadcasted_iota(jnp.int32, (8, 128), 1)
        table = jnp.zeros((8, 128), jnp.float32)
        for kind, values in enumerate((rows, branch, result)):
            squares = jnp.sum(values * values, axis=1, keepdims=True)
            for batch in range(MB):
                one = jnp.sum(squares[batch * T : (batch + 1) * T], axis=0, keepdims=True)
                one = jnp.where(first_key < lengths[batch], one, 0.0)
                table = jnp.where(lane == 3 * batch + kind, one, table)
        sq[layer] = table

    def nothing():
        pass

    def chain(*steps):
        def run():
            for step in steps:
                step()

        return run

    def do(method, *numbers):
        return functools.partial(method, *numbers)

    project_keys(0)
    keys[0][0]()
    project_queries(0)
    early.phases[4]()
    keys[0][2]()
    keys[0][3]()
    for batch in range(MB):
        attend_own(0, batch)
    early.phases[5]()
    early.group(0, 0)
    keys[0][5]()
    keys[0][6]()
    early.group(0, 1)
    attend_near(0, 0)
    attend_near(0, 1)
    keys[0][7]()
    early.group(0, 2)
    attend_near(0, 2)
    keys[0][8]()
    early.group(0, 3)
    early.pass_on(0, 0)
    early.pass_on(0, 1)
    early.group(1, 0)
    store(kvb.at[0], kv.at[0], 0)
    attend_far(0, 0)
    early.pass_on(0, 2)
    early.group(1, 1)
    attend_far(0, 1)
    early.pass_on(0, 3)
    early.group(1, 2)
    early.pass_on(1, 0)
    attend_far(0, 2)
    early.group(1, 3)
    early.pass_on(1, 1)
    late.phases[0]()
    branch = branch_of(0)
    early.pass_on(1, 2)
    feed_forward(
        0,
        branch,
        [
            do(early.ready, 0, 0),
            chain(do(early.ready, 0, 1), do(early.pass_on, 1, 3), late.phases[2], late.phases[3]),
            do(early.ready, 0, 2),
            do(early.ready, 0, 3),
            do(early.ready, 1, 0),
            do(early.ready, 1, 1),
            do(early.ready, 1, 2),
            chain(do(early.ready, 1, 3), late.phases[4]),
        ],
    )
    store(wml, wm.at[0], 2)
    late.phases[5]()
    late.group(0, 0)
    attn[1][8]()
    store(wat, wa, 1)
    project_keys(1)
    keys[1][0]()
    late.group(0, 1)
    project_queries(1)
    keys[1][2]()
    keys[1][3]()
    late.group(0, 2)
    for batch in range(MB):
        attend_own(1, batch)
    keys[1][5]()
    keys[1][6]()
    late.group(0, 3)
    attend_near(1, 0)
    attend_near(1, 1)
    keys[1][7]()
    late.pass_on(0, 0)
    attend_near(1, 2)
    keys[1][8]()
    late.pass_on(0, 1)
    late.pass_on(0, 2)
    late.pass_on(0, 3)
    late.group(1, 0)
    store(kvb.at[1], kv.at[1], 3)
    attend_far(1, 0)
    late.group(1, 1)
    late.group(1, 2)
    late.pass_on(1, 0)
    attend_far(1, 1)
    late.group(1, 3)
    late.pass_on(1, 1)
    attend_far(1, 2)
    early.finish()
    outs[2].wait()
    outs[4].wait()
    branch = branch_of(1)
    late.pass_on(1, 2)
    late.pass_on(1, 3)

    def loads(index):
        start, size = (PARTS[0] + PARTS[1])[index]
        copies = []
        for part in range(3):
            cols = pl.ds(part * FFH + start, size)
            copies.append(
                pltpu.make_async_copy(
                    wm.at[1, :, :, :, :, cols], wml.at[:, :, :, :, cols], wsem.at[3 * index + part]
                )
            )
        return copies

    def fetch(index):
        late.ready(index // ROUNDS, index % ROUNDS)
        for one in loads(index):
            one.start()

    def fetched(index):
        if index + 1 < 2 * ROUNDS:
            fetch(index + 1)
        for one in loads(index):
            one.wait()

    fetch(0)
    feed_forward(1, branch, [do(fetched, index) for index in range(2 * ROUNDS)])
    for index, one in outs.items():
        if index not in (2, 4):
            one.wait()
    late.finish()
    for stages in attn + keys:
        stages[9]()


def forward(*arrays):
    low, full = jnp.bfloat16, jnp.float32
    return pl.pallas_call(
        forward_kernel,
        out_shape=(
            shape((2, 4, 4, 4, 16, CA), low),
            shape((2, 4, 4, 4, 16, CM), low),
            shape((2, 4, 4, 4, MB, T, 128), low),
            shape((2, R, 2 * FFH), full),
            shape((2, R, DP), low),
            shape((2, 8, DP), full),
            shape((2, R, DP), low),
            shape((2, MB, 128, QS), low),
            shape((2, MB, 64, QS), full),
            shape((2, MB, 8, QS), full),
            shape((2, R, QS), low),
            shape((2, R, DP), full),
            shape((2, R, DP), low),
            shape((2, R, DP), low),
            shape((2, 8, 128), full),
            shape((4, 4, 4, T, 128), low),
            shape((2, MB, 128, 128), low),
            shape((MB, T, 128), full),
        ),
        in_specs=[VMEM] * 11,
        out_specs=(ANY,) * 4 + (VMEM,) * 14,
        scratch_shapes=[
            pltpu.VMEM((2, R, DP), low),
            pltpu.VMEM((2, 8, DP), full),
            pltpu.VMEM((16, CA), low),
            pltpu.VMEM((16, CM), low),
            pltpu.VMEM((2, 16, CA), low),
            pltpu.VMEM((2, 16, CM), low),
            pltpu.VMEM((2, 4, 4, 4, 16, CA), low),
            pltpu.VMEM((4, 4, 4, 16, CM), low),
            pltpu.VMEM((2, 4, 4, 4, MB, T, 128), low),
            pltpu.VMEM((R, 2 * FFH), full),
            pltpu.VMEM((2, R, DP), full),
            pltpu.VMEM((2, R, DP), full),
            pltpu.VMEM((MB, 8, QS), full),
            pltpu.VMEM((MB, 128, QS), full),
            DMA((4,)),
            DMA((4,)),
            DMA((4,)),
            DMA((2, 3, 3, 4)),
            DMA((2, 3, 3, 4)),
            DMA((2, 3, 3, 4)),
            DMA((2, 3, 3, 4)),
            DMA((2, 3, 2, 2, ROUNDS)),
            DMA((2, 3, 2, 2, ROUNDS)),
            DMA((2, 3, 2, ROUNDS)),
            DMA((2, 3, 2, ROUNDS)),
            DMA((2, 3, 3, 4)),
            DMA((2, 3, 3, 4)),
            DMA((6,)),
            DMA((24,)),
            DMA((2,)),
            DMA((2,)),
        ],
        compiler_params=params(0, vmem=60),
        name="forward",
    )(*arrays)


def norm_back(grad, rows, gain):
    scale = lax.rsqrt(mean_of(rows * rows) + EPS)
    scaled = grad * gain
    back = scale * scaled - rows * (scale * scale * scale) * mean_of(scaled * rows)
    return back, jnp.sum(grad * rows * scale, axis=0, keepdims=True)


SLOT = 256
FF_SLOTS = tuple((start, min(SLOT, FFH - start)) for start in range(0, FFH, SLOT))
A_SLOTS = ((0, 3), (3, 3), (6, 2))


def slot_view(pool):
    def view(chips, j, part):
        lanes = slice(None) if part is None else pl.ds(part * 128, 128)
        return pool.at[(pl.ds(*A_SLOTS[j]),) + tuple(chips) + (slice(None), lanes)]

    return view


def backward_kernel(
    wa, wm, kv, gu, ends, xs_, gains, n1, qt, mixed, lse, att, mid, n2, squares, cosine, sine,
    km, qm, ob,
    grads, dx, outv, other, small_out,
    pool, gbuf, n2t, dmt, wat, mine, theirs, dout, dmid, da, dot_, acc, low, vlow, kvb, own,
    kh0, kw0, kw1, kw2, slab, got_half, got_whole, spare, mh1, mw1, mw2, ah0, aw0, aw1, aw2,
    sbuf,
    lsem, psem, gsem, usem, xsem, xrsem, ks, kr, hs, hr, os_, or_, ws, wr, ls, ms, mr, as_, ar,
    bs, br, fs, fr, credit,
):
    place = position()
    core = lax.axis_index("section")
    chip = lax.axis_index("dp")
    here = (place["x"], place["y"], place["z"])
    partners = greet(place, core=True, far=True)

    def heads_load(layer):
        return pltpu.make_async_copy(wa.at[layer], wat, lsem.at[2 * layer])

    def keys_load(layer):
        return pltpu.make_async_copy(kv.at[layer], kvb, lsem.at[2 * layer + 1])

    heads_load(1).start()
    keys_load(1).start()
    dout[...] = ends[1].astype(jnp.float32)
    small = [[None] * 4, [None] * 4]
    stored = {}

    def swap(slot):
        return send(mine.at[slot], theirs.at[slot], xsem.at[slot], xrsem.at[slot], other_core())

    def feed_loads(layer, index):
        start, size = FF_SLOTS[index]
        slot = index % 2
        copies = []
        for part in range(3):
            copies.append(
                pltpu.make_async_copy(
                    wm.at[layer, :, :, :, :, pl.ds(part * FFH + start, size)],
                    pool.at[3 * slot + part, :, :, :, :, pl.ds(0, size)],
                    psem.at[slot, part],
                )
            )
        for part in range(2):
            copies.append(
                pltpu.make_async_copy(
                    gu.at[layer, :, pl.ds(part * FFH + start, size)],
                    gbuf.at[slot, part, :, pl.ds(0, size)],
                    usem.at[slot, part],
                )
            )
        return copies

    def feed_start(layer):
        for index in range(2):
            for one in feed_loads(layer, index):
                one.start()

    feed_start(1)

    def back_feed(layer, stream, hooks, free=2):
        sends = {
            2: ((0, 0),),
            3: ((0, 1),),
            4: ((0, 2),),
            6: ((0, 3),),
            7: ((1, 0),),
            8: ((1, 1),),
            9: ((1, 2),),
        }
        grad_in = dout[...]
        grad_low = grad_in.astype(jnp.bfloat16)
        n2t[...] = n2[layer].astype(jnp.float32).T.astype(jnp.bfloat16)
        dmt[...] = grad_low.astype(jnp.float32).T.astype(jnp.bfloat16)
        mine[0] = jnp.zeros((R, DP), jnp.float32)
        for index, (start, size) in enumerate(FF_SLOTS):
            slot = index % 2
            hooks.get(index, lambda: None)()
            for one in feed_loads(layer, index):
                one.wait()

            def weights(part, slot=slot, size=size):
                return pool[3 * slot + part, :, :, :, :, :size].reshape(DP, size)

            grad_hidden = nn(grad_low, weights(2))
            gate = gbuf[slot, 0, :, :size]
            up = gbuf[slot, 1, :, :size]
            sigma = jax.nn.sigmoid(gate)
            hidden = (gate * sigma * up).astype(jnp.bfloat16)
            grad_gate = grad_hidden * up * sigma * (1.0 + gate * (1.0 - sigma))
            grad_gate = grad_gate.astype(jnp.bfloat16)
            grad_up = (grad_hidden * gate * sigma).astype(jnp.bfloat16)
            mine[0] += nt(grad_gate, weights(0)) + nt(grad_up, weights(1))
            if index + 2 < len(FF_SLOTS):
                for one in feed_loads(layer, index + 2):
                    one.start()
            products = ((n2t, grad_gate), (n2t, grad_up), (dmt, hidden))
            for part, (left, right) in enumerate(products):
                held = 6 + 3 * slot + part
                if held in stored:
                    stored.pop(held).wait()
                pool[held, :, :, :, :, :size] = (
                    nn(left[...], right).astype(jnp.bfloat16).reshape(4, 4, 4, 16, size)
                )
                stored[held] = pltpu.make_async_copy(
                    pool.at[held, :, :, :, :, pl.ds(0, size)],
                    grads.at[layer, :, :, :, :, pl.ds(part * FFH + start, size)],
                    gsem.at[slot, part],
                )
                stored[held].start()
            if index == free:
                for earlier in range(2, index):
                    for half, r in sends.get(earlier, ()):
                        stream.group(half, r)
            if index >= free:
                for half, r in sends.get(index, ()):
                    stream.group(half, r)
        for held in list(stored):
            stored.pop(held).wait()
        stream.group(1, 3)
        stream.load()
        one = swap(0)
        one.start()
        one.wait()
        back, gain_row = norm_back(mine[0] + theirs[0], mid[layer], gains[layer, 3:4, :])
        small[layer][1] = gain_row
        middle = grad_in + back
        dmid[...] = middle
        middle_low = middle.astype(jnp.bfloat16)
        da[layer] = middle_low
        heads_load(layer).wait()
        turned = nn(middle_low, wat[:, :, :, :, QS:].reshape(DP, QS))
        turned = without_first_slot(turned.astype(jnp.bfloat16).astype(jnp.float32))
        for batch in range(MB):
            columns = to_columns(turned[batch * T : (batch + 1) * T]).astype(jnp.bfloat16)
            dot_[batch] = jnp.concatenate([jnp.zeros_like(columns), columns], axis=0)

    def terms(layer, batch, rows, scores):
        slopes_out = dot_[batch]
        inner = jnp.sum(
            mixed[layer, batch] * slopes_out[64:, :].astype(jnp.float32), axis=0, keepdims=True
        )
        probs = jnp.exp(scores - lse[layer, batch, 0:1, :])
        slopes = (probs * (nn(rows, slopes_out) - inner)).astype(jnp.bfloat16)
        both = nt(slopes, qt[layer, batch]) + nt(probs.astype(jnp.bfloat16), slopes_out)
        return both.astype(jnp.bfloat16), tn(rows[:, :64], slopes)

    def back_plane(layer, batch, offset, begin=False):
        spot = plane(batch, (place[ORDERS[batch][2]] + offset) % 4)
        rows = kvb[spot + (batch,)].reshape(KB, 128)
        marked = jnp.concatenate([qt[layer, batch], all_heads(qm[0, batch])], axis=0)
        scores = nn(jnp.concatenate([rows, km[spot].reshape(KB, 128)], axis=1), marked)
        both, more = terms(layer, batch, rows, scores)
        kvb[spot + (batch,)] = both.reshape(4, 4, T, 128)
        acc[batch] = more if begin else acc[batch] + more

    def back_own(layer, batch):
        rows = kvb[here + (batch,)]
        back_plane(layer, batch, 0)
        marked = jnp.concatenate([qt[layer, batch], all_heads(qm[1, batch])], axis=0)
        scores = nn(jnp.concatenate([rows, km[here]], axis=1), marked) + all_heads(ob[batch])
        both, more = terms(layer, batch, rows, scores)
        kvb[here + (batch,)] = both
        acc[batch] += more

    def back_queries(layer):
        whole = jnp.concatenate([to_rows(acc[batch] * 0.125) for batch in range(MB)], axis=0)
        turned = turn(whole, tiled(cosine[...]), -tiled(sine[...])).astype(jnp.bfloat16)
        low[layer] = turned
        mine[1] = nt(turned, wat[:, :, :, :, 0:QS].reshape(DP, QS))

    def back_keys(layer):
        key_grads = own[...].reshape(R, 128)
        none = jnp.zeros((R, 64), jnp.float32)
        turned = turn(
            jnp.concatenate([key_grads[:, :64], none], axis=1),
            tiled(cosine[...], 128),
            -tiled(sine[...], 128),
        ).astype(jnp.bfloat16)
        values = jnp.concatenate([key_grads[:, 64:], none], axis=1).astype(jnp.bfloat16)
        low[layer, :, 0:128] = low[layer, :, 0:128] + turned
        vlow[layer] = values
        small[layer][2] = jnp.concatenate(
            [
                jnp.sum(low[layer].astype(jnp.float32), axis=0, keepdims=True),
                jnp.sum(values.astype(jnp.float32), axis=0, keepdims=True),
                jnp.zeros((1, QS - 128), jnp.float32),
            ],
            axis=1,
        )
        mine[1] += nt(turned, wat[:, :, :, :, 0:128].reshape(DP, 128)) + nt(
            values, wat[:, :, :, :, QS : QS + 128].reshape(DP, 128)
        )
        one = swap(1)
        one.start()
        one.wait()
        rows = (ends[0] if layer == 0 else xs_[0]).astype(jnp.float32)
        back, gain_row = norm_back(mine[1] + theirs[1], rows, gains[layer, 2:3, :])
        small[layer][0] = gain_row
        small[layer][3] = jnp.concatenate(
            [squares[layer, 0:1, :], jnp.zeros((1, DP - 128), jnp.float32)], axis=1
        )
        result = (dmid[...] + back).astype(jnp.bfloat16)
        if layer == 0:
            dx[...] = result
        else:
            dout[...] = result.astype(jnp.float32)

    def put(slot, start, product):
        wide = product.shape[1]
        pool[slot, :, :, :, :, pl.ds(start, wide)] = product.astype(jnp.bfloat16).reshape(
            4, 4, 4, 16, wide
        )

    def query_products(layer):
        first = tn(n1[layer], low[layer])
        second = tn(da[layer], att[layer])
        for side, product in enumerate((first, second)):
            put(4 * layer + 2 * side, 128, product[:, 128:SLOT])
            put(4 * layer + 2 * side + 1, 0, product[:, SLOT:])

    def key_products(layer):
        put(4 * layer, 0, tn(n1[layer], low[layer, :, 0:128]))
        put(
            4 * layer + 2,
            0,
            tn(n1[layer], vlow[layer]) + tn(da[layer], att[layer, :, 0:128]),
        )

    def total(terms):
        return sum(term[...].astype(jnp.float32) for term in terms)

    def key_final(j, *terms):
        own[j] = total(terms)

    key_halves = [lambda j, k, ref=ref: ref.at[j, k] for ref in (kh0,)]
    key_wholes = [lambda j, k, ref=ref: ref.at[j, k] for ref in (kw0, kw1, kw2)]
    keys = [
        scatter_stages(
            token_view(kvb), key_halves, key_wholes, place, ks.at[layer], kr.at[layer], key_final
        )
        for layer in range(2)
    ]

    def feed_final(layer):
        def final(j, *terms):
            outv[layer, :, pl.ds(j * FFH, FFH)] = total(terms)

        return final

    def lanes(ref, size):
        return lambda j, k: ref.at[
            (j, k) + (slice(None),) * (len(ref.shape) - 3) + (pl.ds(0, size(k)),)
        ]

    inner_halves = [None, lanes(mh1, lambda k: half_of(FFH, k)[1])]
    inner_wholes = [None] + [lanes(ref, lambda k: FFH) for ref in (mw1, mw2)]
    feed = [
        LargeScatter(
            grads.at[layer], slab, got_half, got_whole, spare, inner_halves, inner_wholes, place,
            (hs.at[layer], hr.at[layer]), (os_.at[layer], or_.at[layer]),
            (ws.at[layer], wr.at[layer]), ls.at[layer], ms.at[layer], mr.at[layer],
            feed_final(layer),
        )
        for layer in range(2)
    ]
    late, early = feed

    def slots(ref):
        return lambda j, k: ref.at[j, k, pl.ds(0, A_SLOTS[j][1])]

    def heads_final(j, *terms):
        begin, count = A_SLOTS[j]
        for index in range(count):
            layer, spot = divmod(begin + index, 4)
            outv[layer, :, pl.ds(CM + spot * SLOT, SLOT)] = total(
                [term.at[index] for term in terms]
            )

    heads = scatter_stages(
        slot_view(pool), [slots(ah0)],
        [slots(ref) for ref in (aw0, aw1, aw2)], place, as_, ar, heads_final,
    )

    def total_small(phase, axis):
        copies = [
            send(
                sbuf.at[4 * phase],
                sbuf.at[4 * phase + k],
                bs.at[phase, k - 1],
                br.at[phase, k - 1],
                chip_id(moved(place, axis, distance)),
            )
            for k, distance in ((1, 1), (2, -1), (3, 2))
        ]

        def begin():
            for one in copies:
                one.start()

        def end():
            for one in copies:
                one.wait()
            total = (
                sbuf[4 * phase] + sbuf[4 * phase + 1] + sbuf[4 * phase + 2] + sbuf[4 * phase + 3]
            )
            if phase < 2:
                sbuf[4 * phase + 4] = total
            else:
                small_out[...] = total

        return begin, end

    def rounds_of(*methods):
        for method in methods:
            for r in range(ROUNDS):
                method(r)

    def back_attend(layer, stream):
        keys_load(layer).wait()
        for batch in range(MB):
            back_plane(layer, batch, 2, True)
        keys[layer][0]()
        stream.pass_on(0)
        for batch in range(MB):
            back_plane(layer, batch, 1)
        stream.pass_on(1)
        for batch in range(MB):
            back_plane(layer, batch, 3)
        keys[layer][1]()
        stream.pass_on(2)
        for batch in range(MB):
            back_own(layer, batch)
        keys[layer][2]()
        keys[layer][3]()
        stream.pass_on(3)
        back_queries(layer)
        keys[layer][5]()
        keys[layer][6]()
        stream.third()
        stream.phases[0]()

    def settle_early():
        early.phases[5]()
        early.finish()
        for axis in "xyz":
            for distance in (1, -1, 2):
                pl.semaphore_signal(
                    credit,
                    inc=1,
                    device_id=chip_id(moved(place, axis, distance)),
                    device_id_type=MESH,
                )
        pl.semaphore_wait(credit, 9)

    back_feed(1, early, {1: lambda: settle(partners)})
    back_attend(1, early)
    feed_start(0)
    keys[1][8]()
    keys[1][9]()
    keys_load(0).start()
    back_keys(1)
    heads_load(0).start()
    back_feed(
        0,
        late,
        {
            0: early.phases[1],
            2: lambda: (early.phases[2](), early.phases[3]()),
            4: settle_early,
        },
        4,
    )
    back_attend(0, late)
    query_products(1)
    key_products(1)
    query_products(0)
    keys[0][8]()
    keys[0][9]()
    back_keys(0)
    key_products(0)
    sbuf[0] = jnp.concatenate(small[0] + small[1], axis=0)
    sums = [total_small(phase, axis) for phase, axis in enumerate("xyz")]
    sums[0][0]()
    heads[0]()
    late.phases[1]()
    sums[0][1]()
    sums[1][0]()
    heads[1]()
    late.phases[2]()
    late.phases[3]()
    heads[2]()
    heads[3]()
    sums[1][1]()
    sums[2][0]()
    late.phases[5]()
    heads[5]()
    heads[6]()
    sums[2][1]()
    heads[8]()
    for layer in range(2):
        outv[layer, 14:15, pl.ds(CM, CA)] = small_out[4 * layer + 2 : 4 * layer + 3, :]
    trade = send(outv.at[1 - core], other, fs, fr, other_core())
    trade.start()
    late.finish()
    heads[9]()
    trade.wait()


def backward(*arrays):
    low, full = jnp.bfloat16, jnp.float32
    half = FFH - FFH // 256 * 128

    def ring(last, phase, count=2):
        return pltpu.VMEM((3, count) + last[:-2] + (4,) * (2 - phase) + last[-2:], low)

    return pl.pallas_call(
        backward_kernel,
        out_shape=(
            shape((2, 4, 4, 4, 16, CM), low),
            shape((R, DP), low),
            shape((2, 16, C), full),
            shape((16, C), full),
            shape((8, DP), full),
        ),
        in_specs=[ANY] * 4 + [VMEM] * 16,
        out_specs=(ANY,) + (VMEM,) * 4,
        scratch_shapes=[
            pltpu.VMEM((12, 4, 4, 4, 16, SLOT), low),
            pltpu.VMEM((2, 2, R, SLOT), full),
            pltpu.VMEM((DP, R), low),
            pltpu.VMEM((DP, R), low),
            pltpu.VMEM((4, 4, 4, 16, CA), low),
            pltpu.VMEM((2, R, DP), full),
            pltpu.VMEM((2, R, DP), full),
            pltpu.VMEM((R, DP), full),
            pltpu.VMEM((R, DP), full),
            pltpu.VMEM((2, R, DP), low),
            pltpu.VMEM((MB, 128, QS), low),
            pltpu.VMEM((MB, 64, QS), full),
            pltpu.VMEM((2, R, QS), low),
            pltpu.VMEM((2, R, 128), low),
            pltpu.VMEM((4, 4, 4, MB, T, 128), low),
            pltpu.VMEM((MB, T, 128), full),
        ]
        + [
            ring((T // 2, 128), 0),
            ring((T, 128), 0),
            ring((T, 128), 1, 3),
            ring((T, 128), 2, 3),
            pltpu.VMEM((3, 4, 4, 16, FFH), low),
            ring((16, half), 0),
            ring((16, FFH), 0),
            ring((16, 384), 0),
            ring((16, half), 1),
            ring((16, FFH), 1),
            ring((16, FFH), 2, 3),
            ring((3, 16, 128), 0),
            ring((3, 16, SLOT), 0),
            ring((3, 16, SLOT), 1, 3),
            ring((3, 16, SLOT), 2, 3),
        ]
        + [
            pltpu.VMEM((12, 8, DP), full),
            DMA((4,)),
            DMA((2, 3)),
            DMA((2, 3)),
            DMA((2, 2)),
            DMA((2,)),
            DMA((2,)),
            DMA((2, 3, 3, 4)),
            DMA((2, 3, 3, 4)),
            DMA((2, 3, 2, ROUNDS)),
            DMA((2, 3, 2, ROUNDS)),
            DMA((2, 3, 2, ROUNDS)),
            DMA((2, 3, 2, ROUNDS)),
            DMA((2, 3, 2, ROUNDS)),
            DMA((2, 3, 2, ROUNDS)),
            DMA((2, 9)),
            DMA((2, 3, 3, 4)),
            DMA((2, 3, 3, 4)),
            DMA((3, 3, 4)),
            DMA((3, 3, 4)),
            DMA((3, 3)),
            DMA((3, 3)),
            DMA,
            DMA,
            pltpu.SemaphoreType.REGULAR,
        ],
        compiler_params=params(1, vmem=63),
        name="backward",
    )(*arrays)


def assemble_kernel(
    kept, other, dx, xs_, sums, valid, boundary, grad_qkv, grad_bias, grad_out, grad_gu, grad_down,
    grad_gain, rms,
):
    core = lax.axis_index("section")
    own, far = jnp.where(core == 0, kept[0], kept[1]), other[...]
    sides = (jnp.where(core == 0, own, far), jnp.where(core == 0, far, own))

    def column(start, size):
        return [side[:, start : start + size] for side in sides]

    qkv = jnp.concatenate(column(CM + 64, 448) + column(CM, 64) + column(CM + QS, 64), axis=1)
    out = jnp.concatenate(column(CM + QS + 64, 448), axis=1)
    gate_up = jnp.concatenate(column(0, FFH) + column(FFH, FFH), axis=1)
    down = jnp.concatenate(column(2 * FFH, FFH), axis=1)
    for row in range(14):
        grad_qkv[row] = qkv[row : row + 1, :]
        grad_out[row] = out[row : row + 1, :]
        grad_gu[row] = gate_up[row : row + 1, :]
        grad_down[row] = down[row : row + 1, :]
    rows = [side[14:15, CM:] for side in sides]
    grad_bias[...] = jnp.concatenate(
        [row[:, 64:QS] for row in rows]
        + [row[:, :64] for row in rows]
        + [row[:, QS : QS + 64] for row in rows],
        axis=1,
    )
    mine = jnp.where(core == 0, sums[0:4, :], sums[4:8, :])
    rest = jnp.concatenate([mine, jnp.zeros((12, DP), jnp.float32)], axis=0)
    terms = []
    for _ in range(3):
        term = rest.astype(jnp.bfloat16)
        rest = rest - term.astype(jnp.float32)
        terms.append(term)
    result = jnp.where(core == 0, dx[...].astype(jnp.float32), xs_[1].astype(jnp.float32))
    narrow = nt(
        jnp.concatenate([result.astype(jnp.bfloat16)] + terms, axis=0), spread_matrix()
    )
    boundary[...] = narrow[:R].astype(jnp.bfloat16)
    grad_gain[...] = narrow[R : R + 2] + narrow[R + 16 : R + 18] + narrow[R + 32 : R + 34]
    for batch in range(MB):
        count = jnp.sum(valid[batch : batch + 1, :].astype(jnp.float32), axis=1, keepdims=True)
        rms[batch] = jnp.sqrt(mine[3:4, 3 * batch : 3 * batch + 3] / (count * float(BLOCK * D)))


def assemble(*arrays):
    full = jnp.float32
    return pl.pallas_call(
        assemble_kernel,
        out_shape=(
            shape((R, D), jnp.bfloat16),
            shape((14, 1, D + 256), full),
            shape((1, D + 256), full),
            shape((14, 1, D), full),
            shape((14, 1, 4 * FFH), full),
            shape((14, 1, 2 * FFH), full),
            shape((2, D), full),
            shape((MB, 1, MB), full),
        ),
        in_specs=[VMEM] * 6,
        out_specs=(VMEM,) * 8,
        compiler_params=params(),
        name="assemble",
    )(*arrays)


def shards(
    ends,
    segment_ids,
    valid_blocks,
    qkv_weight,
    qkv_bias,
    out_weight,
    gate_up_weight,
    down_weight,
    norm_gains,
):
    chip = lax.axis_index("dp")
    places = chip * T + jnp.arange(T, dtype=jnp.int32)
    frequency = THETA ** (-(jnp.arange(128) % 32).astype(jnp.float32) * 2.0 / 64)
    sign = jnp.where(jnp.arange(128) % 64 < 32, -1.0, 1.0)
    angles = places.astype(jnp.float32)[:, None] * frequency[None, :]
    cosine = jnp.cos(angles)
    sine = jnp.sin(angles) * sign[None, :]

    (
        wa, wm, kv, gu, ends_all, gains, n1, qt, mixed, lse, att, mid, n2, xs_, sq, km, qm, ob,
    ) = forward(
        gate_up_weight[0],
        down_weight[0],
        qkv_weight[0],
        out_weight[0],
        qkv_bias,
        norm_gains[0],
        ends.reshape(R, D),
        segment_ids,
        valid_blocks,
        cosine,
        sine,
    )
    _, dx, kept, other, sums = backward(
        wa, wm, kv, gu, ends_all, xs_, gains, n1, qt, mixed, lse, att, mid, n2, sq, cosine, sine,
        km, qm, ob,
    )
    boundary, *grads, rms = assemble(kept, other, dx, xs_, sums, valid_blocks)
    grad_qkv, grad_bias, grad_out, grad_gu, grad_down, grad_gain = grads
    return (
        boundary.reshape(1, MB, T, D),
        grad_qkv.transpose(1, 0, 2),
        grad_bias,
        grad_out.transpose(1, 0, 2),
        grad_gu.transpose(1, 0, 2),
        grad_down.transpose(1, 0, 2),
        grad_gain[None],
        rms.transpose(1, 0, 2),
    )


def solution(mesh):
    in_specs = (
        P("section", None, "dp", None),
        P(),
        P(),
        P("section", "dp", None),
        P("section", None),
        P("section", "dp", None),
        P("section", "dp", None),
        P("section", "dp", None),
        P("section", None, None),
    )
    out_specs = (
        P("section", None, "dp", None),
        P("section", "dp", None),
        P("section", None),
        P("section", "dp", None),
        P("section", "dp", None),
        P("section", "dp", None),
        P("section", None, None),
        P("section", None, None),
    )
    return jax.shard_map(shards, mesh=mesh, in_specs=in_specs, out_specs=out_specs, check_vma=False)
```
